256 devices in a mesh: grp: 4 (over y), path: 64 (over x, z, core).
Axes of the slice: x: 4, y: 4, z: 8, core: 2. Of those that a mesh axis runs over, the one named last changes fastest.
Arguments:
- path_sens: bfloat16 [65536, 4800], P(('grp', 'path')), may hold values from -6 to 6
- discounts: bfloat16 [65536, 128], P(('grp', 'path')), may hold values from 0.29882812 to 1
- cash_flows: float32 [2048, 8], P('grp'), may hold values from -384 to 384
- flow_index: int32 [2048, 8], P('grp'), may hold values from 0 to 127
- exercise_step: int32 [2048], P('grp'), may hold values from 0 to 127
- trade_steps: int32 [2048], P('grp'), may hold values from 1 to 40
- jacobian_inv: bfloat16 [4800, 4800], P('path'), may hold values from -0.09375 to 0.09375
Outputs:
- quote_vega: float32 [2048, 4800], P(('grp', 'path'))
The draws below stay inside these ranges and needn't reach their ends.
All inputs are finite; a program needn't handle non-finite values.
Results may differ from the reference program's by a relative error of at most 0.004.
Values may be sent and summed in bfloat16 or wider, within the bound.
A program may use at most 64 MiB of HBM per device.

```python
import math
import jax
import jax.numpy as jnp
from jax import lax

P_SIZE = 4800
Q = 4800
NB = 40
NF = 128
C = 8
PATHS = 65536
TRADES = 2048
N_GRP = 4


def set_ends(values, rng, smallest, largest):
    dims = values.shape
    spot = [jax.random.randint(jax.random.fold_in(rng, axis), (), 0, dims[axis]) for axis in range(len(dims))]
    values = values.at[tuple(spot)].set(smallest)
    longest = dims.index(max(dims))
    spot[longest] = (spot[longest] + 1) % dims[longest]
    return values.at[tuple(spot)].set(largest)


def block_scale(key, shape, shards, least, largest):
    level, own = 1.0, jax.random.fold_in(key, 6)
    for position, blocks in shards:
        steps = jnp.exp(jax.random.uniform(jax.random.fold_in(own, position), (blocks,), jnp.float32, least / len(shards), largest / len(shards)))
        level = level * jnp.repeat(steps, shape[position] // blocks).reshape([-1 if axis == position else 1 for axis in range(len(shape))])
    return level


def scatter_about(rng, shape, width, reach, cuts=(), kind=jnp.bfloat16):
    values = jax.random.normal(rng, shape, jnp.float32) * width
    if len(cuts) > 0:
        values = block_scale(rng, shape, cuts, -0.22, 0.18) * values
    return jnp.clip(values, min=-reach, max=reach).astype(kind)


def setup_inputs(seed: int = 0) -> dict:
    seeds = jax.random.split(jax.random.key(seed), 8)
    path_sens = scatter_about(seeds[0], (PATHS, P_SIZE), 1.0, 6.0, ((0, 256),))
    discounts = jnp.clip(jnp.exp(math.log(1.0) - 1.2078867 * jax.random.uniform(seeds[1], (PATHS, NF), jnp.float32) ** block_scale(seeds[1], (PATHS, NF), ((0, 256),), -0.2, 0.2)), 0.29882812, 1.0).astype(jnp.bfloat16)
    cash_flows = scatter_about(seeds[2], (TRADES, C), (PATHS ** 0.5 / 4), 384.0, ((0, 4),), jnp.float32)
    flow_index = set_ends(jax.random.randint(seeds[3], (TRADES, C), 0, NF), jax.random.fold_in(seeds[3], 1), 0, NF - 1).astype(jnp.int32)
    exercise_step = set_ends(jax.random.randint(seeds[4], (TRADES,), 0, NF), jax.random.fold_in(seeds[4], 1), 0, NF - 1).astype(jnp.int32)
    trade_steps = set_ends(jax.random.randint(seeds[5], (TRADES,), 1, NB + 1), jax.random.fold_in(seeds[5], 1), 1, NB).astype(jnp.int32)
    jacobian_inv = scatter_about(seeds[6], (P_SIZE, Q), P_SIZE ** -0.5, 0.09375, ((0, 64),))
    return {"path_sens": path_sens, "discounts": discounts, "cash_flows": cash_flows, "flow_index": flow_index, "exercise_step": exercise_step, "trade_steps": trade_steps, "jacobian_inv": jacobian_inv}


def adjoint_weights(cash_flows, flow_index, exercise_step, forward_count):
    forwards = jnp.arange(forward_count, dtype=jnp.int32)
    live = (flow_index[:, :, None] == forwards[None, None, :]) & (forwards[None, None, :] >= exercise_step[:, None, None])
    return jnp.einsum("tc,tcf->ft", cash_flows.astype(jnp.float32), live.astype(jnp.float32), precision=lax.Precision.HIGHEST)


def reference(path_sens, discounts, cash_flows, flow_index, exercise_step, trade_steps, jacobian_inv):
    group_rows = TRADES // N_GRP
    bucket_width = P_SIZE // NB
    bucket = jnp.arange(P_SIZE, dtype=jnp.int32) // bucket_width
    disc_float = discounts.astype(jnp.float32)

    def one_group(packed):
        cash_group, index_group, exer_group, steps_group = packed
        weights = adjoint_weights(cash_group, index_group, exer_group, NF)
        adjoint = jnp.dot(disc_float, weights, precision=lax.Precision.HIGHEST).astype(jnp.bfloat16)
        vega = jnp.dot(adjoint.T, path_sens, preferred_element_type=jnp.float32) * (1.0 / PATHS)
        masked = jnp.where(bucket[None, :] < steps_group[:, None], vega, 0.0).astype(jnp.bfloat16)
        return jnp.dot(masked, jacobian_inv, preferred_element_type=jnp.float32)

    packed = (cash_flows.reshape(N_GRP, group_rows, C), flow_index.reshape(N_GRP, group_rows, C),
              exercise_step.reshape(N_GRP, group_rows), trade_steps.reshape(N_GRP, group_rows))
    result = lax.map(one_group, packed)
    return result.reshape(TRADES, Q)
```

```python
import jax
import jax.numpy as jnp
from jax import lax
from jax.sharding import PartitionSpec as P

NB = 40


def per_device(
    path_sens, discounts, cash_flows, flow_index, exercise_step, trade_steps, jacobian_inv
):
    params = path_sens.shape[1]
    path_scale = 1.0 / (path_sens.shape[0] * lax.axis_size("path") * lax.axis_size("grp"))
    bucket_width = params // NB
    forward_count = discounts.shape[1]
    by_quote = lax.all_to_all(jacobian_inv, "path", split_axis=1, concat_axis=0, tiled=True)
    moments = lax.dot_general(
        discounts, path_sens, (((0,), (0,)), ((), ())), preferred_element_type=jnp.float32
    )
    moments = lax.psum(moments, ("grp", "path"))
    forwards = jnp.arange(forward_count, dtype=jnp.int32)
    live = (flow_index[:, :, None] == forwards[None, None, :]) & (
        forwards[None, None, :] >= exercise_step[:, None, None]
    )
    weights = jnp.einsum(
        "tc,tcf->tf", cash_flows, live.astype(jnp.float32), precision=lax.Precision.HIGHEST
    )
    vega = jnp.dot(weights, moments, precision=lax.Precision.HIGHEST) * path_scale
    bucket = jnp.arange(params, dtype=jnp.int32) // bucket_width
    masked = jnp.where(bucket[None, :] < trade_steps[:, None], vega, 0.0).astype(jnp.bfloat16)
    quotes = jnp.dot(masked, by_quote, preferred_element_type=jnp.float32)
    return lax.all_to_all(quotes, "path", split_axis=0, concat_axis=1, tiled=True)


def solution(mesh):
    placed = (
        P(("grp", "path"), None),
        P(("grp", "path"), None),
        P("grp", None),
        P("grp", None),
        P("grp"),
        P("grp"),
        P("path", None),
    )
    return jax.shard_map(
        per_device, mesh=mesh, in_specs=placed, out_specs=P(("grp", "path"), None), check_vma=False
    )
```

```python
import jax
import jax.numpy as jnp
from jax import lax
from jax.experimental import pallas as pl
from jax.experimental.pallas import tpu as pltpu
from jax.sharding import PartitionSpec as P

NB = 40
LANE = 128
RING = 4
DEPTH = 8
CHIPS = RING * DEPTH
EXTRA = 6
F32 = jnp.float32
BF16 = jnp.bfloat16


def kernel(
    disc, sens, cash, index, exer, steps, jac, out,
    s_out, s_in, d_in, xp, r1, y2, r2, zb, rz, zr, zf, g2, xf,
    jp, jr, jf, jb, mk, pm, pr, po, ob,
    ss_s, rs_s, ss_1, rs_1, ss_2, rs_2, ss_z, rs_z, ss_g, rs_g,
    ss_a2, rs_a2, ss_a1, rs_a1, ss_j, rs_j, ss_p, rs_p, ss_o, rs_o,
):
    y = lax.axis_index("grp")
    me = lax.axis_index("path")
    j = lax.div(me, 2)
    c = lax.rem(me, 2)
    x = lax.div(j, DEPTH)
    z = lax.rem(j, DEPTH)
    sib = 1 - c
    paths = 2 * CHIPS
    half = xp.shape[0]
    params = sens.shape[1]
    width = params // NB
    split = half * LANE
    cut = half // 2 + 1
    quarter = (cut + 1) // 2
    parts = ((0, cut), (cut, half - cut))

    def halves(part):
        t0, n = parts[part]
        return (t0, quarter), (t0 + quarter, n - quarter)

    def at_chip(xx, zz, cc):
        return {"grp": y, "path": (xx * DEPTH + zz) * 2 + cc}

    def at_grp(yy):
        return {"grp": yy, "path": me}

    def rdma(src, dst, ss, rs, dev):
        return pltpu.make_async_remote_copy(
            src_ref=src, dst_ref=dst, send_sem=ss, recv_sem=rs,
            device_id=dev, device_id_type=pl.DeviceIdType.MESH,
        )

    sent = []

    def send(*args):
        d = rdma(*args)
        d.start()
        sent.append(d)

    ring_x = (x, at_chip(lax.rem(x + 1, RING), z, c), at_chip(lax.rem(x + 3, RING), z, c))
    ring_y = (y, at_grp(lax.rem(y + 1, RING)), at_grp(lax.rem(y + 3, RING)))
    sibling = at_chip(x, z, sib)

    barrier = pltpu.get_barrier_semaphore()
    for d in (ring_y[1], ring_y[2]):
        pl.semaphore_signal(barrier, inc=1, device_id=d, device_id_type=pl.DeviceIdType.MESH)

    @pl.loop(1, paths)
    def _(k):
        pl.semaphore_signal(
            barrier, inc=1, device_id={"grp": y, "path": lax.rem(me + k, paths)},
            device_id_type=pl.DeviceIdType.MESH,
        )

    last = half - 1
    tail = params - split - last * LANE

    @pl.loop(0, last)
    def _(t):
        s_out[t] = sens[:, pl.ds(pl.multiple_of((sib * half + t) * LANE, LANE), LANE)]

    @pl.when(sib == 0)
    def _():
        s_out[last] = sens[:, last * LANE : split]

    @pl.when(sib == 1)
    def _():
        s_out[last] = jnp.zeros(s_out.shape[1:], BF16)
        s_out[last, :, 0:tail] = sens[:, split + last * LANE : params]

    d_own = disc[...].astype(F32).T.astype(BF16)

    pl.semaphore_wait(barrier, paths + 1)

    send(disc, d_in, ss_s.at[4], rs_s.at[4], sibling)
    pieces = (halves(0)[0], halves(1)[0], halves(0)[1], halves(1)[1])
    for q, (t0, n) in enumerate(pieces):
        blk = pl.ds(t0, n)
        send(s_out.at[blk], s_in.at[blk], ss_s.at[q], rs_s.at[q], sibling)

    @pl.loop(0, last)
    def _(t):
        xp[t] = jnp.dot(
            d_own, sens[:, pl.ds(pl.multiple_of((c * half + t) * LANE, LANE), LANE)],
            preferred_element_type=F32,
        )

    @pl.when(c == 0)
    def _():
        xp[last] = jnp.dot(d_own, sens[:, last * LANE : split], preferred_element_type=F32)

    @pl.when(c == 1)
    def _():
        xp[last] = jnp.zeros(xp.shape[1:], F32)
        xp[last, :, 0:tail] = jnp.dot(
            d_own, sens[:, split + last * LANE : params], preferred_element_type=F32
        )

    rdma(disc, d_in, ss_s.at[4], rs_s.at[4], sibling).wait_recv()
    d_sib = d_in[...].astype(F32).T.astype(BF16)

    def rows(k, size):
        return pl.ds(pl.multiple_of(k * size, size), size)

    class Scatter:
        def __init__(self, src, rbuf, ss, rs, ring, hs, size):
            self.src, self.rbuf, self.ss, self.rs, self.hs = src, rbuf, ss, rs, hs
            i, self.right, self.left = ring
            self.own = rows(i, size)
            self.nr, self.far, self.nl = (rows(lax.rem(i + k, RING), size) for k in (1, 2, 3))

        def msg(self, n, h, rws, dev):
            t0, cnt = self.hs[h]
            return (
                self.src.at[pl.ds(t0, cnt), rws], self.rbuf.at[n, pl.ds(0, cnt)],
                self.ss.at[n], self.rs.at[n], dev,
            )

        def first(self, h):
            if h == 0:
                send(*self.msg(0, 0, self.far, self.right))
                send(*self.msg(1, 0, self.nl, self.left))
            else:
                send(*self.msg(2, 1, self.far, self.left))
                send(*self.msg(3, 1, self.nr, self.right))

        def second(self, h):
            n, rws, dev = ((0, self.nr, self.right), (2, self.nl, self.left))[h]
            t0, cnt = self.hs[h]
            rdma(*self.msg(n, h, rws, dev)).wait_recv()
            self.src[pl.ds(t0, cnt), rws] += self.rbuf[n, 0:cnt]
            send(*self.msg(4 + h, h, rws, dev))

        def result(self, h):
            t0, cnt = self.hs[h]
            n = (1, 3)[h]
            rdma(*self.msg(n, h, self.own, self.left)).wait_recv()
            rdma(*self.msg(4 + h, h, self.own, self.left)).wait_recv()
            return (
                self.src[pl.ds(t0, cnt), self.own]
                + self.rbuf[n, 0:cnt]
                + self.rbuf[4 + h, 0:cnt]
            )

    rings = (ring_x, ring_y)
    big, small = xp.shape[1] // RING, xp.shape[1] // RING // RING
    one = [
        Scatter(xp, r1.at[p], ss_1.at[p], rs_1.at[p], rings[p], halves(p), big) for p in (0, 1)
    ]
    for q, (t0, n) in enumerate(pieces):
        blk = pl.ds(t0, n)
        rdma(s_out.at[blk], s_in.at[blk], ss_s.at[q], rs_s.at[q], sibling).wait_recv()

        @pl.loop(t0, t0 + n)
        def _(t):
            xp[t] += jnp.dot(d_sib, s_in[t], preferred_element_type=F32)

        one[q % 2].first(q // 2)

    jt = jp.shape[0]
    jrows = jac.shape[0]
    jp[...] = jnp.zeros(jp.shape, BF16)

    @pl.loop(0, jt - 1)
    def _(t):
        jp[t, 0:jrows] = jac[:, pl.ds(pl.multiple_of(t * LANE, LANE), LANE)]

    jl = params - (jt - 1) * LANE
    jp[jt - 1, 0:jrows, 0:jl] = jac[:, (jt - 1) * LANE : params]

    for h in (0, 1):
        for p in (0, 1):
            one[p].second(h)

    top = lax.div(me, CHIPS)
    slot = me - CHIPS * top
    straddle = me == CHIPS

    def j_one(tile, e, chip, core, sl, sem):
        dst = chip * 2 + core

        @pl.when(dst == me)
        def _():
            pltpu.make_async_copy(jp.at[tile], jr.at[e, sl], rs_j.at[e, sl]).start()

        @pl.when(dst != me)
        def _():
            rdma(
                jp.at[tile], jr.at[e, sl], sem, rs_j.at[e, sl], {"grp": y, "path": dst}
            ).start()

    @pl.loop(0, CHIPS)
    def _(k):
        chip = lax.rem(j + k, CHIPS)
        j_one(chip, 0, chip, top, slot, ss_j.at[0, chip])

        @pl.when(straddle)
        def _():
            j_one(chip, 0, chip, 0, CHIPS, ss_j.at[1, chip])

    @pl.loop(0, EXTRA)
    def _(e):
        chip = 5 * e + 2
        j_one(CHIPS + e, 1, chip, top, slot, ss_j.at[0, CHIPS + e])

        @pl.when(straddle)
        def _():
            j_one(CHIPS + e, 1, chip, 0, CHIPS, ss_j.at[1, CHIPS + e])

    trades, slots = cash.shape
    forwards = lax.broadcasted_iota(jnp.int32, (trades, LANE), 1)
    late = forwards >= exer[...]
    weights = jnp.zeros((trades, LANE), F32)
    for s in range(slots):
        weights += jnp.where(late & (index[:, s : s + 1] == forwards), cash[:, s : s + 1], 0.0)
    weights = weights * (1.0 / (sens.shape[0] * paths * RING))
    w_hi = weights.astype(BF16)
    w_lo = (weights - w_hi.astype(F32)).astype(BF16)
    wide = jnp.concatenate([w_hi, w_hi, w_lo], axis=1)
    jf[...] = jnp.zeros(jf.shape, F32)

    two = [
        Scatter(y2, r2.at[p], ss_2.at[p], rs_2.at[p], rings[1 - p], halves(p), small)
        for p in (0, 1)
    ]
    for h in (0, 1):
        for p in (0, 1):
            t0, cnt = halves(p)[h]
            y2[pl.ds(t0, cnt)] = one[p].result(h)
            two[p].first(h)
    for h in (0, 1):
        for p in (0, 1):
            two[p].second(h)
    share = zr.shape[0]
    zb[pl.ds(half, zb.shape[0] - half)] = jnp.zeros((zb.shape[0] - half,) + zb.shape[1:], F32)
    for h in (0, 1):
        for p in (0, 1):
            t0, cnt = halves(p)[h]
            zb[pl.ds(t0, cnt)] = two[p].result(h)

    def z_at(k):
        return lax.rem(z + k, DEPTH)

    for k in range(1, DEPTH):
        d = z_at(k)
        send(
            zb.at[pl.ds(d * share, share)], rz.at[z], ss_z.at[k], rs_z.at[z], at_chip(x, d, c)
        )
    acc = zb[pl.ds(z * share, share)]
    for k in range(1, DEPTH):
        d = z_at(k)
        rdma(zr, rz.at[d], ss_z.at[k], rs_z.at[d], at_chip(x, d, c)).wait_recv()
        acc += rz[d]
    zr[...] = acc
    mine = pl.ds(z * share, share)
    for k in range(1, DEPTH):
        d = z_at(k)
        send(zr, zf.at[mine], ss_g.at[k], rs_g.at[z], at_chip(x, d, c))
    zf[mine] = acc

    has_extra = (lax.rem(j, 5) == 2) & (j < 5 * EXTRA)
    pad_rows = jp.shape[1]

    def take(e):
        lanes = slice(e * LANE, (e + 1) * LANE)

        def strip_rows(s):
            pltpu.make_async_copy(jp.at[0], jr.at[e, s], rs_j.at[e, s]).wait()
            return jr[e, s].astype(F32)

        @pl.loop(0, CHIPS // DEPTH)
        def _(q):
            first = pl.multiple_of(q * (jrows * DEPTH), DEPTH)
            view = jf.at[pl.ds(first, jrows * DEPTH + DEPTH)]
            for r in range(DEPTH):
                view[r * jrows : r * jrows + pad_rows, lanes] = strip_rows(q * DEPTH + r)

        @pl.when(c == 0)
        def _():
            jf[CHIPS * jrows : CHIPS * jrows + pad_rows, lanes] = strip_rows(CHIPS)

    take(0)

    @pl.when(has_extra)
    def _():
        take(1)

    base = split - (split // jrows) * jrows
    jb[...] = jf[pl.ds(pl.multiple_of(base * c, 8), jb.shape[0])].astype(BF16)

    for k in range(1, DEPTH):
        d = z_at(k)
        rdma(zr, zf.at[pl.ds(d * share, share)], ss_g.at[k], rs_g.at[d], sibling).wait_recv()

    class Gather:
        def __init__(self, buf, ss, rs, ring, hs, size):
            self.buf, self.ss, self.rs, self.hs = buf, ss, rs, hs
            i, self.right, self.left = ring
            self.own = rows(i, size)
            self.nr, self.far, self.nl = (rows(lax.rem(i + k, RING), size) for k in (1, 2, 3))

        def msg(self, n, h, rws, dev):
            t0, cnt = self.hs[h]
            ref = self.buf.at[pl.ds(t0, cnt), rws]
            return ref, ref, self.ss.at[n], self.rs.at[n], dev

        def start(self):
            send(*self.msg(0, 0, self.own, self.right))
            send(*self.msg(2, 1, self.own, self.left))
            send(*self.msg(1, 1, self.own, self.right))
            send(*self.msg(3, 0, self.own, self.left))

        def forward(self):
            rdma(*self.msg(0, 0, self.nl, self.right)).wait_recv()
            send(*self.msg(4, 0, self.nl, self.right))
            rdma(*self.msg(2, 1, self.nr, self.left)).wait_recv()
            send(*self.msg(5, 1, self.nr, self.left))

        def finish(self):
            rdma(*self.msg(1, 1, self.nl, self.right)).wait_recv()
            rdma(*self.msg(3, 0, self.nr, self.left)).wait_recv()
            rdma(*self.msg(4, 0, self.far, self.right)).wait_recv()
            rdma(*self.msg(5, 1, self.far, self.left)).wait_recv()

    back2 = [
        Gather(g2, ss_a2.at[p], rs_a2.at[p], rings[1 - p], halves(p), small) for p in (0, 1)
    ]
    for p in (0, 1):
        t0, cnt = parts[p]
        g2[pl.ds(t0, cnt), back2[p].own] = zf[pl.ds(t0, cnt)]
        back2[p].start()
    for p in (0, 1):
        back2[p].forward()
    back1 = [Gather(xf, ss_a1.at[p], rs_a1.at[p], rings[p], halves(p), big) for p in (0, 1)]
    for p in (0, 1):
        t0, cnt = parts[p]
        back2[p].finish()
        xf[pl.ds(t0, cnt), back1[p].own] = g2[pl.ds(t0, cnt)]
        back1[p].start()
    for p in (0, 1):
        back1[p].forward()
    for p in (0, 1):
        back1[p].finish()

    reach = steps[...] * width - c * split

    def masked(t, n):
        span = n * LANE
        block = jnp.concatenate([xf[t + k] for k in range(n)], axis=1)
        hi = block.astype(BF16)
        lo = (block - hi.astype(F32)).astype(BF16)
        vega = jnp.dot(wide, jnp.concatenate([hi, lo, hi], axis=0), preferred_element_type=F32)
        column = lax.broadcasted_iota(jnp.int32, (trades, span), 1) + t * LANE
        cols = pl.ds(pl.multiple_of(t * LANE, LANE), span)
        mk[:, cols] = jnp.where(column < reach, vega, 0.0).astype(BF16)

    @pl.loop(0, half // 2)
    def _(i):
        masked(2 * i, 2)

    masked(half - 1, 1)

    block_rows = trades // RING
    strip = out.shape[0]

    def block_copy(e, b):
        blk = rows(b, DEPTH)
        return (
            pm.at[e, blk, sib], pr.at[e, blk], ss_p.at[e, b], rs_p.at[e, b], sibling,
        )

    @pl.loop(0, RING)
    def _(b):
        part = jnp.dot(
            mk[rows(b, block_rows)], jb[...], preferred_element_type=F32
        )
        for e in (0, 1):
            pm[e, rows(b, DEPTH)] = part[:, e * LANE : (e + 1) * LANE].reshape(
                DEPTH, 2, strip, LANE
            )
        rdma(*block_copy(0, b)).start()

        @pl.when(has_extra)
        def _():
            rdma(*block_copy(1, b)).start()

    def finish_block(e, tile, b):
        rdma(*block_copy(e, b)).wait()
        blk = rows(b, DEPTH)
        po[e, blk] = pm[e, blk, c] + pr[e, blk]

        @pl.loop(b * DEPTH, (b + 1) * DEPTH)
        def _(k):
            @pl.when(k != j)
            def _():
                rdma(
                    po.at[e, k], ob.at[tile], ss_o.at[e, k], rs_o.at[tile],
                    {"grp": y, "path": 2 * k + c},
                ).start()

            @pl.when(k == j)
            def _():
                ob[tile] = po[e, k]

    @pl.loop(0, RING)
    def _(b):
        finish_block(0, j, b)

        @pl.when(has_extra)
        def _():
            finish_block(1, CHIPS + lax.div(j, 5), b)

    @pl.loop(0, jt)
    def _(t):
        owner = jnp.where(t < CHIPS, t, 5 * (t - CHIPS) + 2)

        @pl.when(owner != j)
        def _():
            rdma(po.at[0, 0], ob.at[t], ss_o.at[0, 0], rs_o.at[t], sibling).wait_recv()

    for t in range(jt - 1):
        out[:, t * LANE : (t + 1) * LANE] = ob[t]
    out[:, (jt - 1) * LANE : params] = ob[jt - 1, :, 0:jl]

    for d in sent:
        d.wait_send()

    def j_sent(n, tile, chip, core):
        @pl.when(chip * 2 + core != me)
        def _():
            rdma(
                jp.at[0], jr.at[0, 0], ss_j.at[n, tile], rs_j.at[0, 0], sibling
            ).wait_send()

    @pl.loop(0, jt)
    def _(t):
        owner = jnp.where(t < CHIPS, t, 5 * (t - CHIPS) + 2)
        j_sent(0, t, owner, top)

        @pl.when(straddle)
        def _():
            j_sent(1, t, owner, 0)

    @pl.loop(0, CHIPS)
    def _(k):
        @pl.when(k != j)
        def _():
            rdma(po.at[0, 0], ob.at[0], ss_o.at[0, k], rs_o.at[0], sibling).wait_send()

            @pl.when(has_extra)
            def _():
                rdma(po.at[0, 0], ob.at[0], ss_o.at[1, k], rs_o.at[0], sibling).wait_send()


def per_device(
    path_sens, discounts, cash_flows, flow_index, exercise_step, trade_steps, jacobian_inv
):
    paths_own, params = path_sens.shape
    forwards = discounts.shape[1]
    trades = cash_flows.shape[0]
    jrows = jacobian_inv.shape[0]
    strip = trades // (2 * CHIPS)
    tiles = -(-params // LANE)
    half = -(-tiles // 2)
    cut = half // 2 + 1
    quarter = (cut + 1) // 2
    big, small = forwards // RING, forwards // RING // RING
    share = -(-half // DEPTH)
    padded = -(-jrows // 16) * 16
    vm = pltpu.VMEM
    dma = pltpu.SemaphoreType.DMA
    scratch = [
        vm((half, paths_own, LANE), BF16),
        vm((half, paths_own, LANE), BF16),
        vm((paths_own, forwards), BF16),
        vm((half, forwards, LANE), F32),
        vm((2, 6, quarter, big, LANE), F32),
        vm((half, big, LANE), F32),
        vm((2, 6, quarter, small, LANE), F32),
        vm((share * DEPTH, small, LANE), F32),
        vm((DEPTH, share, small, LANE), F32),
        vm((share, small, LANE), F32),
        vm((share * DEPTH, small, LANE), F32),
        vm((half, big, LANE), F32),
        vm((half, forwards, LANE), F32),
        vm((tiles, padded, LANE), BF16),
        vm((2, CHIPS + 1, padded, LANE), BF16),
        vm(((CHIPS + 2) * padded, 2 * LANE), F32),
        vm((half * LANE, 2 * LANE), BF16),
        vm((trades, half * LANE), BF16),
        vm((2, CHIPS, 2, strip, LANE), F32),
        vm((2, CHIPS, strip, LANE), F32),
        vm((2, CHIPS, strip, LANE), F32),
        vm((tiles, strip, LANE), F32),
        dma((5,)), dma((5,)),
        dma((2, 6)), dma((2, 6)),
        dma((2, 6)), dma((2, 6)),
        dma((DEPTH,)), dma((DEPTH,)),
        dma((DEPTH,)), dma((DEPTH,)),
        dma((2, 6)), dma((2, 6)),
        dma((2, 6)), dma((2, 6)),
        dma((2, tiles)), dma((2, CHIPS + 1)),
        dma((2, RING)), dma((2, RING)),
        dma((2, CHIPS)), dma((tiles,)),
    ]
    return pl.pallas_call(
        kernel,
        out_shape=jax.ShapeDtypeStruct((strip, params), F32),
        in_specs=[pl.BlockSpec(memory_space=pltpu.VMEM)] * 7,
        out_specs=pl.BlockSpec(memory_space=pltpu.VMEM),
        scratch_shapes=scratch,
        compiler_params=pltpu.CompilerParams(
            collective_id=0, has_side_effects=True, vmem_limit_bytes=56 * 1024 * 1024
        ),
    )(
        discounts,
        path_sens,
        cash_flows,
        flow_index,
        exercise_step.reshape(trades, 1),
        trade_steps.reshape(trades, 1),
        jacobian_inv,
    )


def solution(mesh):
    placed = (
        P(("grp", "path"), None),
        P(("grp", "path"), None),
        P("grp", None),
        P("grp", None),
        P("grp"),
        P("grp"),
        P("path", None),
    )
    return jax.shard_map(
        per_device, mesh=mesh, in_specs=placed, out_specs=P(("grp", "path"), None), check_vma=False
    )
```

```python
import jax
import jax.numpy as jnp
from jax import lax
from jax.experimental import pallas as pl
from jax.experimental.pallas import tpu as pltpu
from jax.sharding import PartitionSpec as P

NB = 40
LANE = 128
RING = 4
DEPTH = 8
CHIPS = RING * DEPTH
PATHS = 2 * CHIPS
EXTRA = 6
F32 = jnp.float32
BF16 = jnp.bfloat16
MESH = pl.DeviceIdType.MESH


def kernel(
    disc, sens, cash, index, exer, steps, jac, out,
    s_own, s_in, d_in, xs, xp, r1, y2, r2, zb, rz, zr, zf, xf,
    jv, jp, jr, jt, mk, acc, acce, pr, pre, po, ob,
    ss_s, rs_s, ls, ss_1, rs_1, ss_2, rs_2, ss_z, rs_z, ss_g, rs_g,
    ss_a2, rs_a2, ss_a1, rs_a1, ss_j, rs_j, ss_ja, rs_ja, ss_p, rs_p, ss_o, rs_o,
):
    y = lax.axis_index("grp")
    me = lax.axis_index("path")
    j = lax.div(me, 2)
    c = lax.rem(me, 2)
    x = lax.div(j, DEPTH)
    z = lax.rem(j, DEPTH)
    sib = 1 - c
    params = sens.shape[0]
    width = params // NB
    half = params // 2
    jrows = jac.shape[0]
    pad = xp.shape[2] // 2
    trades = cash.shape[1]

    def at_chip(xx, zz, cc):
        return {"grp": y, "path": (xx * DEPTH + zz) * 2 + cc}

    def rdma(src, dst, ss, rs, dev):
        return pltpu.make_async_remote_copy(
            src_ref=src, dst_ref=dst, send_sem=ss, recv_sem=rs, device_id=dev, device_id_type=MESH
        )

    sent = []

    def send(*args):
        d = rdma(*args)
        d.start()
        sent.append(d)

    sibling = at_chip(x, z, sib)

    def on_x(k):
        return at_chip(lax.rem(x + k, RING), z, c)

    def on_y(k):
        return {"grp": lax.rem(y + k, RING), "path": me}

    def on_z(k):
        return at_chip(x, lax.rem(z + k, DEPTH), c)

    lines = ((x, on_x), (y, on_y))

    barrier = pltpu.get_barrier_semaphore()
    partners = (
        [sibling]
        + [on_x(k) for k in range(1, RING)]
        + [on_y(k) for k in range(1, RING)]
        + [on_z(k) for k in range(1, DEPTH)]
    )
    for d in partners:
        pl.semaphore_signal(barrier, inc=1, device_id=d, device_id_type=MESH)

    own_half = pltpu.make_async_copy(
        sens.at[pl.ds(pl.multiple_of(c * half, 16), half)], s_own, ls.at[0]
    )
    own_half.start()
    jac_in = pltpu.make_async_copy(jac, jv, ls.at[1])
    jac_in.start()

    first_cut = (half // 4 // 16 + 1) * 16
    cuts = (0, first_cut, half // 2, half // 2 + first_cut, half)
    order = (0, 2, 1, 3)

    def s_copy(q):
        n = cuts[q + 1] - cuts[q]
        return (
            sens.at[pl.ds(pl.multiple_of(sib * half + cuts[q], 16), n)],
            s_in.at[pl.ds(cuts[q], n)], ss_s.at[q], rs_s.at[q], sibling,
        )

    d_copy = (disc, d_in, ss_s.at[4], rs_s.at[4], sibling)

    slots = cash.shape[0]
    forwards = lax.broadcasted_iota(jnp.int32, (LANE, trades), 0)
    late = forwards >= exer[...]
    weights = jnp.zeros((LANE, trades), F32)
    for s in range(slots):
        weights += jnp.where(late & (index[s : s + 1] == forwards), cash[s : s + 1], 0.0)
    weights = weights * (1.0 / (disc.shape[0] * PATHS * RING))
    w_hi = weights.astype(BF16)
    w_lo = (weights - w_hi.astype(F32)).astype(BF16)
    wide = jnp.concatenate([w_hi, w_hi, w_lo], axis=0)

    pl.semaphore_wait(barrier, len(partners))
    send(*d_copy)
    for q in order:
        send(*s_copy(q))

    own_half.wait()
    xs[half : half + 8] = jnp.zeros((8, LANE), F32)
    for q in order:
        xs[cuts[q] : cuts[q + 1]] = jnp.dot(
            s_own[cuts[q] : cuts[q + 1]], disc[...], preferred_element_type=F32
        )

    class Scatter:
        def __init__(self, p):
            self.p = p
            self.i, self.on = lines[p]
            self.own = self.i
            self.nr, self.far, self.nl = (lax.rem(self.i + k, RING) for k in (1, 2, 3))
            self.right, self.left = self.on(1), self.on(3)

        def msg(self, n, h, k, dev):
            p = self.p
            return xp.at[2 * p + h, k], r1.at[p, n], ss_1.at[p, n], rs_1.at[p, n], dev

        def first(self, h):
            if h == 0:
                send(*self.msg(0, 0, self.far, self.right))
                send(*self.msg(1, 0, self.nl, self.left))
            else:
                send(*self.msg(2, 1, self.far, self.left))
                send(*self.msg(3, 1, self.nr, self.right))

        def second(self, h):
            n, k, dev = ((0, self.nr, self.right), (2, self.nl, self.left))[h]
            rdma(*self.msg(n, h, k, dev)).wait_recv()
            xp[2 * self.p + h, k] += r1[self.p, n]
            send(*self.msg(4 + h, h, k, dev))

        def result(self, h):
            n = (1, 3)[h]
            rdma(*self.msg(n, h, self.own, self.left)).wait_recv()
            rdma(*self.msg(4 + h, h, self.own, self.left)).wait_recv()
            return xp[2 * self.p + h, self.own] + r1[self.p, n] + r1[self.p, 4 + h]

    one = [Scatter(p) for p in (0, 1)]
    rdma(*d_copy).wait_recv()
    for q in order:
        rdma(*s_copy(q)).wait_recv()
        xs[cuts[q] : cuts[q + 1]] += jnp.dot(
            s_in[cuts[q] : cuts[q + 1]], d_in[...], preferred_element_type=F32
        )
        for k in range(RING):
            for u in (0, 1):
                top = (8 * q + 2 * k + u) * jrows
                xp[q, k, u * pad : (u + 1) * pad] = xs[top : top + pad]
        one[q // 2].first(q % 2)

    tiles = jp.shape[0]
    tail = params - (tiles - 1) * LANE
    turn = lax.rem(z, RING) == y
    core = lax.div(x, 2)
    strip = jr.at[:, 2 * lax.rem(x, 2) + lax.div(z, RING), y, pl.ds(pl.multiple_of(c * pad, 16), pad)]
    j_sem = 4 * lax.rem(x, 2) + 2 * lax.div(z, RING) + c
    jac_in.wait()

    @pl.when(turn)
    def _():
        jp[...] = jnp.zeros(jp.shape, BF16)

        @pl.loop(0, tiles - 1)
        def _(t):
            jp[t, 0:jrows] = jv[:, pl.ds(pl.multiple_of(t * LANE, LANE), LANE)]

        jp[tiles - 1, 0:jrows, 0:tail] = jv[:, (tiles - 1) * LANE : params]

    def j_column(step):
        xx = lax.rem(x + step, RING)

        def one_tile(e, tile, zz):
            dst = (xx * DEPTH + zz) * 2 + core
            n = step * (DEPTH + EXTRA) + e * DEPTH + zz

            @pl.when(dst == me)
            def _():
                pltpu.make_async_copy(jp.at[tile], strip.at[e], rs_j.at[e, j_sem]).start()

            @pl.when(dst != me)
            def _():
                rdma(
                    jp.at[tile], strip.at[e], ss_j.at[n], rs_j.at[e, j_sem],
                    {"grp": y, "path": dst},
                ).start()

        @pl.when(turn)
        def _():
            @pl.loop(0, DEPTH)
            def _(zz):
                one_tile(0, xx * DEPTH + zz, zz)

            @pl.loop(0, EXTRA)
            def _(zz):
                one_tile(1, CHIPS + zz, zz)

    j_column(0)
    for h in (0, 1):
        for p in (0, 1):
            one[p].second(h)
    j_column(1)
    j_column(3)

    for h in (0, 1):
        for p in (0, 1):
            y2[p, 2 * h : 2 * h + 2] = one[p].result(h).reshape(2, pad, LANE)

    def two(p, k):
        i, on = lines[1 - p]
        to = lax.rem(i + k, RING)
        return y2.at[p, to], r2.at[p, i], ss_2.at[p, k], rs_2.at[p, i], on(k)

    for k in (1, 3, 2):
        for p in (0, 1):
            send(*two(p, k))
    j_column(2)

    zb[2 * pad :] = jnp.zeros((zb.shape[0] - 2 * pad, LANE), F32)
    for p in (0, 1):
        i, on = lines[1 - p]
        total = y2[p, i]
        for k in (1, 3, 2):
            frm = lax.rem(i + k, RING)
            rdma(y2.at[p, i], r2.at[p, frm], ss_2.at[p, k], rs_2.at[p, frm], on(k)).wait_recv()
            total += r2[p, frm]
        zb[p * pad : (p + 1) * pad] = total

    share = zr.shape[0]

    def z_rows(d):
        return pl.ds(pl.multiple_of(d * share, 8), share)

    spread = (4, 3, 5, 2, 6, 1, 7)
    for k in spread:
        send(zb.at[z_rows(lax.rem(z + k, DEPTH))], rz.at[z], ss_z.at[k], rs_z.at[z], on_z(k))

    has_extra = z < EXTRA
    jblocks = jr.shape[1] * 2

    def j_ring(e, half_, k, n, dev):
        ref = jr.at[e, pl.ds(2 * half_, 2), k]
        return ref, ref, ss_ja.at[e, n], rs_ja.at[e, n], dev

    yr, yl = on_y(1), on_y(3)
    ynr, yfar, ynl = (lax.rem(y + k, RING) for k in (1, 2, 3))

    def j_start(e):
        for n in range(jblocks):
            pltpu.make_async_copy(
                jp.at[0], jr.at[e, n // 2, 0, pl.ds(0, pad)], rs_j.at[e, n]
            ).wait()
        for n, (hh, d) in enumerate(((0, yr), (1, yl), (1, yr), (0, yl))):
            rdma(*j_ring(e, hh, y, n, d)).start()

    def j_forward(e):
        rdma(*j_ring(e, 0, ynl, 0, yr)).wait_recv()
        rdma(*j_ring(e, 0, ynl, 4, yr)).start()
        rdma(*j_ring(e, 1, ynr, 1, yl)).wait_recv()
        rdma(*j_ring(e, 1, ynr, 5, yl)).start()

    def j_finish(e):
        for hh, k, n, d in ((1, ynl, 2, yr), (0, ynr, 3, yl), (0, yfar, 4, yr), (1, yfar, 5, yl)):
            rdma(*j_ring(e, hh, k, n, d)).wait_recv()

        @pl.loop(0, jr.shape[1] * RING)
        def _(n):
            block = jr[e, lax.div(n, RING), lax.rem(n, RING)]
            jt[e, n] = block.astype(F32).T.astype(BF16)

    def both(f):
        f(0)

        @pl.when(has_extra)
        def _():
            f(1)

    total = zb[z_rows(z)]
    for k in spread:
        d = lax.rem(z + k, DEPTH)
        rdma(zr, rz.at[d], ss_z.at[k], rs_z.at[d], on_z(k)).wait_recv()
        total += rz[d]
    zr[...] = total
    for k in spread:
        send(zr, zf.at[z_rows(z)], ss_g.at[k], rs_g.at[z], on_z(k))
    zf[z_rows(z)] = total

    both(j_start)

    for k in spread:
        d = lax.rem(z + k, DEPTH)
        rdma(zr, zf.at[z_rows(d)], ss_g.at[k], rs_g.at[d], on_z(k)).wait_recv()

    def strip_of(p, i):
        k = lines[p][0]
        return xf.at[2 * p + lax.div(i, 2), k, pl.ds(pl.multiple_of(lax.rem(i, 2) * pad, 8), pad)]

    def back2(p, k):
        i, on = lines[1 - p]
        return zf.at[pl.ds(p * pad, pad)], strip_of(p, i), ss_a2.at[p, k], rs_a2.at[p, i], on(k)

    for k in (2, 1, 3):
        for p in (0, 1):
            send(*back2(p, k))
    for p in (0, 1):
        i, _ = lines[1 - p]
        strip_of(p, i)[...] = zf[p * pad : (p + 1) * pad]

    both(j_forward)

    reach = steps[...] * width
    row = lax.broadcasted_iota(jnp.int32, (2 * pad, trades), 0)
    row = row - jnp.where(row >= pad, pad - jrows, 0) + c * half

    def block(ab, k, fresh=False):
        values = xf[ab, k]
        hi = values.astype(BF16)
        lo = (values - hi.astype(F32)).astype(BF16)
        vega = jnp.dot(jnp.concatenate([hi, lo, hi], axis=1), wide, preferred_element_type=F32)
        keep = row < reach - (8 * ab + 2 * k) * jrows
        masked = jnp.where(keep, vega, 0.0).astype(BF16)
        mk[...] = masked
        n = RING * ab + k
        part = jnp.dot(jt[0, n], masked, preferred_element_type=F32)
        for s in (0, 1):
            span = slice(s * trades // 2, (s + 1) * trades // 2)
            if fresh:
                acc[s] = part[:, span]
            else:
                acc[s] += part[:, span]

        @pl.when(has_extra)
        def _():
            mine = mk[:, pl.ds(pl.multiple_of(x * LANE, LANE), LANE)]
            more = jnp.dot(jt[1, n], mine, preferred_element_type=F32)
            if fresh:
                acce[...] = more
            else:
                acce[...] += more

    class Gather:
        def __init__(self, p):
            self.p = p
            self.i, self.on = lines[p]
            self.nr, self.far, self.nl = (lax.rem(self.i + k, RING) for k in (1, 2, 3))
            self.right, self.left = self.on(1), self.on(3)

        def msg(self, n, h, k, dev):
            ref = xf.at[2 * self.p + h, k]
            return ref, ref, ss_a1.at[self.p, n], rs_a1.at[self.p, n], dev

        def start(self):
            send(*self.msg(0, 0, self.i, self.right))
            send(*self.msg(1, 1, self.i, self.left))
            send(*self.msg(2, 1, self.i, self.right))
            send(*self.msg(3, 0, self.i, self.left))

        def forward(self):
            rdma(*self.msg(0, 0, self.nl, self.right)).wait_recv()
            send(*self.msg(4, 0, self.nl, self.right))
            rdma(*self.msg(1, 1, self.nr, self.left)).wait_recv()
            send(*self.msg(5, 1, self.nr, self.left))

        def near(self):
            rdma(*self.msg(2, 1, self.nl, self.right)).wait_recv()
            rdma(*self.msg(3, 0, self.nr, self.left)).wait_recv()

        def end(self):
            rdma(*self.msg(4, 0, self.far, self.right)).wait_recv()
            rdma(*self.msg(5, 1, self.far, self.left)).wait_recv()

    ring = [Gather(p) for p in (0, 1)]
    for p in (0, 1):
        i, on = lines[1 - p]
        for k in (1, 3, 2):
            frm = lax.rem(i + k, RING)
            rdma(
                zf.at[pl.ds(p * pad, pad)], strip_of(p, frm), ss_a2.at[p, k], rs_a2.at[p, frm],
                on(k),
            ).wait_recv()
        ring[p].start()

    both(j_finish)

    def blocks(p, k, fresh=False):
        if fresh:
            block(2 * p, k, True)
            block(2 * p + 1, k)
        else:

            @pl.loop(2 * p, 2 * p + 2)
            def _(ab):
                block(ab, k)

    ring[0].forward()
    ring[1].forward()
    blocks(0, ring[0].i, True)
    blocks(1, ring[1].i)
    for p in (0, 1):
        ring[p].near()
        blocks(p, ring[p].nl)
        blocks(p, ring[p].nr)
    for p in (0, 1):
        ring[p].end()
        blocks(p, ring[p].far)

    swap = (acc.at[sib], pr, ss_p.at[0], rs_p.at[0], sibling)
    send(*swap)
    closer = lax.rem(z, 2)
    swap_extra = (acce, pre, ss_p.at[1], rs_p.at[1], sibling)

    @pl.when(has_extra & (c != closer))
    def _():
        rdma(*swap_extra).start()

    strip_rows = out.shape[0]
    rdma(*swap).wait_recv()
    po[0] = (acc[c] + pr[...]).T.reshape(CHIPS, strip_rows, LANE)

    def deliver(e, n, tile, dst):
        @pl.when(dst != me)
        def _():
            rdma(
                po.at[e, n], ob.at[tile], ss_o.at[e, n], rs_o.at[tile], {"grp": y, "path": dst}
            ).start()

        @pl.when(dst == me)
        def _():
            ob[tile] = po[e, n]

    @pl.loop(0, CHIPS)
    def _(n):
        deliver(0, n, j, c * CHIPS + n)

    closing = has_extra & (c == closer)

    @pl.when(closing)
    def _():
        rdma(*swap_extra).wait_recv()
        po[1, 0 : CHIPS // 2] = (acce[...] + pre[...]).T.reshape(CHIPS // 2, strip_rows, LANE)

        @pl.loop(0, CHIPS // 2)
        def _(n):
            deliver(1, n, CHIPS + z, x * (CHIPS // 2) + n)

    def arrived(tile, frm):
        @pl.when(frm != me)
        def _():
            rdma(po.at[0, 0], ob.at[tile], ss_o.at[0, 0], rs_o.at[tile], sibling).wait_recv()

    @pl.loop(0, CHIPS)
    def _(t):
        arrived(t, 2 * t + core)

    @pl.loop(0, EXTRA)
    def _(e):
        arrived(CHIPS + e, (x * DEPTH + e) * 2 + lax.rem(e, 2))

    for t in range(tiles - 1):
        out[:, t * LANE : (t + 1) * LANE] = ob[t]
    out[:, (tiles - 1) * LANE : params] = ob[tiles - 1, :, 0:tail]

    for d in sent:
        d.wait_send()

    @pl.when(has_extra & (c != closer))
    def _():
        rdma(*swap_extra).wait_send()

    def j_sent(e):
        for n, hh in enumerate((0, 1, 1, 0, 0, 1)):
            rdma(*j_ring(e, hh, y, n, yr)).wait_send()

    both(j_sent)

    @pl.when(turn)
    def _():
        for step in range(RING):
            xx = lax.rem(x + step, RING)

            @pl.loop(0, DEPTH + EXTRA)
            def _(n):
                zz = jnp.where(n < DEPTH, n, n - DEPTH)

                @pl.when((xx * DEPTH + zz) * 2 + core != me)
                def _():
                    rdma(
                        jp.at[0], strip.at[0], ss_j.at[step * (DEPTH + EXTRA) + n],
                        rs_j.at[0, 0], sibling,
                    ).wait_send()

    def po_sent(e, n, dst):
        @pl.when(dst != me)
        def _():
            rdma(po.at[0, 0], ob.at[0], ss_o.at[e, n], rs_o.at[0], sibling).wait_send()

    @pl.loop(0, CHIPS)
    def _(n):
        po_sent(0, n, c * CHIPS + n)

    @pl.when(closing)
    def _():
        @pl.loop(0, CHIPS // 2)
        def _(n):
            po_sent(1, n, x * (CHIPS // 2) + n)


def per_device(
    path_sens, discounts, cash_flows, flow_index, exercise_step, trade_steps, jacobian_inv
):
    paths_own, params = path_sens.shape
    trades = cash_flows.shape[0]
    jrows = jacobian_inv.shape[0]
    strip = trades // PATHS
    tiles = -(-params // LANE)
    pad = -(-jrows // 16) * 16
    half = params // 2
    share = -(-2 * pad // (8 * DEPTH)) * 8
    vm = pltpu.VMEM
    dma = pltpu.SemaphoreType.DMA
    scratch = [
        vm((half, paths_own), BF16),
        vm((half, paths_own), BF16),
        vm((paths_own, LANE), BF16),
        vm((half + 8, LANE), F32),
        vm((RING, RING, 2 * pad, LANE), F32),
        vm((2, 6, 2 * pad, LANE), F32),
        vm((2, RING, pad, LANE), F32),
        vm((2, RING, pad, LANE), F32),
        vm((share * DEPTH, LANE), F32),
        vm((DEPTH, share, LANE), F32),
        vm((share, LANE), F32),
        vm((share * DEPTH, LANE), F32),
        vm((RING, RING, 2 * pad, LANE), F32),
        vm((jrows, params), BF16),
        vm((tiles, pad, LANE), BF16),
        vm((2, RING, RING, 2 * pad, LANE), BF16),
        vm((2, RING * RING, LANE, 2 * pad), BF16),
        vm((2 * pad, trades), BF16),
        vm((2, LANE, trades // 2), F32),
        vm((LANE, LANE), F32),
        vm((LANE, trades // 2), F32),
        vm((LANE, LANE), F32),
        vm((2, CHIPS, strip, LANE), F32),
        vm((tiles, strip, LANE), F32),
        dma((5,)), dma((5,)), dma((2,)),
        dma((2, 6)), dma((2, 6)),
        dma((2, RING)), dma((2, RING)),
        dma((DEPTH,)), dma((DEPTH,)),
        dma((DEPTH,)), dma((DEPTH,)),
        dma((2, RING)), dma((2, RING)),
        dma((2, 6)), dma((2, 6)),
        dma((RING * (DEPTH + EXTRA),)), dma((2, 8)),
        dma((2, 6)), dma((2, 6)),
        dma((2,)), dma((2,)),
        dma((2, CHIPS)), dma((tiles,)),
    ]
    vmem = pl.BlockSpec(memory_space=pltpu.VMEM)
    hbm = pl.BlockSpec(memory_space=pl.ANY)
    return pl.pallas_call(
        kernel,
        out_shape=jax.ShapeDtypeStruct((strip, params), F32),
        in_specs=[vmem, hbm, vmem, vmem, vmem, vmem, hbm],
        out_specs=vmem,
        scratch_shapes=scratch,
        compiler_params=pltpu.CompilerParams(
            collective_id=0, has_side_effects=True, vmem_limit_bytes=56 * 1024 * 1024
        ),
    )(
        discounts,
        path_sens.T,
        cash_flows.T,
        flow_index.T,
        exercise_step.reshape(1, trades),
        trade_steps.reshape(1, trades),
        jacobian_inv,
    )


def solution(mesh):
    placed = (
        P(("grp", "path"), None),
        P(("grp", "path"), None),
        P("grp", None),
        P("grp", None),
        P("grp"),
        P("grp"),
        P("path", None),
    )
    return jax.shard_map(
        per_device, mesh=mesh, in_specs=placed, out_specs=P(("grp", "path"), None), check_vma=False
    )
```

```python
import jax
import jax.numpy as jnp
from jax import lax
from jax.experimental import pallas as pl
from jax.experimental.pallas import tpu as pltpu
from jax.sharding import PartitionSpec as P

NB = 40
LANE = 128
RING = 4
DEPTH = 8
CHIPS = RING * DEPTH
PATHS = 2 * CHIPS
EXTRA = 6
F32 = jnp.float32
BF16 = jnp.bfloat16
MESH = pl.DeviceIdType.MESH


def kernel(
    disc, sens, cash, index, exer, steps, jac, out,
    dv, cv, iv, ev, sv, s_own, s_in, d_in, xs, xp, r1, y2, r2, zb, rz, zr, zf, xf,
    jv, jp, jr, jt, mk, acc, acce, pr, pre, po, ob,
    ss_s, rs_s, ls, ss_1, rs_1, ss_2, rs_2, ss_z, rs_z, ss_g, rs_g,
    ss_a2, rs_a2, ss_a1, rs_a1, ss_j, rs_j, ss_ja, rs_ja, ss_p, rs_p, ss_o, rs_o,
):
    y = lax.axis_index("grp")
    me = lax.axis_index("path")
    j = lax.div(me, 2)
    c = lax.rem(me, 2)
    x = lax.div(j, DEPTH)
    z = lax.rem(j, DEPTH)
    sib = 1 - c
    params = sens.shape[0]
    width = params // NB
    half = params // 2
    jrows = jac.shape[0]
    pad = xp.shape[2] // 2
    trades = cash.shape[1]

    def at_chip(xx, zz, cc):
        return {"grp": y, "path": (xx * DEPTH + zz) * 2 + cc}

    def rdma(src, dst, ss, rs, dev):
        return pltpu.make_async_remote_copy(
            src_ref=src, dst_ref=dst, send_sem=ss, recv_sem=rs, device_id=dev, device_id_type=MESH
        )

    sent = []

    def send(*args):
        d = rdma(*args)
        d.start()
        sent.append((None, d))

    def send_if(cond, *args):
        d = rdma(*args)

        @pl.when(cond)
        def _():
            d.start()

        sent.append((cond, d))

    sibling = at_chip(x, z, sib)

    def on_x(k):
        return at_chip(lax.rem(x + k, RING), z, c)

    def on_y(k):
        return {"grp": lax.rem(y + k, RING), "path": me}

    def on_z(k):
        return at_chip(x, lax.rem(z + k, DEPTH), c)

    lines = ((x, on_x), (y, on_y))

    barrier = pltpu.get_barrier_semaphore()
    partners = (
        [sibling]
        + [on_x(k) for k in range(1, RING)]
        + [on_y(k) for k in range(1, RING)]
        + [on_z(k) for k in range(1, DEPTH)]
    )
    for d in partners:
        pl.semaphore_signal(barrier, inc=1, device_id=d, device_id_type=MESH)

    fetched = [
        pltpu.make_async_copy(src, dst, ls.at[n])
        for n, (src, dst) in enumerate(
            (
                (disc, dv),
                (sens.at[pl.ds(pl.multiple_of(c * half, 16), half)], s_own),
                (cash, cv), (index, iv), (exer, ev), (steps, sv), (jac, jv),
            )
        )
    ]
    for f in fetched:
        f.start()

    first_cut = (half // 4 // 16 + 1) * 16
    cuts = (0, first_cut, half // 2, half // 2 + first_cut, half)

    def s_copy(q):
        n = cuts[q + 1] - cuts[q]
        return (
            sens.at[pl.ds(pl.multiple_of(sib * half + cuts[q], 16), n)],
            s_in.at[pl.ds(cuts[q], n)], ss_s.at[q], rs_s.at[q], sibling,
        )

    d_copy = (disc, d_in, ss_s.at[RING], rs_s.at[RING], sibling)

    pl.semaphore_wait(barrier, len(partners))
    send(*d_copy)
    for q in range(RING):
        send(*s_copy(q))

    xs[half : half + 8] = jnp.zeros((8, LANE), F32)
    for f in fetched[:2]:
        f.wait()
    for q in range(RING):
        xs[cuts[q] : cuts[q + 1]] = jnp.dot(
            s_own[cuts[q] : cuts[q + 1]], dv[...], preferred_element_type=F32
        )

    def part_rows(n, size):
        return pl.ds(pl.multiple_of(n * size, 8), size)

    class Scatter:
        def __init__(self, q):
            self.q = q
            self.i, self.on = lines[q % 2]
            self.nr, self.far, self.nl = (lax.rem(self.i + k, RING) for k in (1, 2, 3))
            self.right, self.left = self.on(1), self.on(3)

        def msg(self, n, h, k, dev):
            q = self.q
            return (
                xp.at[q, k, h * pad : (h + 1) * pad], r1.at[q, n],
                ss_1.at[q, n], rs_1.at[q, n], dev,
            )

        def first(self):
            send(*self.msg(0, 0, self.far, self.right))
            send(*self.msg(2, 1, self.far, self.left))
            send(*self.msg(3, 1, self.nr, self.right))
            send(*self.msg(1, 0, self.nl, self.left))

        def second(self):
            for h, n, k, dev in ((0, 0, self.nr, self.right), (1, 2, self.nl, self.left)):
                rdma(*self.msg(n, h, k, dev)).wait_recv()
                xp[self.q, k, h * pad : (h + 1) * pad] += r1[self.q, n]
                send(*self.msg(4 + h, h, k, dev))

        def result(self):
            for h, n in ((0, 1), (1, 3)):
                rdma(*self.msg(n, h, self.i, self.left)).wait_recv()
                rdma(*self.msg(4 + h, h, self.i, self.left)).wait_recv()
                rws = slice(h * pad, (h + 1) * pad)
                y2[self.q, rws] = xp[self.q, self.i, rws] + r1[self.q, n] + r1[self.q, 4 + h]

    one = [Scatter(q) for q in range(RING)]
    rdma(*d_copy).wait_recv()
    for q in range(RING):
        rdma(*s_copy(q)).wait_recv()
        xs[cuts[q] : cuts[q + 1]] += jnp.dot(
            s_in[cuts[q] : cuts[q + 1]], d_in[...], preferred_element_type=F32
        )
        for k in range(RING):
            for u in (0, 1):
                top = (8 * q + 2 * k + u) * jrows
                xp[q, k, u * pad : (u + 1) * pad] = xs[top : top + pad]
        one[q].first()

    tiles = jp.shape[0]
    tail = params - (tiles - 1) * LANE
    turn = lax.rem(z, RING) == y
    core = lax.div(x, 2)
    strip = jr.at[:, 2 * lax.rem(x, 2) + lax.div(z, RING), y, pl.ds(pl.multiple_of(c * pad, 16), pad)]
    j_sem = 4 * lax.rem(x, 2) + 2 * lax.div(z, RING) + c
    for f in fetched[2:]:
        f.wait()

    @pl.when(turn)
    def _():
        jp[...] = jnp.zeros(jp.shape, BF16)

        @pl.loop(0, tiles - 1)
        def _(t):
            jp[t, 0:jrows] = jv[:, pl.ds(pl.multiple_of(t * LANE, LANE), LANE)]

        jp[tiles - 1, 0:jrows, 0:tail] = jv[:, (tiles - 1) * LANE : params]

    def j_column(step):
        xx = lax.rem(x + step, RING)

        def one_tile(e, tile, zz):
            dst = (xx * DEPTH + zz) * 2 + core
            n = step * (DEPTH + EXTRA) + e * DEPTH + zz

            @pl.when(dst == me)
            def _():
                pltpu.make_async_copy(jp.at[tile], strip.at[e], rs_j.at[e, j_sem]).start()

            @pl.when(dst != me)
            def _():
                rdma(
                    jp.at[tile], strip.at[e], ss_j.at[n], rs_j.at[e, j_sem],
                    {"grp": y, "path": dst},
                ).start()

        @pl.when(turn)
        def _():
            @pl.loop(0, DEPTH)
            def _(k):
                zz = lax.rem(z + k, DEPTH)
                one_tile(0, xx * DEPTH + zz, zz)

                @pl.when(zz < EXTRA)
                def _():
                    one_tile(1, CHIPS + zz, zz)

    j_column(0)
    one[0].second()
    one[1].second()
    j_column(1)
    one[2].second()
    one[3].second()
    j_column(3)

    slots = cash.shape[0]
    forwards = lax.broadcasted_iota(jnp.int32, (LANE, trades), 0)
    late = forwards >= ev[...]
    weights = jnp.zeros((LANE, trades), F32)
    for s in range(slots):
        weights += jnp.where(late & (iv[s : s + 1] == forwards), cv[s : s + 1], 0.0)
    weights = weights * (1.0 / (disc.shape[0] * PATHS * RING))
    w_hi = weights.astype(BF16)
    w_lo = (weights - w_hi.astype(F32)).astype(BF16)
    wide = jnp.concatenate([w_hi, w_hi, w_lo], axis=0)

    part = y2.shape[1] // RING

    def two(q, k):
        i, on = lines[1 - q % 2]
        return (
            y2.at[q, part_rows(lax.rem(i + k, RING), part)], r2.at[q, i],
            ss_2.at[q, k], rs_2.at[q, i], on(k),
        )

    for g in (0, 1):
        for q in (2 * g, 2 * g + 1):
            one[q].result()
            for k in (2, 1, 3):
                send(*two(q, k))
    j_column(2)

    share = zr.shape[1]
    count = 2 * part // share
    spread = (4, 3, 5, 2, 6, 1, 7)

    def turn_of(g, d):
        return lax.rem(d + count * g, DEPTH)

    def z_piece(g, d):
        return part_rows(jnp.minimum(turn_of(g, d), count - 1), share)

    for g in (0, 1):
        for p in (0, 1):
            q = 2 * g + p
            i, on = lines[1 - p]
            total = y2[q, part_rows(i, part)]
            for k in (1, 3, 2):
                frm = lax.rem(i + k, RING)
                rdma(
                    y2.at[q, part_rows(i, part)], r2.at[q, frm], ss_2.at[q, k], rs_2.at[q, frm],
                    on(k),
                ).wait_recv()
                total += r2[q, frm]
            zb[g, p * part : (p + 1) * part] = total
        for k in spread:
            d = lax.rem(z + k, DEPTH)
            send_if(
                turn_of(g, d) < count,
                zb.at[g, z_piece(g, d)], rz.at[g, z], ss_z.at[g, k], rs_z.at[g, z], on_z(k),
            )

    has_extra = z < EXTRA
    jblocks = jr.shape[1] * 2

    def j_ring(e, half_, k, n, dev):
        ref = jr.at[e, pl.ds(2 * half_, 2), k]
        return ref, ref, ss_ja.at[e, n], rs_ja.at[e, n], dev

    yr, yl = on_y(1), on_y(3)
    ynr, yfar, ynl = (lax.rem(y + k, RING) for k in (1, 2, 3))

    def j_start(e):
        for n in range(jblocks):
            pltpu.make_async_copy(
                jp.at[0], jr.at[e, n // 2, 0, pl.ds(0, pad)], rs_j.at[e, n]
            ).wait()
        for n, (hh, d) in enumerate(((0, yr), (1, yl), (1, yr), (0, yl))):
            rdma(*j_ring(e, hh, y, n, d)).start()

    def j_forward(e):
        rdma(*j_ring(e, 0, ynl, 0, yr)).wait_recv()
        rdma(*j_ring(e, 0, ynl, 4, yr)).start()
        rdma(*j_ring(e, 1, ynr, 1, yl)).wait_recv()
        rdma(*j_ring(e, 1, ynr, 5, yl)).start()

    def j_finish(e):
        for hh, k, n, d in ((1, ynl, 2, yr), (0, ynr, 3, yl), (0, yfar, 4, yr), (1, yfar, 5, yl)):
            rdma(*j_ring(e, hh, k, n, d)).wait_recv()

        @pl.loop(0, jr.shape[1] * RING)
        def _(n):
            jt[e, n] = jr[e, lax.div(n, RING), lax.rem(n, RING)].T

    def both(f):
        f(0)

        @pl.when(has_extra)
        def _():
            f(1)

    for g in (0, 1):
        reducer = turn_of(g, z) < count

        @pl.when(reducer)
        def _():
            total = zb[g, z_piece(g, z)]
            for k in spread:
                d = lax.rem(z + k, DEPTH)
                rdma(zr.at[g], rz.at[g, d], ss_z.at[g, k], rs_z.at[g, d], on_z(k)).wait_recv()
                total += rz[g, d]
            zr[g] = total
            zf[g, z_piece(g, z)] = total

        for k in spread:
            send_if(
                reducer, zr.at[g], zf.at[g, z_piece(g, z)], ss_g.at[g, k], rs_g.at[g, z], on_z(k)
            )

    both(j_start)

    def home(q, i):
        return xf.at[q, lines[q % 2][0], part_rows(i, part)]

    for g in (0, 1):
        for k in spread:
            d = lax.rem(z + k, DEPTH)

            @pl.when(turn_of(g, d) < count)
            def _():
                rdma(
                    zr.at[g], zf.at[g, z_piece(g, d)], ss_g.at[g, k], rs_g.at[g, d], on_z(k)
                ).wait_recv()

        for p in (0, 1):
            q = 2 * g + p
            i, on = lines[1 - p]
            mine = zf.at[g, p * part : (p + 1) * part]
            for k in (2, 1, 3):
                send(mine, home(q, i), ss_a2.at[q, k], rs_a2.at[q, i], on(k))
            home(q, i)[...] = mine[...]

    both(j_forward)

    class Gather:
        def __init__(self, q):
            self.q = q
            self.i, self.on = lines[q % 2]
            self.nr, self.far, self.nl = (lax.rem(self.i + k, RING) for k in (1, 2, 3))
            self.right, self.left = self.on(1), self.on(3)

        def msg(self, n, h, k, dev):
            ref = xf.at[self.q, k, h * pad : (h + 1) * pad]
            return ref, ref, ss_a1.at[self.q, n], rs_a1.at[self.q, n], dev

        def start(self):
            q = self.q
            i, on = lines[1 - q % 2]
            for k in (1, 3, 2):
                frm = lax.rem(i + k, RING)
                rdma(
                    zf.at[0, 0:part], home(q, frm), ss_a2.at[q, k], rs_a2.at[q, frm], on(k)
                ).wait_recv()
            send(*self.msg(0, 0, self.i, self.right))
            send(*self.msg(1, 1, self.i, self.left))
            send(*self.msg(2, 1, self.i, self.right))
            send(*self.msg(3, 0, self.i, self.left))

        def forward(self):
            rdma(*self.msg(0, 0, self.nl, self.right)).wait_recv()
            send(*self.msg(4, 0, self.nl, self.right))
            rdma(*self.msg(1, 1, self.nr, self.left)).wait_recv()
            send(*self.msg(5, 1, self.nr, self.left))

        def near(self):
            rdma(*self.msg(2, 1, self.nl, self.right)).wait_recv()
            rdma(*self.msg(3, 0, self.nr, self.left)).wait_recv()

        def end(self):
            rdma(*self.msg(4, 0, self.far, self.right)).wait_recv()
            rdma(*self.msg(5, 1, self.far, self.left)).wait_recv()

    ring = [Gather(q) for q in range(RING)]
    for q in range(RING):
        ring[q].start()
    ring[0].forward()
    ring[1].forward()

    reach = sv[...] * width
    row = lax.broadcasted_iota(jnp.int32, (2 * pad, trades), 0)
    row = row - jnp.where(row >= pad, pad - jrows, 0) + c * half

    def block(q, k, fresh=False):
        values = xf[q, k]
        hi = values.astype(BF16)
        lo = (values - hi.astype(F32)).astype(BF16)
        vega = jnp.dot(jnp.concatenate([hi, lo, hi], axis=1), wide, preferred_element_type=F32)
        keep = row < reach - (8 * q + 2 * k) * jrows
        masked = jnp.where(keep, vega, 0.0).astype(BF16)
        mk[...] = masked
        n = RING * q + k
        prod = jnp.dot(jt[0, n], masked, preferred_element_type=F32)
        for s in (0, 1):
            span = slice(s * trades // 2, (s + 1) * trades // 2)
            if fresh:
                acc[s] = prod[:, span]
            else:
                acc[s] += prod[:, span]

        @pl.when(has_extra)
        def _():
            mine = mk[:, pl.ds(pl.multiple_of(x * LANE, LANE), LANE)]
            more = jnp.dot(jt[1, n], mine, preferred_element_type=F32)
            if fresh:
                acce[...] = more
            else:
                acce[...] += more

    both(j_finish)
    block(0, ring[0].i, True)
    block(1, ring[1].i)
    ring[2].forward()
    ring[3].forward()
    block(2, ring[2].i)
    block(3, ring[3].i)
    for q in range(RING):
        ring[q].near()

        @pl.loop(0, 2)
        def _(n):
            block(q, jnp.where(n == 0, ring[q].nl, ring[q].nr))

    for q in range(RING):
        ring[q].end()
        block(q, ring[q].far)

    swap = (acc.at[sib], pr, ss_p.at[0], rs_p.at[0], sibling)
    send(*swap)
    closer = lax.rem(z, 2)
    swap_extra = (acce, pre, ss_p.at[1], rs_p.at[1], sibling)
    send_if(has_extra & (c != closer), *swap_extra)

    strip_rows = out.shape[0]
    rdma(*swap).wait_recv()
    po[0] = (acc[c] + pr[...]).T.reshape(CHIPS, strip_rows, LANE)

    def deliver(e, n, tile, dst):
        @pl.when(dst != me)
        def _():
            rdma(
                po.at[e, n], ob.at[tile], ss_o.at[e, n], rs_o.at[tile], {"grp": y, "path": dst}
            ).start()

        @pl.when(dst == me)
        def _():
            ob[tile] = po[e, n]

    turned = 2 * z + (CHIPS // 2) * lax.rem(x, 2)

    @pl.loop(0, CHIPS)
    def _(k):
        n = lax.rem(turned + k, CHIPS)
        deliver(0, n, j, c * CHIPS + n)

    closing = has_extra & (c == closer)

    @pl.when(closing)
    def _():
        rdma(*swap_extra).wait_recv()
        po[1, 0 : CHIPS // 2] = (acce[...] + pre[...]).T.reshape(CHIPS // 2, strip_rows, LANE)

        @pl.loop(0, CHIPS // 2)
        def _(k):
            n = lax.rem(2 * z + k, CHIPS // 2)
            deliver(1, n, CHIPS + z, x * (CHIPS // 2) + n)

    for cond, d in sent:
        if cond is None:
            d.wait_send()
        else:
            pl.when(cond)(d.wait_send)

    def j_sent(e):
        for n, hh in enumerate((0, 1, 1, 0, 0, 1)):
            rdma(*j_ring(e, hh, y, n, yr)).wait_send()

    both(j_sent)

    @pl.when(turn)
    def _():
        for step in range(RING):
            xx = lax.rem(x + step, RING)

            @pl.loop(0, DEPTH + EXTRA)
            def _(n):
                zz = jnp.where(n < DEPTH, n, n - DEPTH)

                @pl.when((xx * DEPTH + zz) * 2 + core != me)
                def _():
                    rdma(
                        jp.at[0], strip.at[0], ss_j.at[step * (DEPTH + EXTRA) + n],
                        rs_j.at[0, 0], sibling,
                    ).wait_send()

    def arrived(tile, frm):
        @pl.when(frm != me)
        def _():
            rdma(po.at[0, 0], ob.at[tile], ss_o.at[0, 0], rs_o.at[tile], sibling).wait_recv()

    @pl.loop(0, CHIPS)
    def _(t):
        arrived(t, 2 * t + core)

    @pl.loop(0, EXTRA)
    def _(e):
        arrived(CHIPS + e, (x * DEPTH + e) * 2 + lax.rem(e, 2))

    for t in range(tiles - 1):
        out[:, t * LANE : (t + 1) * LANE] = ob[t]
    out[:, (tiles - 1) * LANE : params] = ob[tiles - 1, :, 0:tail]

    def po_sent(e, n, dst):
        @pl.when(dst != me)
        def _():
            rdma(po.at[0, 0], ob.at[0], ss_o.at[e, n], rs_o.at[0], sibling).wait_send()

    @pl.loop(0, CHIPS)
    def _(n):
        po_sent(0, n, c * CHIPS + n)

    @pl.when(closing)
    def _():
        @pl.loop(0, CHIPS // 2)
        def _(n):
            po_sent(1, n, x * (CHIPS // 2) + n)


def per_device(
    path_sens, discounts, cash_flows, flow_index, exercise_step, trade_steps, jacobian_inv
):
    paths_own, params = path_sens.shape
    trades = cash_flows.shape[0]
    jrows = jacobian_inv.shape[0]
    strip = trades // PATHS
    tiles = -(-params // LANE)
    pad = -(-jrows // 16) * 16
    half = params // 2
    slots = cash_flows.shape[1]
    part = pad // 2
    share = 16
    vm = pltpu.VMEM
    dma = pltpu.SemaphoreType.DMA
    scratch = [
        vm((paths_own, LANE), BF16),
        vm((slots, trades), F32),
        vm((slots, trades), jnp.int32),
        vm((1, trades), jnp.int32),
        vm((1, trades), jnp.int32),
        vm((half, paths_own), BF16),
        vm((half, paths_own), BF16),
        vm((paths_own, LANE), BF16),
        vm((half + 8, LANE), F32),
        vm((RING, RING, 2 * pad, LANE), F32),
        vm((RING, 6, pad, LANE), F32),
        vm((RING, 2 * pad, LANE), F32),
        vm((RING, RING, part, LANE), F32),
        vm((2, 2 * part, LANE), F32),
        vm((2, DEPTH, share, LANE), F32),
        vm((2, share, LANE), F32),
        vm((2, 2 * part, LANE), F32),
        vm((RING, RING, 2 * pad, LANE), F32),
        vm((jrows, params), BF16),
        vm((tiles, pad, LANE), BF16),
        vm((2, RING, RING, 2 * pad, LANE), BF16),
        vm((2, RING * RING, LANE, 2 * pad), BF16),
        vm((2 * pad, trades), BF16),
        vm((2, LANE, trades // 2), F32),
        vm((LANE, LANE), F32),
        vm((LANE, trades // 2), F32),
        vm((LANE, LANE), F32),
        vm((2, CHIPS, strip, LANE), F32),
        vm((tiles, strip, LANE), F32),
        dma((RING + 1,)), dma((RING + 1,)), dma((7,)),
        dma((RING, 6)), dma((RING, 6)),
        dma((RING, RING)), dma((RING, RING)),
        dma((2, DEPTH)), dma((2, DEPTH)),
        dma((2, DEPTH)), dma((2, DEPTH)),
        dma((RING, RING)), dma((RING, RING)),
        dma((RING, 6)), dma((RING, 6)),
        dma((RING * (DEPTH + EXTRA),)), dma((2, 8)),
        dma((2, 6)), dma((2, 6)),
        dma((2,)), dma((2,)),
        dma((2, CHIPS)), dma((tiles,)),
    ]
    vmem = pl.BlockSpec(memory_space=pltpu.VMEM)
    hbm = pl.BlockSpec(memory_space=pl.ANY)
    return pl.pallas_call(
        kernel,
        out_shape=jax.ShapeDtypeStruct((strip, params), F32),
        in_specs=[hbm] * 7,
        out_specs=vmem,
        scratch_shapes=scratch,
        compiler_params=pltpu.CompilerParams(
            collective_id=0, has_side_effects=True, vmem_limit_bytes=56 * 1024 * 1024
        ),
    )(
        discounts,
        path_sens.T,
        cash_flows.T,
        flow_index.T,
        exercise_step.reshape(1, trades),
        trade_steps.reshape(1, trades),
        jacobian_inv,
    )


def solution(mesh):
    placed = (
        P(("grp", "path"), None),
        P(("grp", "path"), None),
        P("grp", None),
        P("grp", None),
        P("grp"),
        P("grp"),
        P("path", None),
    )
    return jax.shard_map(
        per_device, mesh=mesh, in_specs=placed, out_specs=P(("grp", "path"), None), check_vma=False
    )
```

```python
import jax
import jax.numpy as jnp
from jax import lax
from jax.experimental import pallas as pl
from jax.experimental.pallas import tpu as pltpu
from jax.sharding import PartitionSpec as P

NB = 40
LANE = 128
RING = 4
DEPTH = 8
CHIPS = RING * DEPTH
PATHS = 2 * CHIPS
EXTRA = 6
F32 = jnp.float32
BF16 = jnp.bfloat16
MESH = pl.DeviceIdType.MESH


def kernel(
    disc, sens, cash, index, exer, steps, jac, out,
    dv, cv, iv, ev, sv, s_own, s_in, d_in, xs, xp, r1, y2, r2, zb, rz, zr, zf, xf,
    jv, jp, jz, jr, jt, mk, acc, acce, pr, pre, po, ob,
    ss_s, rs_s, ls, ss_1, rs_1, ss_2, rs_2, ss_z, rs_z, ss_g, rs_g,
    ss_a2, rs_a2, ss_a1, rs_a1, ss_j, ss_jx, rs_j, ss_ja, rs_ja, ss_p, rs_p, ss_o, rs_o, near_z,
):
    y = lax.axis_index("grp")
    me = lax.axis_index("path")
    j = lax.div(me, 2)
    c = lax.rem(me, 2)
    x = lax.div(j, DEPTH)
    z = lax.rem(j, DEPTH)
    sib = 1 - c
    params = sens.shape[0]
    width = params // NB
    half = params // 2
    jrows = jac.shape[0]
    pad = xp.shape[2] // 2
    trades = cash.shape[1]

    def at_chip(xx, zz, cc):
        return {"grp": y, "path": (xx * DEPTH + zz) * 2 + cc}

    def rdma(src, dst, ss, rs, dev):
        return pltpu.make_async_remote_copy(
            src_ref=src, dst_ref=dst, send_sem=ss, recv_sem=rs, device_id=dev, device_id_type=MESH
        )

    sent = []

    def send(*args):
        d = rdma(*args)
        d.start()
        sent.append((None, d))

    def send_if(cond, *args):
        d = rdma(*args)

        @pl.when(cond)
        def _():
            d.start()

        sent.append((cond, d))

    sibling = at_chip(x, z, sib)

    def on_x(k):
        return at_chip(lax.rem(x + k, RING), z, c)

    def on_y(k):
        return {"grp": lax.rem(y + k, RING), "path": me}

    def on_z(k):
        return at_chip(x, lax.rem(z + k, DEPTH), c)

    lines = ((x, on_x), (y, on_y))

    barrier = pltpu.get_barrier_semaphore()
    partners = [sibling] + [on(k) for on in (on_x, on_y) for k in (1, RING - 1)]
    z_next = (on_z(1), on_z(DEPTH - 1))
    partners += list(z_next)
    for d in partners:
        pl.semaphore_signal(barrier, inc=1, device_id=d, device_id_type=MESH)

    def z_tell(n):
        for k, d in enumerate(z_next):
            pl.semaphore_signal(near_z.at[n, k], inc=1, device_id=d, device_id_type=MESH)

    def z_hear(n):
        for k in (0, 1):
            pl.semaphore_wait(near_z.at[n, k], 1)

    fetched = [
        pltpu.make_async_copy(src, dst, ls.at[n])
        for n, (src, dst) in enumerate(
            (
                (disc, dv),
                (sens.at[pl.ds(pl.multiple_of(c * half, 16), half)], s_own),
                (cash, cv), (index, iv), (exer, ev), (steps, sv), (jac, jv),
            )
        )
    ]
    for f in fetched:
        f.start()

    first_cut = (half // 4 // 16 + 1) * 16
    cuts = (0, first_cut, half // 2, half // 2 + first_cut, half)

    def s_copy(q):
        n = cuts[q + 1] - cuts[q]
        return (
            sens.at[pl.ds(pl.multiple_of(sib * half + cuts[q], 16), n)],
            s_in.at[pl.ds(cuts[q], n)], ss_s.at[q], rs_s.at[q], sibling,
        )

    d_copy = (disc, d_in, ss_s.at[RING], rs_s.at[RING], sibling)

    xs[half : half + 8] = jnp.zeros((8, LANE), F32)
    for f in fetched[:2]:
        f.wait()
    third = half // 3

    @pl.loop(0, 3)
    def _(n):
        rws = pl.ds(pl.multiple_of(n * third, 16), third)
        xs[rws] = jnp.dot(s_own[rws], dv[...], preferred_element_type=F32)

    pl.semaphore_wait(barrier, len(partners))
    send(*d_copy)
    for q in range(RING):
        send(*s_copy(q))
    z_tell(0)

    tiles = out.shape[1] // LANE + 1
    tail = params - (tiles - 1) * LANE
    turn = lax.rem(z, RING) == y
    core = lax.div(x, 2)
    high = lax.div(z, RING)
    for f in fetched[2:]:
        f.wait()

    @pl.when(turn)
    def _():
        jp[...] = jnp.zeros(jp.shape, BF16)

        @pl.loop(0, DEPTH)
        def _(zz):
            for t in range(RING):
                col = pl.multiple_of((zz * RING + t) * LANE, LANE)
                jp[zz, t, 0:jrows] = jv[:, pl.ds(col, LANE)]

            @pl.when(zz < EXTRA - 1)
            def _():
                col = pl.multiple_of((CHIPS + zz) * LANE, LANE)
                jp[zz, RING, 0:jrows] = jv[:, pl.ds(col, LANE)]

        jp[EXTRA - 1, RING, 0:jrows, 0:tail] = jv[:, (tiles - 1) * LANE : params]
        pltpu.make_async_copy(jp.at[z], jz.at[high], rs_j.at[2, high]).start()

    def j_line(k):
        zz = lax.rem(z + k, DEPTH)
        return jp.at[zz], jz.at[high], ss_j.at[k], rs_j.at[2, high], on_z(k)

    def j_depth(*steps_):
        @pl.when(turn)
        def _():
            for k in steps_:
                rdma(*j_line(k)).start()

    j_depth(1, 7)

    def part_rows(n, size):
        return pl.ds(pl.multiple_of(n * size, 8), size)

    class Scatter:
        def __init__(self, q):
            self.q = q
            self.i, self.on = lines[q % 2]
            self.nr, self.far, self.nl = (lax.rem(self.i + k, RING) for k in (1, 2, 3))
            self.right, self.left = self.on(1), self.on(3)

        def msg(self, n, h, k, dev):
            q = self.q
            return (
                xp.at[q, k, h * pad : (h + 1) * pad], r1.at[q, n],
                ss_1.at[q, n], rs_1.at[q, n], dev,
            )

        def first(self):
            send(*self.msg(0, 0, self.far, self.right))
            send(*self.msg(2, 1, self.far, self.left))
            send(*self.msg(3, 1, self.nr, self.right))
            send(*self.msg(1, 0, self.nl, self.left))

        def second(self):
            for h, n, k, dev in ((0, 0, self.nr, self.right), (1, 2, self.nl, self.left)):
                rdma(*self.msg(n, h, k, dev)).wait_recv()
                xp[self.q, k, h * pad : (h + 1) * pad] += r1[self.q, n]
                send(*self.msg(4 + h, h, k, dev))

        def result(self):
            for h, n in ((0, 1), (1, 3)):
                rdma(*self.msg(n, h, self.i, self.left)).wait_recv()
                rdma(*self.msg(4 + h, h, self.i, self.left)).wait_recv()
                rws = slice(h * pad, (h + 1) * pad)
                y2[self.q, rws] = xp[self.q, self.i, rws] + r1[self.q, n] + r1[self.q, 4 + h]

    one = [Scatter(q) for q in range(RING)]
    rdma(*d_copy).wait_recv()
    for q in range(RING):
        rdma(*s_copy(q)).wait_recv()
        xs[cuts[q] : cuts[q + 1]] += jnp.dot(
            s_in[cuts[q] : cuts[q + 1]], d_in[...], preferred_element_type=F32
        )
        for k in range(RING):
            for u in (0, 1):
                top = (8 * q + 2 * k + u) * jrows
                xp[q, k, u * pad : (u + 1) * pad] = xs[top : top + pad]
        one[q].first()

    z_hear(0)
    z_tell(1)
    j_depth(2, 6)
    one[0].second()
    one[1].second()
    z_hear(1)
    z_tell(2)
    j_depth(3, 5)
    one[2].second()
    one[3].second()
    z_hear(2)
    j_depth(4)

    slots = cash.shape[0]
    forwards = lax.broadcasted_iota(jnp.int32, (LANE, trades), 0)
    late = forwards >= ev[...]
    weights = jnp.zeros((LANE, trades), F32)
    for s in range(slots):
        weights += jnp.where(late & (iv[s : s + 1] == forwards), cv[s : s + 1], 0.0)
    weights = weights * (1.0 / (disc.shape[0] * PATHS * RING))
    w_hi = weights.astype(BF16)
    w_lo = (weights - w_hi.astype(F32)).astype(BF16)
    wide = jnp.concatenate([w_hi, w_hi, w_lo], axis=0)

    part = y2.shape[1] // RING

    def two(q, k):
        i, on = lines[1 - q % 2]
        return (
            y2.at[q, part_rows(lax.rem(i + k, RING), part)], r2.at[q, i],
            ss_2.at[q, k], rs_2.at[q], on(k),
        )

    for g in (0, 1):
        for q in (2 * g, 2 * g + 1):
            one[q].result()
            for k in (2, 1, 3):
                send(*two(q, k))

    has_extra = z < EXTRA

    def j_cross(e, k):
        xx = lax.rem(x + k, RING)
        slot = xx if e == 0 else RING
        dst = jr.at[
            e, pl.ds(2 * lax.rem(x, 2), 2), y, pl.ds(pl.multiple_of(c * pad, 16), pad)
        ]
        return jz.at[:, slot], dst, ss_jx.at[e, k], rs_j.at[e, 0], at_chip(xx, z, core)

    def both(f):
        f(0)

        @pl.when(has_extra)
        def _():
            f(1)

    def j_send(e):
        for k in (2, 1, 3):
            rdma(*j_cross(e, k)).start()
        src, dst, ss, rs, dev = j_cross(e, 0)

        @pl.when(core == c)
        def _():
            pltpu.make_async_copy(src, dst, rs).start()

        @pl.when(core != c)
        def _():
            rdma(src, dst, ss, rs, dev).start()

    for n in (0, 1):
        pltpu.make_async_copy(jp.at[0], jz.at[n], rs_j.at[2, n]).wait()
    both(j_send)

    share = zr.shape[1]
    count = 2 * part // share
    spread = (4, 3, 5, 2, 6, 1, 7)

    def turn_of(g, d):
        return lax.rem(d + count * g, DEPTH)

    def reduces(g):
        return turn_of(g, z) < count

    def z_piece(g, d):
        return part_rows(jnp.minimum(turn_of(g, d), count - 1), share)

    for g in (0, 1):
        for p in (0, 1):
            q = 2 * g + p
            i, on = lines[1 - p]
            total = y2[q, part_rows(i, part)]
            three = r2.at[q, 0 : RING - 1]
            rdma(three, three, ss_2.at[q, 0], rs_2.at[q], sibling).wait_recv()
            for k in (1, 2, 3):
                total += r2[q, lax.rem(i + k, RING)]
            zb[g, p * part : (p + 1) * part] = total
        for k in spread:
            d = lax.rem(z + k, DEPTH)
            send_if(
                turn_of(g, d) < count,
                zb.at[g, z_piece(g, d)], rz.at[g, z], ss_z.at[g, k], rs_z.at[g], on_z(k),
            )


    def j_ring(e, half_, k, n, dev):
        ref = jr.at[e, pl.ds(2 * half_, 2), k]
        return ref, ref, ss_ja.at[e, n], rs_ja.at[e, n], dev

    yr, yl = on_y(1), on_y(3)
    ynr, yfar, ynl = (lax.rem(y + k, RING) for k in (1, 2, 3))

    def j_start(e):
        whole = jr.at[e, :, y]
        pltpu.make_async_copy(whole, whole, rs_j.at[e, 0]).wait()
        for n, (hh, d) in enumerate(((0, yr), (1, yl), (1, yr), (0, yl))):
            rdma(*j_ring(e, hh, y, n, d)).start()

    def j_forward(e):
        rdma(*j_ring(e, 0, ynl, 0, yr)).wait_recv()
        rdma(*j_ring(e, 0, ynl, 4, yr)).start()
        rdma(*j_ring(e, 1, ynr, 1, yl)).wait_recv()
        rdma(*j_ring(e, 1, ynr, 5, yl)).start()

    def j_finish(e):
        for hh, k, n, d in ((1, ynl, 2, yr), (0, ynr, 3, yl), (0, yfar, 4, yr), (1, yfar, 5, yl)):
            rdma(*j_ring(e, hh, k, n, d)).wait_recv()

        @pl.loop(0, jr.shape[1] * RING)
        def _(n):
            jt[e, n] = jr[e, lax.div(n, RING), lax.rem(n, RING)].T

    both(j_start)

    for g in (0, 1):
        reducer = reduces(g)

        @pl.when(reducer)
        def _():
            total = zb[g, z_piece(g, z)]
            seven = rz.at[g, 0 : DEPTH - 1]
            rdma(seven, seven, ss_z.at[g, 0], rs_z.at[g], sibling).wait_recv()
            for k in range(1, DEPTH):
                total += rz[g, lax.rem(z + k, DEPTH)]
            zr[g] = total
            zf[g, z_piece(g, z)] = total

        for k in spread:
            send_if(
                reducer, zr.at[g], zf.at[g, z_piece(g, z)], ss_g.at[g, k], rs_g.at[g], on_z(k)
            )

    both(j_forward)

    def home(q, i):
        return xf.at[q, lines[q % 2][0], part_rows(i, part)]

    for g in (0, 1):
        for some, ref in ((reduces(g), zf.at[g, 0 : (count - 1) * share]), (~reduces(g), zf.at[g])):

            @pl.when(some)
            def _():
                rdma(ref, ref, ss_g.at[g, 0], rs_g.at[g], sibling).wait_recv()

        for p in (0, 1):
            q = 2 * g + p
            i, on = lines[1 - p]
            mine = zf.at[g, p * part : (p + 1) * part]
            for k in (2, 1, 3):
                send(mine, home(q, i), ss_a2.at[q, k], rs_a2.at[q], on(k))
            home(q, i)[...] = mine[...]

    class Gather:
        def __init__(self, q):
            self.q = q
            self.i, self.on = lines[q % 2]
            self.nr, self.far, self.nl = (lax.rem(self.i + k, RING) for k in (1, 2, 3))
            self.right, self.left = self.on(1), self.on(3)

        def msg(self, n, h, k, dev):
            ref = xf.at[self.q, k, h * pad : (h + 1) * pad]
            return ref, ref, ss_a1.at[self.q, n], rs_a1.at[self.q, n], dev

        def start(self):
            q = self.q
            three = xf.at[q, 0, 0 : (RING - 1) * part]
            rdma(three, three, ss_a2.at[q, 0], rs_a2.at[q], sibling).wait_recv()
            send(*self.msg(0, 0, self.i, self.right))
            send(*self.msg(1, 1, self.i, self.left))
            send(*self.msg(2, 1, self.i, self.right))
            send(*self.msg(3, 0, self.i, self.left))

        def forward(self):
            rdma(*self.msg(0, 0, self.nl, self.right)).wait_recv()
            send(*self.msg(4, 0, self.nl, self.right))
            rdma(*self.msg(1, 1, self.nr, self.left)).wait_recv()
            send(*self.msg(5, 1, self.nr, self.left))

    ring = [Gather(q) for q in range(RING)]
    for q in range(RING):
        ring[q].start()
    ring[0].forward()
    ring[1].forward()

    reach = sv[...] * width
    row = lax.broadcasted_iota(jnp.int32, (2 * pad, trades), 0)
    row = row - jnp.where(row >= pad, pad - jrows, 0) + c * half

    acc[...] = jnp.zeros(acc.shape, F32)
    acce[...] = jnp.zeros(acce.shape, F32)

    def block(q, k):
        values = xf[q, k]
        hi = values.astype(BF16)
        lo = (values - hi.astype(F32)).astype(BF16)
        vega = jnp.dot(jnp.concatenate([hi, lo, hi], axis=1), wide, preferred_element_type=F32)
        keep = row < reach - (8 * q + 2 * k) * jrows
        masked = jnp.where(keep, vega, 0.0).astype(BF16)
        mk[...] = masked
        n = RING * q + k
        prod = jnp.dot(jt[0, n], masked, preferred_element_type=F32)
        for s in (0, 1):
            acc[s] += prod[:, s * trades // 2 : (s + 1) * trades // 2]

        @pl.when(has_extra)
        def _():
            mine = mk[:, pl.ds(pl.multiple_of(x * LANE, LANE), LANE)]
            acce[...] += jnp.dot(jt[1, n], mine, preferred_element_type=F32)

    def landed(q, k, h, n):
        ref = xf.at[q, k, h * pad : (h + 1) * pad]
        rdma(ref, ref, ss_a1.at[q, n], rs_a1.at[q, n], sibling).wait_recv()

    def ring_place(q, step):
        return lax.rem(jnp.where(lax.rem(q, 2) == 0, x, y) + step, RING)

    both(j_finish)

    @pl.loop(0, 2)
    def _(q):
        block(q, ring_place(q, 0))

    ring[2].forward()
    ring[3].forward()

    @pl.loop(2, RING)
    def _(q):
        block(q, ring_place(q, 0))

    @pl.loop(0, 2 * RING)
    def _(n):
        q = lax.div(n, 2)
        k = ring_place(q, 3 - 2 * lax.rem(n, 2))

        @pl.when(lax.rem(n, 2) == 0)
        def _():
            landed(q, k, 1, 2)

        @pl.when(lax.rem(n, 2) == 1)
        def _():
            landed(q, k, 0, 3)

        block(q, k)

    @pl.loop(0, RING)
    def _(q):
        k = ring_place(q, 2)
        landed(q, k, 0, 4)
        landed(q, k, 1, 5)
        block(q, k)

    swap = (acc.at[sib], pr, ss_p.at[0], rs_p.at[0], sibling)
    send(*swap)
    closer = lax.rem(z, 2)
    swap_extra = (acce, pre, ss_p.at[1], rs_p.at[1], sibling)
    send_if(has_extra & (c != closer), *swap_extra)

    strip_rows = out.shape[0]
    rdma(*swap).wait_recv()
    po[0] = (acc[c] + pr[...]).T.reshape(CHIPS, strip_rows, LANE)

    def deliver(e, n, tile, dst):
        @pl.when(dst != me)
        def _():
            rdma(
                po.at[e, n], ob.at[tile], ss_o.at[e], rs_o.at[0], {"grp": y, "path": dst}
            ).start()

        @pl.when(dst == me)
        def _():
            pltpu.make_async_copy(po.at[e, n], ob.at[tile], rs_o.at[0]).start()

    for k in (4, 3, 5, 2, 6, 1, 7, 0):
        zz = lax.rem(z + k, DEPTH)
        for side in (0, 1):
            for u in (0, 1):
                n = side * 2 * DEPTH + 2 * zz + u
                deliver(0, n, z * RING + x, c * CHIPS + n)

    closing = has_extra & (c == closer)

    @pl.when(closing)
    def _():
        rdma(*swap_extra).wait_recv()
        po[1, 0 : CHIPS // 2] = (acce[...] + pre[...]).T.reshape(CHIPS // 2, strip_rows, LANE)

        @pl.loop(0, CHIPS // 2)
        def _(k):
            n = lax.rem(2 * z + DEPTH + k, CHIPS // 2)
            deliver(1, n, CHIPS + z, x * (CHIPS // 2) + n)

    for cond, d in sent:
        if cond is None:
            d.wait_send()
        else:
            pl.when(cond)(d.wait_send)

    def j_sent(e):
        for n, hh in enumerate((0, 1, 1, 0, 0, 1)):
            rdma(*j_ring(e, hh, y, n, yr)).wait_send()

    both(j_sent)

    def j_crossed(e):
        for k in (1, 2, 3):
            rdma(*j_cross(e, k)).wait_send()

        @pl.when(core != c)
        def _():
            rdma(*j_cross(e, 0)).wait_send()

    both(j_crossed)

    @pl.when(turn)
    def _():
        for k in range(1, DEPTH):
            rdma(*j_line(k)).wait_send()

    pltpu.make_async_copy(ob, ob, rs_o.at[0]).wait()

    for t in range(tiles - 1):
        out[:, t * LANE : (t + 1) * LANE] = ob[t]
    out[:, (tiles - 1) * LANE : params] = ob[tiles - 1, :, 0:tail]

    def po_sent(e, n):
        rdma(po.at[e, 0:n], po.at[e, 0:n], ss_o.at[e], rs_o.at[0], sibling).wait_send()

    pl.when(core == c)(lambda: po_sent(0, CHIPS - 1))
    pl.when(core != c)(lambda: po_sent(0, CHIPS))
    pl.when(closing)(lambda: po_sent(1, CHIPS // 2 - 1))


def per_device(
    path_sens, discounts, cash_flows, flow_index, exercise_step, trade_steps, jacobian_inv
):
    paths_own, params = path_sens.shape
    trades = cash_flows.shape[0]
    jrows = jacobian_inv.shape[0]
    strip = trades // PATHS
    tiles = -(-params // LANE)
    pad = -(-jrows // 16) * 16
    half = params // 2
    slots = cash_flows.shape[1]
    part = pad // 2
    share = 16
    vm = pltpu.VMEM
    dma = pltpu.SemaphoreType.DMA
    scratch = [
        vm((paths_own, LANE), BF16),
        vm((slots, trades), F32),
        vm((slots, trades), jnp.int32),
        vm((1, trades), jnp.int32),
        vm((1, trades), jnp.int32),
        vm((half, paths_own), BF16),
        vm((half, paths_own), BF16),
        vm((paths_own, LANE), BF16),
        vm((half + 8, LANE), F32),
        vm((RING, RING, 2 * pad, LANE), F32),
        vm((RING, 6, pad, LANE), F32),
        vm((RING, 2 * pad, LANE), F32),
        vm((RING, RING, part, LANE), F32),
        vm((2, 2 * part, LANE), F32),
        vm((2, DEPTH, share, LANE), F32),
        vm((2, share, LANE), F32),
        vm((2, 2 * part, LANE), F32),
        vm((RING, RING, 2 * pad, LANE), F32),
        vm((jrows, params), BF16),
        vm((DEPTH, RING + 1, pad, LANE), BF16),
        vm((2, RING + 1, pad, LANE), BF16),
        vm((2, RING, RING, 2 * pad, LANE), BF16),
        vm((2, RING * RING, LANE, 2 * pad), BF16),
        vm((2 * pad, trades), BF16),
        vm((2, LANE, trades // 2), F32),
        vm((LANE, LANE), F32),
        vm((LANE, trades // 2), F32),
        vm((LANE, LANE), F32),
        vm((2, CHIPS, strip, LANE), F32),
        vm((tiles, strip, LANE), F32),
        dma((RING + 1,)), dma((RING + 1,)), dma((7,)),
        dma((RING, 6)), dma((RING, 6)),
        dma((RING, RING)), dma((RING,)),
        dma((2, DEPTH)), dma((2,)),
        dma((2, DEPTH)), dma((2,)),
        dma((RING, RING)), dma((RING,)),
        dma((RING, 6)), dma((RING, 6)),
        dma((DEPTH,)), dma((2, RING)), dma((3, 2)),
        dma((2, 6)), dma((2, 6)),
        dma((2,)), dma((2,)),
        dma((2,)), dma((1,)),
        pltpu.SemaphoreType.REGULAR((3, 2)),
    ]
    vmem = pl.BlockSpec(memory_space=pltpu.VMEM)
    hbm = pl.BlockSpec(memory_space=pl.ANY)
    return pl.pallas_call(
        kernel,
        out_shape=jax.ShapeDtypeStruct((strip, params), F32),
        in_specs=[hbm] * 7,
        out_specs=vmem,
        scratch_shapes=scratch,
        compiler_params=pltpu.CompilerParams(
            collective_id=0, has_side_effects=True, vmem_limit_bytes=56 * 1024 * 1024
        ),
    )(
        discounts,
        path_sens.T,
        cash_flows.T,
        flow_index.T,
        exercise_step.reshape(1, trades),
        trade_steps.reshape(1, trades),
        jacobian_inv,
    )


def solution(mesh):
    placed = (
        P(("grp", "path"), None),
        P(("grp", "path"), None),
        P("grp", None),
        P("grp", None),
        P("grp"),
        P("grp"),
        P("path", None),
    )
    return jax.shard_map(
        per_device, mesh=mesh, in_specs=placed, out_specs=P(("grp", "path"), None), check_vma=False
    )
```

```python
import jax
import jax.numpy as jnp
from jax import lax
from jax.experimental import pallas as pl
from jax.experimental.pallas import tpu as pltpu
from jax.sharding import PartitionSpec as P

NB = 40
LANE = 128
RING = 4
DEPTH = 8
CHIPS = RING * DEPTH
PATHS = 2 * CHIPS
EXTRA = 6
F32 = jnp.float32
BF16 = jnp.bfloat16
MESH = pl.DeviceIdType.MESH


def kernel(
    disc, sens, cash, index, exer, steps, jac, out,
    dv, cv, iv, ev, sv, s_own, s_in, d_in, xs, xp, r1, y2, r2, zb, rz, zr, zf, xf,
    jv, jp, jz, jr, wt, room, mk, acc, acce, pr, pre, po, ob,
    ss_s, rs_s, ls, ss_1, rs_1, ss_2, rs_2, ss_z, rs_z, ss_g, rs_g,
    ss_a2, rs_a2, ss_a1, rs_a1, ss_j, ss_jx, rs_j, ss_ja, rs_ja, ss_p, rs_p, ss_o, rs_o, near_z,
):
    y = lax.axis_index("grp")
    me = lax.axis_index("path")
    j = lax.div(me, 2)
    c = lax.rem(me, 2)
    x = lax.div(j, DEPTH)
    z = lax.rem(j, DEPTH)
    sib = 1 - c
    params = sens.shape[0]
    width = params // NB
    half = params // 2
    jrows = jac.shape[0]
    pad = xp.shape[2] // 2
    trades = cash.shape[1]

    def at_chip(xx, zz, cc):
        return {"grp": y, "path": (xx * DEPTH + zz) * 2 + cc}

    def rdma(src, dst, ss, rs, dev):
        return pltpu.make_async_remote_copy(
            src_ref=src, dst_ref=dst, send_sem=ss, recv_sem=rs, device_id=dev, device_id_type=MESH
        )

    sent = []

    def send(*args):
        d = rdma(*args)
        d.start()
        sent.append((None, d))

    def send_if(cond, *args):
        d = rdma(*args)

        @pl.when(cond)
        def _():
            d.start()

        sent.append((cond, d))

    sibling = at_chip(x, z, sib)

    def on_x(k):
        return at_chip(lax.rem(x + k, RING), z, c)

    def on_y(k):
        return {"grp": lax.rem(y + k, RING), "path": me}

    def on_z(k):
        return at_chip(x, lax.rem(z + k, DEPTH), c)

    lines = ((x, on_x), (y, on_y))

    barrier = pltpu.get_barrier_semaphore()
    partners = [sibling] + [on(k) for on in (on_x, on_y) for k in (1, RING - 1)]
    partners += [on_z(k) for k in (1, DEPTH - 1, 2, DEPTH - 2)]
    for d in partners:
        pl.semaphore_signal(barrier, inc=1, device_id=d, device_id_type=MESH)

    fetched = [
        pltpu.make_async_copy(src, dst, ls.at[n])
        for n, (src, dst) in enumerate(
            (
                (disc, dv),
                (sens.at[pl.ds(pl.multiple_of(c * half, 16), half)], s_own),
                (cash, cv), (index, iv), (exer, ev), (steps, sv), (jac, jv),
            )
        )
    ]
    for f in fetched:
        f.start()

    first_cut = (half // 4 // 16 + 1) * 16
    cuts = (0, first_cut, half // 2, half // 2 + first_cut, half)

    def s_copy(q):
        n = cuts[q + 1] - cuts[q]
        return (
            sens.at[pl.ds(pl.multiple_of(sib * half + cuts[q], 16), n)],
            s_in.at[pl.ds(cuts[q], n)], ss_s.at[q], rs_s.at[q], sibling,
        )

    d_copy = (disc, d_in, ss_s.at[RING], rs_s.at[RING], sibling)

    xs[half : half + 8] = jnp.zeros((8, LANE), F32)
    for f in fetched[:2]:
        f.wait()
    third = half // 3

    @pl.loop(0, 3)
    def _(n):
        rws = pl.ds(pl.multiple_of(n * third, 16), third)
        xs[rws] = jnp.dot(s_own[rws], dv[...], preferred_element_type=F32)

    pl.semaphore_wait(barrier, len(partners))
    send(*d_copy)
    for q in range(RING):
        send(*s_copy(q))
    for n, k in enumerate((2, DEPTH - 2)):
        pl.semaphore_signal(near_z.at[n], inc=1, device_id=on_z(k), device_id_type=MESH)

    tiles = out.shape[1] // LANE + 1
    tail = params - (tiles - 1) * LANE
    turn = lax.rem(z, RING) == y
    core = lax.div(x, 2)
    high = lax.div(z, RING)
    for f in fetched[2:]:
        f.wait()

    @pl.when(turn)
    def _():
        jp[...] = jnp.zeros(jp.shape, BF16)

        @pl.loop(0, DEPTH)
        def _(zz):
            for t in range(RING):
                col = pl.multiple_of((zz * RING + t) * LANE, LANE)
                jp[zz, t, 0:jrows] = jv[:, pl.ds(col, LANE)]

            @pl.when(zz < EXTRA - 1)
            def _():
                col = pl.multiple_of((CHIPS + zz) * LANE, LANE)
                jp[zz, RING, 0:jrows] = jv[:, pl.ds(col, LANE)]

        jp[EXTRA - 1, RING, 0:jrows, 0:tail] = jv[:, (tiles - 1) * LANE : params]
        pltpu.make_async_copy(jp.at[z], jz.at[high], rs_j.at[2, high]).start()

    def j_line(k):
        zz = lax.rem(z + k, DEPTH)
        return jp.at[zz], jz.at[high], ss_j.at[k], rs_j.at[2, high], on_z(k)

    def j_depth(*steps_):
        @pl.when(turn)
        def _():
            for k in steps_:
                rdma(*j_line(k)).start()

    j_depth(2, 6, 1, 7)

    def part_rows(n, size):
        return pl.ds(pl.multiple_of(n * size, 8), size)

    class Scatter:
        def __init__(self, q):
            self.q = q
            self.i, self.on = lines[q % 2]
            self.nr, self.far, self.nl = (lax.rem(self.i + k, RING) for k in (1, 2, 3))
            self.right, self.left = self.on(1), self.on(3)

        def msg(self, n, h, k, dev):
            q = self.q
            return (
                xp.at[q, k, h * pad : (h + 1) * pad], r1.at[q, n],
                ss_1.at[q, n], rs_1.at[q, n], dev,
            )

        def first(self):
            send(*self.msg(0, 0, self.far, self.right))
            send(*self.msg(2, 1, self.far, self.left))
            send(*self.msg(3, 1, self.nr, self.right))
            send(*self.msg(1, 0, self.nl, self.left))

        def second(self):
            for h, n, k, dev in ((0, 0, self.nr, self.right), (1, 2, self.nl, self.left)):
                rdma(*self.msg(n, h, k, dev)).wait_recv()
                xp[self.q, k, h * pad : (h + 1) * pad] += r1[self.q, n]
                send(*self.msg(4 + h, h, k, dev))

        def result(self):
            for h, n in ((0, 1), (1, 3)):
                rdma(*self.msg(n, h, self.i, self.left)).wait_recv()
                rdma(*self.msg(4 + h, h, self.i, self.left)).wait_recv()
                rws = slice(h * pad, (h + 1) * pad)
                y2[self.q, rws] = xp[self.q, self.i, rws] + r1[self.q, n] + r1[self.q, 4 + h]

    one = [Scatter(q) for q in range(RING)]
    rdma(*d_copy).wait_recv()
    for q in range(RING):
        rdma(*s_copy(q)).wait_recv()
        xs[cuts[q] : cuts[q + 1]] += jnp.dot(
            s_in[cuts[q] : cuts[q + 1]], d_in[...], preferred_element_type=F32
        )
        for k in range(RING):
            for u in (0, 1):
                top = (8 * q + 2 * k + u) * jrows
                xp[q, k, u * pad : (u + 1) * pad] = xs[top : top + pad]
        one[q].first()

    for n in (0, 1):
        pl.semaphore_wait(near_z.at[n], 1)
    j_depth(4, 3, 5)
    one[0].second()
    one[1].second()
    one[2].second()
    one[3].second()

    slots = cash.shape[0]
    forwards = lax.broadcasted_iota(jnp.int32, (LANE, trades), 0)
    late = forwards >= ev[...]
    weights = jnp.zeros((LANE, trades), F32)
    for s in range(slots):
        weights += jnp.where(late & (iv[s : s + 1] == forwards), cv[s : s + 1], 0.0)
    weights = weights * (1.0 / (disc.shape[0] * PATHS * RING))
    weights = weights.T
    w_hi = weights.astype(BF16)
    w_lo = (weights - w_hi.astype(F32)).astype(BF16)
    wt[...] = jnp.concatenate([w_hi, w_hi, w_lo], axis=1)
    reach = jnp.broadcast_to((sv[...] * width).astype(F32), (LANE, trades)).T.astype(jnp.int32)
    lane = lax.broadcasted_iota(jnp.int32, (trades, 2 * pad), 1)
    room[...] = (
        jnp.concatenate([reach, reach[:, : 2 * pad - LANE]], axis=1)
        - lane + jnp.where(lane >= pad, pad - jrows, 0) - c * half
    )

    part = y2.shape[1] // RING

    def two(q, k):
        i, on = lines[1 - q % 2]
        return (
            y2.at[q, part_rows(lax.rem(i + k, RING), part)], r2.at[q, i],
            ss_2.at[q, k], rs_2.at[q], on(k),
        )

    for g in (0, 1):
        for q in (2 * g, 2 * g + 1):
            one[q].result()
            for k in (2, 1, 3):
                send(*two(q, k))

    has_extra = z < EXTRA

    def j_cross(e, k):
        xx = lax.rem(x + k, RING)
        slot = xx if e == 0 else RING
        dst = jr.at[
            e, pl.ds(2 * lax.rem(x, 2), 2), y, pl.ds(pl.multiple_of(c * pad, 16), pad)
        ]
        return jz.at[:, slot], dst, ss_jx.at[e, k], rs_j.at[e, 0], at_chip(xx, z, core)

    def both(f):
        f(0)

        @pl.when(has_extra)
        def _():
            f(1)

    def j_send(e):
        for k in (2, 1, 3):
            rdma(*j_cross(e, k)).start()
        src, dst, ss, rs, dev = j_cross(e, 0)

        @pl.when(core == c)
        def _():
            pltpu.make_async_copy(src, dst, rs).start()

        @pl.when(core != c)
        def _():
            rdma(src, dst, ss, rs, dev).start()

    for n in (0, 1):
        pltpu.make_async_copy(jp.at[0], jz.at[n], rs_j.at[2, n]).wait()
    both(j_send)

    share = zr.shape[1]
    count = 2 * part // share
    spread = (4, 3, 5, 2, 6, 1, 7)

    def turn_of(g, d):
        return lax.rem(d + count * g, DEPTH)

    def reduces(g):
        return turn_of(g, z) < count

    def z_piece(g, d):
        return part_rows(jnp.minimum(turn_of(g, d), count - 1), share)

    for g in (0, 1):
        for p in (0, 1):
            q = 2 * g + p
            i, on = lines[1 - p]
            total = y2[q, part_rows(i, part)]
            three = r2.at[q, 0 : RING - 1]
            rdma(three, three, ss_2.at[q, 0], rs_2.at[q], sibling).wait_recv()
            for k in (1, 2, 3):
                total += r2[q, lax.rem(i + k, RING)]
            zb[g, p * part : (p + 1) * part] = total
        for k in spread:
            d = lax.rem(z + k, DEPTH)
            send_if(
                turn_of(g, d) < count,
                zb.at[g, z_piece(g, d)], rz.at[g, z], ss_z.at[g, k], rs_z.at[g], on_z(k),
            )


    def j_ring(e, half_, k, n, dev):
        ref = jr.at[e, pl.ds(2 * half_, 2), k]
        return ref, ref, ss_ja.at[e, n], rs_ja.at[e, n], dev

    yr, yl = on_y(1), on_y(3)
    ynr, yfar, ynl = (lax.rem(y + k, RING) for k in (1, 2, 3))

    def j_start(e):
        whole = jr.at[e, :, y]
        pltpu.make_async_copy(whole, whole, rs_j.at[e, 0]).wait()
        for n, (hh, d) in enumerate(((0, yr), (1, yl), (1, yr), (0, yl))):
            rdma(*j_ring(e, hh, y, n, d)).start()

    def j_forward(e):
        rdma(*j_ring(e, 0, ynl, 0, yr)).wait_recv()
        rdma(*j_ring(e, 0, ynl, 4, yr)).start()
        rdma(*j_ring(e, 1, ynr, 1, yl)).wait_recv()
        rdma(*j_ring(e, 1, ynr, 5, yl)).start()

    def j_finish(e):
        for hh, k, n, d in ((1, ynl, 2, yr), (0, ynr, 3, yl), (0, yfar, 4, yr), (1, yfar, 5, yl)):
            rdma(*j_ring(e, hh, k, n, d)).wait_recv()

    j_start(0)

    for g in (0, 1):
        reducer = reduces(g)

        @pl.when(reducer)
        def _():
            total = zb[g, z_piece(g, z)]
            seven = rz.at[g, 0 : DEPTH - 1]
            rdma(seven, seven, ss_z.at[g, 0], rs_z.at[g], sibling).wait_recv()
            for k in range(1, DEPTH):
                total += rz[g, lax.rem(z + k, DEPTH)]
            zr[g] = total
            zf[g, z_piece(g, z)] = total

        for k in spread:
            send_if(
                reducer, zr.at[g], zf.at[g, z_piece(g, z)], ss_g.at[g, k], rs_g.at[g], on_z(k)
            )

    j_forward(0)
    pl.when(has_extra)(lambda: j_start(1))

    def home(q, i):
        return xf.at[q, lines[q % 2][0], part_rows(i, part)]

    for g in (0, 1):
        for some, ref in ((reduces(g), zf.at[g, 0 : (count - 1) * share]), (~reduces(g), zf.at[g])):

            @pl.when(some)
            def _():
                rdma(ref, ref, ss_g.at[g, 0], rs_g.at[g], sibling).wait_recv()

        for p in (0, 1):
            q = 2 * g + p
            i, on = lines[1 - p]
            mine = zf.at[g, p * part : (p + 1) * part]
            for k in (2, 1, 3):
                send(mine, home(q, i), ss_a2.at[q, k], rs_a2.at[q], on(k))
            home(q, i)[...] = mine[...]

    pl.when(has_extra)(lambda: j_forward(1))

    class Gather:
        def __init__(self, q):
            self.q = q
            self.i, self.on = lines[q % 2]
            self.nr, self.far, self.nl = (lax.rem(self.i + k, RING) for k in (1, 2, 3))
            self.right, self.left = self.on(1), self.on(3)

        def msg(self, n, h, k, dev):
            ref = xf.at[self.q, k, h * pad : (h + 1) * pad]
            return ref, ref, ss_a1.at[self.q, n], rs_a1.at[self.q, n], dev

        def start(self):
            q = self.q
            three = xf.at[q, 0, 0 : (RING - 1) * part]
            rdma(three, three, ss_a2.at[q, 0], rs_a2.at[q], sibling).wait_recv()
            send(*self.msg(0, 0, self.i, self.right))
            send(*self.msg(1, 1, self.i, self.left))
            send(*self.msg(2, 1, self.i, self.right))
            send(*self.msg(3, 0, self.i, self.left))

        def forward(self):
            rdma(*self.msg(0, 0, self.nl, self.right)).wait_recv()
            send(*self.msg(4, 0, self.nl, self.right))
            rdma(*self.msg(1, 1, self.nr, self.left)).wait_recv()
            send(*self.msg(5, 1, self.nr, self.left))

    ring = [Gather(q) for q in range(RING)]
    for q in range(RING):
        ring[q].start()
    ring[0].forward()
    ring[1].forward()

    acc[...] = jnp.zeros(acc.shape, F32)

    def block(q, k):
        values = xf[q, k]
        hi = values.astype(BF16)
        lo = (values - hi.astype(F32)).astype(BF16)
        vega = lax.dot_general(
            wt[...], jnp.concatenate([hi, lo, hi], axis=1), (((1,), (1,)), ((), ())),
            preferred_element_type=F32,
        )
        masked = jnp.where(room[...] > (8 * q + 2 * k) * jrows, vega, 0.0).astype(BF16)
        mk[RING * q + k] = masked
        acc[...] += jnp.dot(masked, jr[0, q, k], preferred_element_type=F32)

    def landed(q, k, h, n):
        ref = xf.at[q, k, h * pad : (h + 1) * pad]
        rdma(ref, ref, ss_a1.at[q, n], rs_a1.at[q, n], sibling).wait_recv()

    def ring_place(q, step):
        return lax.rem(jnp.where(lax.rem(q, 2) == 0, x, y) + step, RING)

    j_finish(0)

    @pl.loop(0, 2)
    def _(q):
        block(q, ring_place(q, 0))

    ring[2].forward()
    ring[3].forward()

    @pl.loop(2, RING)
    def _(q):
        block(q, ring_place(q, 0))

    @pl.loop(0, 2 * RING)
    def _(n):
        q = lax.div(n, 2)
        k = ring_place(q, 3 - 2 * lax.rem(n, 2))

        @pl.when(lax.rem(n, 2) == 0)
        def _():
            landed(q, k, 1, 2)

        @pl.when(lax.rem(n, 2) == 1)
        def _():
            landed(q, k, 0, 3)

        block(q, k)

    @pl.loop(0, RING)
    def _(q):
        k = ring_place(q, 2)
        landed(q, k, 0, 4)
        landed(q, k, 1, 5)
        block(q, k)

    rows_c = pl.ds(pl.multiple_of(c * (trades // 2), 8), trades // 2)
    rows_sib = pl.ds(pl.multiple_of(sib * (trades // 2), 8), trades // 2)
    swap = (acc.at[rows_sib], pr, ss_p.at[0], rs_p.at[0], sibling)
    send(*swap)
    swap_extra = (acce.at[:, sib], pre, ss_p.at[1], rs_p.at[1], sibling)

    @pl.when(has_extra)
    def _():
        j_finish(1)
        mine = pl.ds(pl.multiple_of(x * LANE, LANE), LANE)
        total = jnp.zeros((LANE, LANE), F32)
        for n in range(RING * RING):
            total += jnp.dot(mk[n, mine], jr[1, n // RING, n % RING], preferred_element_type=F32)
        acce[...] = total.reshape(acce.shape)
        rdma(*swap_extra).start()

    strip_rows = out.shape[0]
    rdma(*swap).wait_recv()
    po[0] = (acc[rows_c] + pr[...]).reshape(CHIPS, strip_rows, LANE)

    def deliver(e, n, tile, dst):
        @pl.when(dst != me)
        def _():
            rdma(
                po.at[e, n], ob.at[tile], ss_o.at[e], rs_o.at[0], {"grp": y, "path": dst}
            ).start()

        @pl.when(dst == me)
        def _():
            pltpu.make_async_copy(po.at[e, n], ob.at[tile], rs_o.at[0]).start()

    for k in (4, 3, 5, 2, 6, 1, 7, 0):
        zz = lax.rem(z + k, DEPTH)
        for side in (0, 1):
            for u in (0, 1):
                n = side * 2 * DEPTH + 2 * zz + u
                deliver(0, n, z * RING + x, c * CHIPS + n)

    @pl.when(has_extra)
    def _():
        rdma(*swap_extra).wait_recv()
        po[1, 0:DEPTH] = acce[:, c] + pre[...]
        for k in (4, 3, 5, 2, 6, 1, 7, 0):
            zz = lax.rem(z + k, DEPTH)
            deliver(1, zz, CHIPS + z, (x * DEPTH + zz) * 2 + c)

    for cond, d in sent:
        if cond is None:
            d.wait_send()
        else:
            pl.when(cond)(d.wait_send)

    def j_sent(e):
        for n, hh in enumerate((0, 1, 1, 0, 0, 1)):
            rdma(*j_ring(e, hh, y, n, yr)).wait_send()

    both(j_sent)

    def j_crossed(e):
        for k in (1, 2, 3):
            rdma(*j_cross(e, k)).wait_send()

        @pl.when(core != c)
        def _():
            rdma(*j_cross(e, 0)).wait_send()

    both(j_crossed)

    @pl.when(has_extra)
    def _():
        rdma(*swap_extra).wait_send()

    @pl.when(turn)
    def _():
        for k in range(1, DEPTH):
            rdma(*j_line(k)).wait_send()

    pltpu.make_async_copy(ob, ob, rs_o.at[0]).wait()

    for t in range(tiles - 1):
        out[:, t * LANE : (t + 1) * LANE] = ob[t]
    out[:, (tiles - 1) * LANE : params] = ob[tiles - 1, :, 0:tail]

    def po_sent(e, n):
        rdma(po.at[e, 0:n], po.at[e, 0:n], ss_o.at[e], rs_o.at[0], sibling).wait_send()

    pl.when(core == c)(lambda: po_sent(0, CHIPS - 1))
    pl.when(core != c)(lambda: po_sent(0, CHIPS))
    pl.when(has_extra)(lambda: po_sent(1, DEPTH - 1))


def per_device(
    path_sens, discounts, cash_flows, flow_index, exercise_step, trade_steps, jacobian_inv
):
    paths_own, params = path_sens.shape
    trades = cash_flows.shape[0]
    jrows = jacobian_inv.shape[0]
    strip = trades // PATHS
    tiles = -(-params // LANE)
    pad = -(-jrows // 16) * 16
    half = params // 2
    slots = cash_flows.shape[1]
    part = pad // 2
    share = 16
    vm = pltpu.VMEM
    dma = pltpu.SemaphoreType.DMA
    scratch = [
        vm((paths_own, LANE), BF16),
        vm((slots, trades), F32),
        vm((slots, trades), jnp.int32),
        vm((1, trades), jnp.int32),
        vm((1, trades), jnp.int32),
        vm((half, paths_own), BF16),
        vm((half, paths_own), BF16),
        vm((paths_own, LANE), BF16),
        vm((half + 8, LANE), F32),
        vm((RING, RING, 2 * pad, LANE), F32),
        vm((RING, 6, pad, LANE), F32),
        vm((RING, 2 * pad, LANE), F32),
        vm((RING, RING, part, LANE), F32),
        vm((2, 2 * part, LANE), F32),
        vm((2, DEPTH, share, LANE), F32),
        vm((2, share, LANE), F32),
        vm((2, 2 * part, LANE), F32),
        vm((RING, RING, 2 * pad, LANE), F32),
        vm((jrows, params), BF16),
        vm((DEPTH, RING + 1, pad, LANE), BF16),
        vm((2, RING + 1, pad, LANE), BF16),
        vm((2, RING, RING, 2 * pad, LANE), BF16),
        vm((trades, 3 * LANE), BF16),
        vm((trades, 2 * pad), jnp.int32),
        vm((RING * RING, trades, 2 * pad), BF16),
        vm((trades, LANE), F32),
        vm((DEPTH, 2, strip, LANE), F32),
        vm((trades // 2, LANE), F32),
        vm((DEPTH, strip, LANE), F32),
        vm((2, CHIPS, strip, LANE), F32),
        vm((tiles, strip, LANE), F32),
        dma((RING + 1,)), dma((RING + 1,)), dma((7,)),
        dma((RING, 6)), dma((RING, 6)),
        dma((RING, RING)), dma((RING,)),
        dma((2, DEPTH)), dma((2,)),
        dma((2, DEPTH)), dma((2,)),
        dma((RING, RING)), dma((RING,)),
        dma((RING, 6)), dma((RING, 6)),
        dma((DEPTH,)), dma((2, RING)), dma((3, 2)),
        dma((2, 6)), dma((2, 6)),
        dma((2,)), dma((2,)),
        dma((2,)), dma((1,)),
        pltpu.SemaphoreType.REGULAR((2,)),
    ]
    vmem = pl.BlockSpec(memory_space=pltpu.VMEM)
    hbm = pl.BlockSpec(memory_space=pl.ANY)
    return pl.pallas_call(
        kernel,
        out_shape=jax.ShapeDtypeStruct((strip, params), F32),
        in_specs=[hbm] * 7,
        out_specs=vmem,
        scratch_shapes=scratch,
        compiler_params=pltpu.CompilerParams(
            collective_id=0, has_side_effects=True, vmem_limit_bytes=56 * 1024 * 1024
        ),
    )(
        discounts,
        path_sens.T,
        cash_flows.T,
        flow_index.T,
        exercise_step.reshape(1, trades),
        trade_steps.reshape(1, trades),
        jacobian_inv,
    )


def solution(mesh):
    placed = (
        P(("grp", "path"), None),
        P(("grp", "path"), None),
        P("grp", None),
        P("grp", None),
        P("grp"),
        P("grp"),
        P("path", None),
    )
    return jax.shard_map(
        per_device, mesh=mesh, in_specs=placed, out_specs=P(("grp", "path"), None), check_vma=False
    )
```

```python
import jax
import jax.numpy as jnp
from jax import lax
from jax.experimental import pallas as pl
from jax.experimental.pallas import tpu as pltpu
from jax.sharding import PartitionSpec as P

NB = 40
LANE = 128
RING = 4
DEPTH = 8
CHIPS = RING * DEPTH
PATHS = 2 * CHIPS
EXTRA = 6
F32 = jnp.float32
BF16 = jnp.bfloat16
MESH = pl.DeviceIdType.MESH


def kernel(
    disc, sens, cash, index, exer, steps, jac, out,
    dv, cv, iv, ev, sv, s_own, s_in, d_in, xs, xp, r1, y2, r2, zb, rz, zr, zf, xf,
    jv, jp, jz, jr, wt, room, mk, acc, acce, pr, pre, po, ob,
    ss_s, rs_s, ls, ss_1, rs_1, ss_2, rs_2, ss_z, rs_z, ss_g, rs_g,
    ss_a2, rs_a2, ss_a1, rs_a1, ss_j, ss_jx, rs_j, ss_ja, rs_ja, ss_p, rs_p, ss_o, rs_o, near_z,
):
    y = lax.axis_index("grp")
    me = lax.axis_index("path")
    j = lax.div(me, 2)
    c = lax.rem(me, 2)
    x = lax.div(j, DEPTH)
    z = lax.rem(j, DEPTH)
    sib = 1 - c
    params = sens.shape[0]
    width = params // NB
    half = params // 2
    jrows = jac.shape[0]
    pad = xp.shape[2] // 2
    trades = cash.shape[1]

    def at_chip(xx, zz, cc):
        return {"grp": y, "path": (xx * DEPTH + zz) * 2 + cc}

    def rdma(src, dst, ss, rs, dev):
        return pltpu.make_async_remote_copy(
            src_ref=src, dst_ref=dst, send_sem=ss, recv_sem=rs, device_id=dev, device_id_type=MESH
        )

    sent = []

    def send(*args):
        d = rdma(*args)
        d.start()
        sent.append((None, d))

    def send_if(cond, *args):
        d = rdma(*args)

        @pl.when(cond)
        def _():
            d.start()

        sent.append((cond, d))

    sibling = at_chip(x, z, sib)

    def on_x(k):
        return at_chip(lax.rem(x + k, RING), z, c)

    def on_y(k):
        return {"grp": lax.rem(y + k, RING), "path": me}

    def on_z(k):
        return at_chip(x, lax.rem(z + k, DEPTH), c)

    lines = ((x, on_x), (y, on_y))

    barrier = pltpu.get_barrier_semaphore()
    partners = [sibling] + [on(k) for on in (on_x, on_y) for k in (1, RING - 1)]
    partners += [on_z(k) for k in (1, DEPTH - 1, 2, DEPTH - 2)]
    for d in partners:
        pl.semaphore_signal(barrier, inc=1, device_id=d, device_id_type=MESH)

    fetched = [
        pltpu.make_async_copy(src, dst, ls.at[n])
        for n, (src, dst) in enumerate(
            (
                (disc, dv),
                (sens.at[pl.ds(pl.multiple_of(c * half, 16), half)], s_own),
                (cash, cv), (index, iv), (exer, ev), (steps, sv), (jac, jv),
            )
        )
    ]
    for f in fetched:
        f.start()

    first_cut = (half // 4 // 16 + 1) * 16
    cuts = (0, first_cut, half // 2, half // 2 + first_cut, half)

    def s_copy(q):
        n = cuts[q + 1] - cuts[q]
        return (
            sens.at[pl.ds(pl.multiple_of(sib * half + cuts[q], 16), n)],
            s_in.at[pl.ds(cuts[q], n)], ss_s.at[q], rs_s.at[q], sibling,
        )

    d_copy = (disc, d_in, ss_s.at[RING], rs_s.at[RING], sibling)

    xs[half : half + 8] = jnp.zeros((8, LANE), F32)
    for f in fetched[:2]:
        f.wait()
    third = half // 3

    @pl.loop(0, 3)
    def _(n):
        rws = pl.ds(pl.multiple_of(n * third, 16), third)
        xs[rws] = jnp.dot(s_own[rws], dv[...], preferred_element_type=F32)

    pl.semaphore_wait(barrier, len(partners))
    send(*d_copy)
    for q in range(RING):
        send(*s_copy(q))
    for n, k in enumerate((2, DEPTH - 2)):
        pl.semaphore_signal(near_z.at[n], inc=1, device_id=on_z(k), device_id_type=MESH)

    tiles = out.shape[1] // LANE + 1
    tail = params - (tiles - 1) * LANE
    turn = lax.rem(z, RING) == y
    core = lax.div(x, 2)
    high = lax.div(z, RING)
    for f in fetched[2:]:
        f.wait()

    @pl.when(turn)
    def _():
        jp[...] = jnp.zeros(jp.shape, BF16)

        @pl.loop(0, DEPTH)
        def _(zz):
            for t in range(RING):
                col = pl.multiple_of((zz * RING + t) * LANE, LANE)
                jp[zz, t, 0:jrows] = jv[:, pl.ds(col, LANE)]

            @pl.when(zz < EXTRA - 1)
            def _():
                col = pl.multiple_of((CHIPS + zz) * LANE, LANE)
                jp[zz, RING, 0:jrows] = jv[:, pl.ds(col, LANE)]

        jp[EXTRA - 1, RING, 0:jrows, 0:tail] = jv[:, (tiles - 1) * LANE : params]
        pltpu.make_async_copy(jp.at[z], jz.at[high], rs_j.at[2, high]).start()

    def j_line(k):
        zz = lax.rem(z + k, DEPTH)
        return jp.at[zz], jz.at[high], ss_j.at[k], rs_j.at[2, high], on_z(k)

    def j_depth(*steps_):
        @pl.when(turn)
        def _():
            for k in steps_:
                rdma(*j_line(k)).start()

    j_depth(2, 6, 1, 7)

    def part_rows(n, size):
        return pl.ds(pl.multiple_of(n * size, 8), size)

    class Scatter:
        def __init__(self, q):
            self.q = q
            self.i, self.on = lines[q % 2]
            self.nr, self.far, self.nl = (lax.rem(self.i + k, RING) for k in (1, 2, 3))
            self.right, self.left = self.on(1), self.on(3)

        def msg(self, n, h, k, dev):
            q = self.q
            return (
                xp.at[q, k, h * pad : (h + 1) * pad], r1.at[q, n],
                ss_1.at[q, n], rs_1.at[q, n], dev,
            )

        def first(self):
            send(*self.msg(0, 0, self.far, self.right))
            send(*self.msg(2, 1, self.far, self.left))
            send(*self.msg(3, 1, self.nr, self.right))
            send(*self.msg(1, 0, self.nl, self.left))

        def second(self):
            for h, n, k, dev in ((0, 0, self.nr, self.right), (1, 2, self.nl, self.left)):
                rdma(*self.msg(n, h, k, dev)).wait_recv()
                xp[self.q, k, h * pad : (h + 1) * pad] += r1[self.q, n]
                send(*self.msg(4 + h, h, k, dev))

        def result(self):
            for h, n in ((0, 1), (1, 3)):
                rdma(*self.msg(n, h, self.i, self.left)).wait_recv()
                rdma(*self.msg(4 + h, h, self.i, self.left)).wait_recv()
                rws = slice(h * pad, (h + 1) * pad)
                y2[self.q, rws] = xp[self.q, self.i, rws] + r1[self.q, n] + r1[self.q, 4 + h]

    one = [Scatter(q) for q in range(RING)]
    rdma(*d_copy).wait_recv()
    for q in range(RING):
        rdma(*s_copy(q)).wait_recv()
        xs[cuts[q] : cuts[q + 1]] += jnp.dot(
            s_in[cuts[q] : cuts[q + 1]], d_in[...], preferred_element_type=F32
        )
        for k in range(RING):
            for u in (0, 1):
                top = (8 * q + 2 * k + u) * jrows
                xp[q, k, u * pad : (u + 1) * pad] = xs[top : top + pad]
        one[q].first()

    for n in (0, 1):
        pl.semaphore_wait(near_z.at[n], 1)
    j_depth(4, 3, 5)
    one[0].second()
    one[1].second()
    one[2].second()
    one[3].second()

    has_extra = z < EXTRA

    def j_cross(e, k):
        xx = lax.rem(x + k, RING)
        slot = xx if e == 0 else RING
        dst = jr.at[
            e, pl.ds(2 * lax.rem(x, 2), 2), y, pl.ds(pl.multiple_of(c * pad, 16), pad)
        ]
        return jz.at[:, slot], dst, ss_jx.at[e, k], rs_j.at[e, 0], at_chip(xx, z, core)

    def both(f):
        f(0)

        @pl.when(has_extra)
        def _():
            f(1)

    def j_send(e):
        for k in (1, 3):
            rdma(*j_cross(e, k)).start()
        src, dst, ss, rs, dev = j_cross(e, 0)

        @pl.when(core == c)
        def _():
            pltpu.make_async_copy(src, dst, rs).start()

        @pl.when(core != c)
        def _():
            rdma(src, dst, ss, rs, dev).start()

    for n in (0, 1):
        pltpu.make_async_copy(jp.at[0], jz.at[n], rs_j.at[2, n]).wait()
    both(j_send)

    slots = cash.shape[0]
    forwards = lax.broadcasted_iota(jnp.int32, (LANE, trades), 0)
    late = forwards >= ev[...]
    weights = jnp.zeros((LANE, trades), F32)
    for s in range(slots):
        weights += jnp.where(late & (iv[s : s + 1] == forwards), cv[s : s + 1], 0.0)
    weights = weights * (1.0 / (disc.shape[0] * PATHS * RING))
    weights = weights.T
    w_hi = weights.astype(BF16)
    w_lo = (weights - w_hi.astype(F32)).astype(BF16)
    wt[...] = jnp.concatenate([w_hi, w_hi, w_lo], axis=1)
    reach = jnp.broadcast_to((sv[...] * width).astype(F32), (LANE, trades)).T.astype(jnp.int32)
    lane = lax.broadcasted_iota(jnp.int32, (trades, 2 * pad), 1)
    room[...] = (
        jnp.concatenate([reach, reach[:, : 2 * pad - LANE]], axis=1)
        - lane + jnp.where(lane >= pad, pad - jrows, 0) - c * half
    )

    part = y2.shape[1] // RING

    def two(q, k):
        i, on = lines[1 - q % 2]
        return (
            y2.at[q, part_rows(lax.rem(i + k, RING), part)], r2.at[q, i],
            ss_2.at[q, k], rs_2.at[q], on(k),
        )

    for g in (0, 1):
        for q in (2 * g, 2 * g + 1):
            one[q].result()
            for k in (2, 1, 3):
                send(*two(q, k))
    both(lambda e: rdma(*j_cross(e, 2)).start())

    share = zr.shape[1]
    count = 2 * part // share
    spread = (4, 3, 5, 2, 6, 1, 7)

    def turn_of(g, d):
        return lax.rem(d + count * g, DEPTH)

    def reduces(g):
        return turn_of(g, z) < count

    def z_piece(g, d):
        return part_rows(jnp.minimum(turn_of(g, d), count - 1), share)

    for g in (0, 1):
        for p in (0, 1):
            q = 2 * g + p
            i, on = lines[1 - p]
            total = y2[q, part_rows(i, part)]
            three = r2.at[q, 0 : RING - 1]
            rdma(three, three, ss_2.at[q, 0], rs_2.at[q], sibling).wait_recv()
            for k in (1, 2, 3):
                total += r2[q, lax.rem(i + k, RING)]
            zb[g, p * part : (p + 1) * part] = total
        for k in spread:
            d = lax.rem(z + k, DEPTH)
            send_if(
                turn_of(g, d) < count,
                zb.at[g, z_piece(g, d)], rz.at[g, z], ss_z.at[g, k], rs_z.at[g], on_z(k),
            )


    def j_ring(e, half_, k, n, dev):
        ref = jr.at[e, pl.ds(2 * half_, 2), k]
        return ref, ref, ss_ja.at[e, n], rs_ja.at[e, n], dev

    yr, yl = on_y(1), on_y(3)
    ynr, yfar, ynl = (lax.rem(y + k, RING) for k in (1, 2, 3))

    def j_start(e):
        whole = jr.at[e, :, y]
        pltpu.make_async_copy(whole, whole, rs_j.at[e, 0]).wait()
        for n, (hh, d) in enumerate(((0, yr), (1, yl), (1, yr), (0, yl))):
            rdma(*j_ring(e, hh, y, n, d)).start()

    def j_forward(e):
        rdma(*j_ring(e, 0, ynl, 0, yr)).wait_recv()
        rdma(*j_ring(e, 0, ynl, 4, yr)).start()
        rdma(*j_ring(e, 1, ynr, 1, yl)).wait_recv()
        rdma(*j_ring(e, 1, ynr, 5, yl)).start()

    def j_finish(e):
        for hh, k, n, d in ((1, ynl, 2, yr), (0, ynr, 3, yl), (0, yfar, 4, yr), (1, yfar, 5, yl)):
            rdma(*j_ring(e, hh, k, n, d)).wait_recv()

    j_start(0)

    for g in (0, 1):
        reducer = reduces(g)

        @pl.when(reducer)
        def _():
            total = zb[g, z_piece(g, z)]
            seven = rz.at[g, 0 : DEPTH - 1]
            rdma(seven, seven, ss_z.at[g, 0], rs_z.at[g], sibling).wait_recv()
            for k in range(1, DEPTH):
                total += rz[g, lax.rem(z + k, DEPTH)]
            zr[g] = total
            zf[g, z_piece(g, z)] = total

        for k in spread:
            send_if(
                reducer, zr.at[g], zf.at[g, z_piece(g, z)], ss_g.at[g, k], rs_g.at[g], on_z(k)
            )

    pl.when(has_extra)(lambda: j_start(1))
    j_forward(0)

    def home(q, i):
        return xf.at[q, lines[q % 2][0], part_rows(i, part)]

    for g in (0, 1):
        for some, ref in ((reduces(g), zf.at[g, 0 : (count - 1) * share]), (~reduces(g), zf.at[g])):

            @pl.when(some)
            def _():
                rdma(ref, ref, ss_g.at[g, 0], rs_g.at[g], sibling).wait_recv()

        for p in (0, 1):
            q = 2 * g + p
            i, on = lines[1 - p]
            mine = zf.at[g, p * part : (p + 1) * part]
            for k in (2, 1, 3):
                send(mine, home(q, i), ss_a2.at[q, k], rs_a2.at[q], on(k))
            home(q, i)[...] = mine[...]

    class Gather:
        def __init__(self, q):
            self.q = q
            self.i, self.on = lines[q % 2]
            self.nr, self.far, self.nl = (lax.rem(self.i + k, RING) for k in (1, 2, 3))
            self.right, self.left = self.on(1), self.on(3)

        def msg(self, n, h, k, dev):
            ref = xf.at[self.q, k, h * pad : (h + 1) * pad]
            return ref, ref, ss_a1.at[self.q, n], rs_a1.at[self.q, n], dev

        def start(self):
            q = self.q
            three = xf.at[q, 0, 0 : (RING - 1) * part]
            rdma(three, three, ss_a2.at[q, 0], rs_a2.at[q], sibling).wait_recv()
            send(*self.msg(0, 0, self.i, self.right))
            send(*self.msg(1, 1, self.i, self.left))
            send(*self.msg(2, 1, self.i, self.right))
            send(*self.msg(3, 0, self.i, self.left))

        def forward(self):
            rdma(*self.msg(0, 0, self.nl, self.right)).wait_recv()
            send(*self.msg(4, 0, self.nl, self.right))
            rdma(*self.msg(1, 1, self.nr, self.left)).wait_recv()
            send(*self.msg(5, 1, self.nr, self.left))

    ring = [Gather(q) for q in range(RING)]
    for q in range(RING):
        ring[q].start()
    pl.when(has_extra)(lambda: j_forward(1))
    ring[0].forward()
    ring[1].forward()

    acc[...] = jnp.zeros(acc.shape, F32)
    acce[...] = jnp.zeros(acce.shape, F32)

    def block(q, k):
        values = xf[q, k]
        hi = values.astype(BF16)
        lo = (values - hi.astype(F32)).astype(BF16)
        vega = lax.dot_general(
            wt[...], jnp.concatenate([hi, lo, hi], axis=1), (((1,), (1,)), ((), ())),
            preferred_element_type=F32,
        )
        masked = jnp.where(room[...] > (8 * q + 2 * k) * jrows, vega, 0.0).astype(BF16)
        mk[RING * q + k] = masked
        acc[...] += jnp.dot(masked, jr[0, q, k], preferred_element_type=F32)

    def landed(q, k, h, n):
        ref = xf.at[q, k, h * pad : (h + 1) * pad]
        rdma(ref, ref, ss_a1.at[q, n], rs_a1.at[q, n], sibling).wait_recv()

    def ring_place(q, step):
        return lax.rem(jnp.where(lax.rem(q, 2) == 0, x, y) + step, RING)

    j_finish(0)

    @pl.loop(0, 2)
    def _(q):
        block(q, ring_place(q, 0))

    ring[2].forward()
    ring[3].forward()

    @pl.loop(2, RING)
    def _(q):
        block(q, ring_place(q, 0))

    @pl.loop(0, 2 * RING)
    def _(n):
        q = lax.div(n, 2)
        k = ring_place(q, 3 - 2 * lax.rem(n, 2))

        @pl.when(lax.rem(n, 2) == 0)
        def _():
            landed(q, k, 1, 2)

        @pl.when(lax.rem(n, 2) == 1)
        def _():
            landed(q, k, 0, 3)

        block(q, k)

    pl.when(has_extra)(lambda: j_finish(1))

    @pl.loop(0, RING)
    def _(q):
        k = ring_place(q, 2)
        landed(q, k, 0, 4)
        landed(q, k, 1, 5)
        block(q, k)

        @pl.when(has_extra)
        def _():
            mine = pl.ds(pl.multiple_of(x * LANE, LANE), LANE)
            more = jnp.zeros((LANE, LANE), F32)
            for kk in range(RING):
                more += jnp.dot(
                    mk[RING * q + kk, mine], jr[1, q, kk], preferred_element_type=F32
                )
            acce[...] += more.reshape(acce.shape)

    rows_c = pl.ds(pl.multiple_of(c * (trades // 2), 8), trades // 2)
    rows_sib = pl.ds(pl.multiple_of(sib * (trades // 2), 8), trades // 2)
    swap = (acc.at[rows_sib], pr, ss_p.at[0], rs_p.at[0], sibling)
    send(*swap)
    swap_extra = (acce.at[:, sib], pre, ss_p.at[1], rs_p.at[1], sibling)

    @pl.when(has_extra)
    def _():
        rdma(*swap_extra).start()

    strip_rows = out.shape[0]
    rdma(*swap).wait_recv()
    po[0] = (acc[rows_c] + pr[...]).reshape(CHIPS, strip_rows, LANE)

    def deliver(e, n, tile, dst):
        @pl.when(dst != me)
        def _():
            rdma(
                po.at[e, n], ob.at[tile], ss_o.at[e], rs_o.at[0], {"grp": y, "path": dst}
            ).start()

        @pl.when(dst == me)
        def _():
            pltpu.make_async_copy(po.at[e, n], ob.at[tile], rs_o.at[0]).start()

    for k in (4, 3, 5, 2, 6, 1, 7, 0):
        zz = lax.rem(z + k, DEPTH)
        for side in (0, 1):
            for u in (0, 1):
                n = side * 2 * DEPTH + 2 * zz + u
                deliver(0, n, z * RING + x, c * CHIPS + n)

    @pl.when(has_extra)
    def _():
        rdma(*swap_extra).wait_recv()
        po[1, 0:DEPTH] = acce[:, c] + pre[...]
        for k in (4, 3, 5, 2, 6, 1, 7, 0):
            zz = lax.rem(z + k, DEPTH)
            deliver(1, zz, CHIPS + z, (x * DEPTH + zz) * 2 + c)

    for cond, d in sent:
        if cond is None:
            d.wait_send()
        else:
            pl.when(cond)(d.wait_send)

    def j_sent(e):
        for n, hh in enumerate((0, 1, 1, 0, 0, 1)):
            rdma(*j_ring(e, hh, y, n, yr)).wait_send()

    both(j_sent)

    def j_crossed(e):
        for k in (1, 2, 3):
            rdma(*j_cross(e, k)).wait_send()

        @pl.when(core != c)
        def _():
            rdma(*j_cross(e, 0)).wait_send()

    both(j_crossed)

    @pl.when(has_extra)
    def _():
        rdma(*swap_extra).wait_send()

    @pl.when(turn)
    def _():
        for k in range(1, DEPTH):
            rdma(*j_line(k)).wait_send()

    pltpu.make_async_copy(ob, ob, rs_o.at[0]).wait()

    for t in range(tiles - 1):
        out[:, t * LANE : (t + 1) * LANE] = ob[t]
    out[:, (tiles - 1) * LANE : params] = ob[tiles - 1, :, 0:tail]

    def po_sent(e, n):
        rdma(po.at[e, 0:n], po.at[e, 0:n], ss_o.at[e], rs_o.at[0], sibling).wait_send()

    pl.when(core == c)(lambda: po_sent(0, CHIPS - 1))
    pl.when(core != c)(lambda: po_sent(0, CHIPS))
    pl.when(has_extra)(lambda: po_sent(1, DEPTH - 1))


def per_device(
    path_sens, discounts, cash_flows, flow_index, exercise_step, trade_steps, jacobian_inv
):
    paths_own, params = path_sens.shape
    trades = cash_flows.shape[0]
    jrows = jacobian_inv.shape[0]
    strip = trades // PATHS
    tiles = -(-params // LANE)
    pad = -(-jrows // 16) * 16
    half = params // 2
    slots = cash_flows.shape[1]
    part = pad // 2
    share = 16
    vm = pltpu.VMEM
    dma = pltpu.SemaphoreType.DMA
    scratch = [
        vm((paths_own, LANE), BF16),
        vm((slots, trades), F32),
        vm((slots, trades), jnp.int32),
        vm((1, trades), jnp.int32),
        vm((1, trades), jnp.int32),
        vm((half, paths_own), BF16),
        vm((half, paths_own), BF16),
        vm((paths_own, LANE), BF16),
        vm((half + 8, LANE), F32),
        vm((RING, RING, 2 * pad, LANE), F32),
        vm((RING, 6, pad, LANE), F32),
        vm((RING, 2 * pad, LANE), F32),
        vm((RING, RING, part, LANE), F32),
        vm((2, 2 * part, LANE), F32),
        vm((2, DEPTH, share, LANE), F32),
        vm((2, share, LANE), F32),
        vm((2, 2 * part, LANE), F32),
        vm((RING, RING, 2 * pad, LANE), F32),
        vm((jrows, params), BF16),
        vm((DEPTH, RING + 1, pad, LANE), BF16),
        vm((2, RING + 1, pad, LANE), BF16),
        vm((2, RING, RING, 2 * pad, LANE), BF16),
        vm((trades, 3 * LANE), BF16),
        vm((trades, 2 * pad), jnp.int32),
        vm((RING * RING, trades, 2 * pad), BF16),
        vm((trades, LANE), F32),
        vm((DEPTH, 2, strip, LANE), F32),
        vm((trades // 2, LANE), F32),
        vm((DEPTH, strip, LANE), F32),
        vm((2, CHIPS, strip, LANE), F32),
        vm((tiles, strip, LANE), F32),
        dma((RING + 1,)), dma((RING + 1,)), dma((7,)),
        dma((RING, 6)), dma((RING, 6)),
        dma((RING, RING)), dma((RING,)),
        dma((2, DEPTH)), dma((2,)),
        dma((2, DEPTH)), dma((2,)),
        dma((RING, RING)), dma((RING,)),
        dma((RING, 6)), dma((RING, 6)),
        dma((DEPTH,)), dma((2, RING)), dma((3, 2)),
        dma((2, 6)), dma((2, 6)),
        dma((2,)), dma((2,)),
        dma((2,)), dma((1,)),
        pltpu.SemaphoreType.REGULAR((2,)),
    ]
    vmem = pl.BlockSpec(memory_space=pltpu.VMEM)
    hbm = pl.BlockSpec(memory_space=pl.ANY)
    return pl.pallas_call(
        kernel,
        out_shape=jax.ShapeDtypeStruct((strip, params), F32),
        in_specs=[hbm] * 7,
        out_specs=vmem,
        scratch_shapes=scratch,
        compiler_params=pltpu.CompilerParams(
            collective_id=0, has_side_effects=True, vmem_limit_bytes=56 * 1024 * 1024
        ),
    )(
        discounts,
        path_sens.T,
        cash_flows.T,
        flow_index.T,
        exercise_step.reshape(1, trades),
        trade_steps.reshape(1, trades),
        jacobian_inv,
    )


def solution(mesh):
    placed = (
        P(("grp", "path"), None),
        P(("grp", "path"), None),
        P("grp", None),
        P("grp", None),
        P("grp"),
        P("grp"),
        P("path", None),
    )
    return jax.shard_map(
        per_device, mesh=mesh, in_specs=placed, out_specs=P(("grp", "path"), None), check_vma=False
    )
```

```python
import jax
import jax.numpy as jnp
from jax import lax
from jax.experimental import pallas as pl
from jax.experimental.pallas import tpu as pltpu
from jax.sharding import PartitionSpec as P

NB = 40
LANE = 128
RING = 4
DEPTH = 8
CHIPS = RING * DEPTH
PATHS = 2 * CHIPS
GROUP = 16
F32 = jnp.float32
BF16 = jnp.bfloat16
MESH = pl.DeviceIdType.MESH


def kernel(
    disc, sens, cash, index, exer, steps, jac, out,
    dv, cv, iv, ev, sv, s_own, s_in, d_in, xs, xp, r1, y2, r2, zb, rz, zr, zf, xf,
    jv, je, jp, jz, jr, jx, jb, wt, room, acc, pr, po, ob,
    ss_s, rs_s, ls, ss_1, rs_1, ss_2, rs_2, ss_z, rs_z, ss_g, rs_g,
    ss_a2, rs_a2, ss_a1, rs_a1, ss_j, ss_jx, rs_j, ss_ja, rs_ja, ss_p, rs_p, ss_o, rs_o, near_z,
):
    y = lax.axis_index("grp")
    me = lax.axis_index("path")
    j = lax.div(me, 2)
    c = lax.rem(me, 2)
    x = lax.div(j, DEPTH)
    z = lax.rem(j, DEPTH)
    sib = 1 - c
    params = sens.shape[0]
    width = params // NB
    half = params // 2
    jrows = jac.shape[0]
    pad = xp.shape[2] // 2
    trades = cash.shape[1]

    def at_chip(xx, zz, cc):
        return {"grp": y, "path": (xx * DEPTH + zz) * 2 + cc}

    def rdma(src, dst, ss, rs, dev):
        return pltpu.make_async_remote_copy(
            src_ref=src, dst_ref=dst, send_sem=ss, recv_sem=rs, device_id=dev, device_id_type=MESH
        )

    sent = []

    def send(*args):
        d = rdma(*args)
        d.start()
        sent.append((None, d))

    def send_if(cond, *args):
        d = rdma(*args)

        @pl.when(cond)
        def _():
            d.start()

        sent.append((cond, d))

    sibling = at_chip(x, z, sib)

    def on_x(k):
        return at_chip(lax.rem(x + k, RING), z, c)

    def on_y(k):
        return {"grp": lax.rem(y + k, RING), "path": me}

    def on_z(k):
        return at_chip(x, lax.rem(z + k, DEPTH), c)

    lines = ((x, on_x), (y, on_y))

    barrier = pltpu.get_barrier_semaphore()
    partners = [sibling] + [on(k) for on in (on_x, on_y) for k in (1, RING - 1)]
    partners += [on_z(k) for k in (1, DEPTH - 1, 2, DEPTH - 2)]
    for d in partners:
        pl.semaphore_signal(barrier, inc=1, device_id=d, device_id_type=MESH)

    fetched = [
        pltpu.make_async_copy(src, dst, ls.at[n])
        for n, (src, dst) in enumerate(
            (
                (disc, dv),
                (sens.at[pl.ds(pl.multiple_of(c * half, 16), half)], s_own),
                (cash, cv), (index, iv), (exer, ev), (steps, sv), (jac, jv),
            )
        )
    ]
    for f in fetched:
        f.start()

    first_cut = (half // 4 // 16 + 1) * 16
    cuts = (0, first_cut, half // 2, half // 2 + first_cut, half)

    def s_copy(q):
        n = cuts[q + 1] - cuts[q]
        return (
            sens.at[pl.ds(pl.multiple_of(sib * half + cuts[q], 16), n)],
            s_in.at[pl.ds(cuts[q], n)], ss_s.at[q], rs_s.at[q], sibling,
        )

    d_copy = (disc, d_in, ss_s.at[RING], rs_s.at[RING], sibling)

    xs[half : half + 8] = jnp.zeros((8, LANE), F32)
    for f in fetched[:2]:
        f.wait()
    third = half // 3

    @pl.loop(0, 3)
    def _(n):
        rws = pl.ds(pl.multiple_of(n * third, 16), third)
        xs[rws] = jnp.dot(s_own[rws], dv[...], preferred_element_type=F32)

    pl.semaphore_wait(barrier, len(partners))
    send(*d_copy)
    for q in range(RING):
        send(*s_copy(q))
    for n, k in enumerate((2, DEPTH - 2)):
        pl.semaphore_signal(near_z.at[n], inc=1, device_id=on_z(k), device_id_type=MESH)

    main = CHIPS * LANE
    more = (params - main) // CHIPS
    groups = pad // GROUP
    turn = lax.rem(z, RING) == y
    core = lax.div(x, 2)
    high = lax.div(z, RING)
    for f in fetched[2:]:
        f.wait()

    @pl.when(turn)
    def _():
        jp[...] = jnp.zeros(jp.shape, BF16)

        @pl.loop(0, DEPTH)
        def _(zz):
            for t in range(RING):
                col = pl.multiple_of((zz * RING + t) * LANE, LANE)
                jp[zz, t, 0:jrows] = jv[:, pl.ds(col, LANE)]

        je[...] = jnp.zeros(je.shape, F32)
        je[0:jrows, 0 : params - main] = jv[:, main:params].astype(F32)
        for t in range(CHIPS):
            packed = [
                je[r * GROUP : (r + 1) * GROUP, t * more : (t + 1) * more] for r in range(groups)
            ]
            packed.append(jnp.zeros((GROUP, LANE - groups * more), F32))
            jp[t // RING, t % RING, pad : pad + GROUP] = jnp.concatenate(packed, axis=1).astype(BF16)

        pltpu.make_async_copy(jp.at[z], jz.at[high], rs_j.at[2, high]).start()

    def j_line(k):
        zz = lax.rem(z + k, DEPTH)
        return jp.at[zz], jz.at[high], ss_j.at[k], rs_j.at[2, high], on_z(k)

    def j_depth(*steps_):
        @pl.when(turn)
        def _():
            for k in steps_:
                rdma(*j_line(k)).start()

    j_depth(2, 6, 1, 7)

    def part_rows(n, size):
        return pl.ds(pl.multiple_of(n * size, 8), size)

    class Scatter:
        def __init__(self, q):
            self.q = q
            self.i, self.on = lines[q % 2]
            self.nr, self.far, self.nl = (lax.rem(self.i + k, RING) for k in (1, 2, 3))
            self.right, self.left = self.on(1), self.on(3)

        def msg(self, n, h, k, dev):
            q = self.q
            return (
                xp.at[q, k, h * pad : (h + 1) * pad], r1.at[q, n],
                ss_1.at[q, n], rs_1.at[q, n], dev,
            )

        def first(self):
            send(*self.msg(0, 0, self.far, self.right))
            send(*self.msg(2, 1, self.far, self.left))
            send(*self.msg(3, 1, self.nr, self.right))
            send(*self.msg(1, 0, self.nl, self.left))

        def second(self):
            for h, n, k, dev in ((0, 0, self.nr, self.right), (1, 2, self.nl, self.left)):
                rdma(*self.msg(n, h, k, dev)).wait_recv()
                xp[self.q, k, h * pad : (h + 1) * pad] += r1[self.q, n]
                send(*self.msg(4 + h, h, k, dev))

        def result(self):
            for h, n in ((0, 1), (1, 3)):
                rdma(*self.msg(n, h, self.i, self.left)).wait_recv()
                rdma(*self.msg(4 + h, h, self.i, self.left)).wait_recv()
                rws = slice(h * pad, (h + 1) * pad)
                y2[self.q, rws] = xp[self.q, self.i, rws] + r1[self.q, n] + r1[self.q, 4 + h]

    one = [Scatter(q) for q in range(RING)]
    rdma(*d_copy).wait_recv()
    for q in range(RING):
        rdma(*s_copy(q)).wait_recv()
        xs[cuts[q] : cuts[q + 1]] += jnp.dot(
            s_in[cuts[q] : cuts[q + 1]], d_in[...], preferred_element_type=F32
        )
        for k in range(RING):
            for u in (0, 1):
                top = (8 * q + 2 * k + u) * jrows
                xp[q, k, u * pad : (u + 1) * pad] = xs[top : top + pad]
        one[q].first()

    for n in (0, 1):
        pl.semaphore_wait(near_z.at[n], 1)
    j_depth(4, 3, 5)
    one[0].second()
    one[1].second()
    one[2].second()
    one[3].second()

    def j_cross(e, k):
        xx = lax.rem(x + k, RING)
        two_ = pl.ds(2 * lax.rem(x, 2), 2)
        if e == 0:
            src = jz.at[:, xx, 0:pad]
            dst = jr.at[two_, y, pl.ds(pl.multiple_of(c * pad, 16), pad)]
        else:
            src = jz.at[:, xx, pad : pad + GROUP]
            dst = jx.at[two_, y, c]
        return src, dst, ss_jx.at[e, k], rs_j.at[e, 0], at_chip(xx, z, core)

    def both(f):
        f(0)
        f(1)

    def j_send(e):
        for k in (1, 3):
            rdma(*j_cross(e, k)).start()
        src, dst, ss, rs, dev = j_cross(e, 0)

        @pl.when(core == c)
        def _():
            pltpu.make_async_copy(src, dst, rs).start()

        @pl.when(core != c)
        def _():
            rdma(src, dst, ss, rs, dev).start()

    for n in (0, 1):
        pltpu.make_async_copy(jp.at[0], jz.at[n], rs_j.at[2, n]).wait()
    both(j_send)

    slots = cash.shape[0]
    forwards = lax.broadcasted_iota(jnp.int32, (LANE, trades), 0)
    late = forwards >= ev[...]
    weights = jnp.zeros((LANE, trades), F32)
    for s in range(slots):
        weights += jnp.where(late & (iv[s : s + 1] == forwards), cv[s : s + 1], 0.0)
    weights = weights * (1.0 / (disc.shape[0] * PATHS * RING))
    weights = weights.T
    w_hi = weights.astype(BF16)
    w_lo = (weights - w_hi.astype(F32)).astype(BF16)
    wt[...] = jnp.concatenate([w_hi, w_hi, w_lo], axis=1)
    reach = jnp.broadcast_to((sv[...] * width).astype(F32), (LANE, trades)).T.astype(jnp.int32)
    lane = lax.broadcasted_iota(jnp.int32, (trades, 2 * pad), 1)
    room[...] = (
        jnp.concatenate([reach, reach[:, : 2 * pad - LANE]], axis=1)
        - lane + jnp.where(lane >= pad, pad - jrows, 0) - c * half
    )

    part = y2.shape[1] // RING

    def two(q, k):
        i, on = lines[1 - q % 2]
        return (
            y2.at[q, part_rows(lax.rem(i + k, RING), part)], r2.at[q, i],
            ss_2.at[q, k], rs_2.at[q], on(k),
        )

    for g in (0, 1):
        for q in (2 * g, 2 * g + 1):
            one[q].result()
            for k in (2, 1, 3):
                send(*two(q, k))
    both(lambda e: rdma(*j_cross(e, 2)).start())

    share = zr.shape[1]
    count = 2 * part // share
    spread = (4, 3, 5, 2, 6, 1, 7)

    def turn_of(g, d):
        return lax.rem(d + count * g, DEPTH)

    def reduces(g):
        return turn_of(g, z) < count

    def z_piece(g, d):
        return part_rows(jnp.minimum(turn_of(g, d), count - 1), share)

    for g in (0, 1):
        for p in (0, 1):
            q = 2 * g + p
            i, on = lines[1 - p]
            total = y2[q, part_rows(i, part)]
            three = r2.at[q, 0 : RING - 1]
            rdma(three, three, ss_2.at[q, 0], rs_2.at[q], sibling).wait_recv()
            for k in (1, 2, 3):
                total += r2[q, lax.rem(i + k, RING)]
            zb[g, p * part : (p + 1) * part] = total
        for k in spread:
            d = lax.rem(z + k, DEPTH)
            send_if(
                turn_of(g, d) < count,
                zb.at[g, z_piece(g, d)], rz.at[g, z], ss_z.at[g, k], rs_z.at[g], on_z(k),
            )


    def j_ring(half_, k, n, dev):
        ref = jr.at[pl.ds(2 * half_, 2), k]
        return ref, ref, ss_ja.at[0, n], rs_ja.at[0, n], dev

    def j_fan(k):
        ref = jx.at[:, y]
        return ref, ref, ss_ja.at[1, k], rs_ja.at[1, 0], on_y(k)

    yr, yl = on_y(1), on_y(3)
    ynr, yfar, ynl = (lax.rem(y + k, RING) for k in (1, 2, 3))

    def j_start():
        for e, whole in ((0, jr.at[:, y]), (1, jx.at[:, y])):
            pltpu.make_async_copy(whole, whole, rs_j.at[e, 0]).wait()
        for n, (hh, d) in enumerate(((0, yr), (1, yl), (1, yr), (0, yl))):
            send(*j_ring(hh, y, n, d))
        for k in (2, 1, 3):
            send(*j_fan(k))

    def j_forward():
        rdma(*j_ring(0, ynl, 0, yr)).wait_recv()
        send(*j_ring(0, ynl, 4, yr))
        rdma(*j_ring(1, ynr, 1, yl)).wait_recv()
        send(*j_ring(1, ynr, 5, yl))

    def j_finish():
        for hh, k, n, d in ((1, ynl, 2, yr), (0, ynr, 3, yl), (0, yfar, 4, yr), (1, yfar, 5, yl)):
            rdma(*j_ring(hh, k, n, d)).wait_recv()
        three = jx.at[0 : RING - 1]
        rdma(three, three, ss_ja.at[1, 0], rs_ja.at[1, 0], sibling).wait_recv()

        @pl.loop(0, RING * RING)
        def _(n):
            q, k = lax.div(n, RING), lax.rem(n, RING)
            for u in (0, 1):
                tile = jx[q, k, u].astype(F32)
                for r in range(groups):
                    at = u * pad + r * GROUP
                    turned_ = tile if r == 0 else pltpu.roll(tile, LANE - r * more, 1)
                    jb[n, at : at + GROUP] = turned_.astype(BF16)

    j_start()

    for g in (0, 1):
        reducer = reduces(g)

        @pl.when(reducer)
        def _():
            total = zb[g, z_piece(g, z)]
            seven = rz.at[g, 0 : DEPTH - 1]
            rdma(seven, seven, ss_z.at[g, 0], rs_z.at[g], sibling).wait_recv()
            for k in range(1, DEPTH):
                total += rz[g, lax.rem(z + k, DEPTH)]
            zr[g] = total
            zf[g, z_piece(g, z)] = total

        for k in spread:
            send_if(
                reducer, zr.at[g], zf.at[g, z_piece(g, z)], ss_g.at[g, k], rs_g.at[g], on_z(k)
            )

    j_forward()

    def home(q, i):
        return xf.at[q, lines[q % 2][0], part_rows(i, part)]

    for g in (0, 1):
        for some, ref in ((reduces(g), zf.at[g, 0 : (count - 1) * share]), (~reduces(g), zf.at[g])):

            @pl.when(some)
            def _():
                rdma(ref, ref, ss_g.at[g, 0], rs_g.at[g], sibling).wait_recv()

        for p in (0, 1):
            q = 2 * g + p
            i, on = lines[1 - p]
            mine = zf.at[g, p * part : (p + 1) * part]
            for k in (2, 1, 3):
                send(mine, home(q, i), ss_a2.at[q, k], rs_a2.at[q], on(k))
            home(q, i)[...] = mine[...]

    class Gather:
        def __init__(self, q):
            self.q = q
            self.i, self.on = lines[q % 2]
            self.nr, self.far, self.nl = (lax.rem(self.i + k, RING) for k in (1, 2, 3))
            self.right, self.left = self.on(1), self.on(3)

        def msg(self, n, h, k, dev):
            ref = xf.at[self.q, k, h * pad : (h + 1) * pad]
            return ref, ref, ss_a1.at[self.q, n], rs_a1.at[self.q, n], dev

        def start(self):
            q = self.q
            three = xf.at[q, 0, 0 : (RING - 1) * part]
            rdma(three, three, ss_a2.at[q, 0], rs_a2.at[q], sibling).wait_recv()
            send(*self.msg(0, 0, self.i, self.right))
            send(*self.msg(1, 1, self.i, self.left))
            send(*self.msg(2, 1, self.i, self.right))
            send(*self.msg(3, 0, self.i, self.left))

        def forward(self):
            rdma(*self.msg(0, 0, self.nl, self.right)).wait_recv()
            send(*self.msg(4, 0, self.nl, self.right))
            rdma(*self.msg(1, 1, self.nr, self.left)).wait_recv()
            send(*self.msg(5, 1, self.nr, self.left))

    ring = [Gather(q) for q in range(RING)]
    for q in range(RING):
        ring[q].start()
    ring[0].forward()
    ring[1].forward()

    acc[...] = jnp.zeros(acc.shape, F32)

    def block(q, k):
        values = xf[q, k]
        hi = values.astype(BF16)
        lo = (values - hi.astype(F32)).astype(BF16)
        vega = lax.dot_general(
            wt[...], jnp.concatenate([hi, lo, hi], axis=1), (((1,), (1,)), ((), ())),
            preferred_element_type=F32,
        )
        masked = jnp.where(room[...] > (8 * q + 2 * k) * jrows, vega, 0.0).astype(BF16)
        both_ = jnp.concatenate([jr[q, k], jb[RING * q + k]], axis=1)
        acc[...] += jnp.dot(masked, both_, preferred_element_type=F32)

    def landed(q, k, h, n):
        ref = xf.at[q, k, h * pad : (h + 1) * pad]
        rdma(ref, ref, ss_a1.at[q, n], rs_a1.at[q, n], sibling).wait_recv()

    def ring_place(q, step):
        return lax.rem(jnp.where(lax.rem(q, 2) == 0, x, y) + step, RING)

    j_finish()

    @pl.loop(0, 2)
    def _(q):
        block(q, ring_place(q, 0))

    ring[2].forward()
    ring[3].forward()

    @pl.loop(2, RING)
    def _(q):
        block(q, ring_place(q, 0))

    @pl.loop(0, 2 * RING)
    def _(n):
        q = lax.div(n, 2)
        k = ring_place(q, 3 - 2 * lax.rem(n, 2))

        @pl.when(lax.rem(n, 2) == 0)
        def _():
            landed(q, k, 1, 2)

        @pl.when(lax.rem(n, 2) == 1)
        def _():
            landed(q, k, 0, 3)

        block(q, k)

    @pl.loop(0, RING)
    def _(q):
        k = ring_place(q, 2)
        landed(q, k, 0, 4)
        landed(q, k, 1, 5)
        block(q, k)

    rows_c = pl.ds(pl.multiple_of(c * (trades // 2), 8), trades // 2)
    rows_sib = pl.ds(pl.multiple_of(sib * (trades // 2), 8), trades // 2)
    swap = (acc.at[rows_sib], pr, ss_p.at[0], rs_p.at[0], sibling)
    send(*swap)
    strip_rows = out.shape[0]
    rdma(*swap).wait_recv()
    total = acc[rows_c] + pr[...]
    po[...] = jnp.concatenate(
        [total[:, s * LANE : (s + 1) * LANE].reshape(CHIPS, strip_rows, LANE) for s in (0, 1)], axis=1
    ).astype(BF16)

    def deliver(n, dst):
        tile = ob.at[z * RING + x]

        @pl.when(dst != me)
        def _():
            rdma(po.at[n], tile, ss_o.at[0], rs_o.at[0], {"grp": y, "path": dst}).start()

        @pl.when(dst == me)
        def _():
            pltpu.make_async_copy(po.at[n], tile, rs_o.at[0]).start()

    for k in (4, 3, 5, 2, 6, 1, 7, 0):
        zz = lax.rem(z + k, DEPTH)
        for side in (0, 1):
            for u in (0, 1):
                n = side * 2 * DEPTH + 2 * zz + u
                deliver(n, c * CHIPS + n)

    for cond, d in sent:
        if cond is None:
            d.wait_send()
        else:
            pl.when(cond)(d.wait_send)

    def j_crossed(e):
        for k in (1, 2, 3):
            rdma(*j_cross(e, k)).wait_send()

        @pl.when(core != c)
        def _():
            rdma(*j_cross(e, 0)).wait_send()

    both(j_crossed)

    @pl.when(turn)
    def _():
        for k in range(1, DEPTH):
            rdma(*j_line(k)).wait_send()

    pltpu.make_async_copy(ob, ob, rs_o.at[0]).wait()

    rest = []
    for t in range(CHIPS):
        tile = ob[t].astype(F32)
        out[:, t * LANE : (t + 1) * LANE] = tile[0:strip_rows]
        rest.append(tile[strip_rows : 2 * strip_rows, 0:more])
    out[:, main:params] = jnp.concatenate(rest, axis=1)

    def po_sent(n):
        rdma(po.at[0:n], po.at[0:n], ss_o.at[0], rs_o.at[0], sibling).wait_send()

    pl.when(core == c)(lambda: po_sent(CHIPS - 1))
    pl.when(core != c)(lambda: po_sent(CHIPS))


def per_device(
    path_sens, discounts, cash_flows, flow_index, exercise_step, trade_steps, jacobian_inv
):
    paths_own, params = path_sens.shape
    trades = cash_flows.shape[0]
    jrows = jacobian_inv.shape[0]
    strip = trades // PATHS
    rest = params - CHIPS * LANE
    pad = -(-jrows // 16) * 16
    half = params // 2
    slots = cash_flows.shape[1]
    part = pad // 2
    share = 16
    vm = pltpu.VMEM
    dma = pltpu.SemaphoreType.DMA
    scratch = [
        vm((paths_own, LANE), BF16),
        vm((slots, trades), F32),
        vm((slots, trades), jnp.int32),
        vm((1, trades), jnp.int32),
        vm((1, trades), jnp.int32),
        vm((half, paths_own), BF16),
        vm((half, paths_own), BF16),
        vm((paths_own, LANE), BF16),
        vm((half + 8, LANE), F32),
        vm((RING, RING, 2 * pad, LANE), F32),
        vm((RING, 6, pad, LANE), F32),
        vm((RING, 2 * pad, LANE), F32),
        vm((RING, RING, part, LANE), F32),
        vm((2, 2 * part, LANE), F32),
        vm((2, DEPTH, share, LANE), F32),
        vm((2, share, LANE), F32),
        vm((2, 2 * part, LANE), F32),
        vm((RING, RING, 2 * pad, LANE), F32),
        vm((jrows, params), BF16),
        vm((pad, -(-rest // LANE) * LANE), F32),
        vm((DEPTH, RING, pad + GROUP, LANE), BF16),
        vm((2, RING, pad + GROUP, LANE), BF16),
        vm((RING, RING, 2 * pad, LANE), BF16),
        vm((RING, RING, 2, GROUP, LANE), BF16),
        vm((RING * RING, 2 * pad, LANE), BF16),
        vm((trades, 3 * LANE), BF16),
        vm((trades, 2 * pad), jnp.int32),
        vm((trades, 2 * LANE), F32),
        vm((trades // 2, 2 * LANE), F32),
        vm((CHIPS, 2 * strip, LANE), BF16),
        vm((CHIPS, 2 * strip, LANE), BF16),
        dma((RING + 1,)), dma((RING + 1,)), dma((7,)),
        dma((RING, 6)), dma((RING, 6)),
        dma((RING, RING)), dma((RING,)),
        dma((2, DEPTH)), dma((2,)),
        dma((2, DEPTH)), dma((2,)),
        dma((RING, RING)), dma((RING,)),
        dma((RING, 6)), dma((RING, 6)),
        dma((DEPTH,)), dma((2, RING)), dma((3, 2)),
        dma((2, 6)), dma((2, 6)),
        dma((2,)), dma((2,)),
        dma((1,)), dma((1,)),
        pltpu.SemaphoreType.REGULAR((2,)),
    ]
    vmem = pl.BlockSpec(memory_space=pltpu.VMEM)
    hbm = pl.BlockSpec(memory_space=pl.ANY)
    return pl.pallas_call(
        kernel,
        out_shape=jax.ShapeDtypeStruct((strip, params), F32),
        in_specs=[hbm] * 7,
        out_specs=vmem,
        scratch_shapes=scratch,
        compiler_params=pltpu.CompilerParams(
            collective_id=0, has_side_effects=True, vmem_limit_bytes=56 * 1024 * 1024
        ),
    )(
        discounts,
        path_sens.T,
        cash_flows.T,
        flow_index.T,
        exercise_step.reshape(1, trades),
        trade_steps.reshape(1, trades),
        jacobian_inv,
    )


def solution(mesh):
    placed = (
        P(("grp", "path"), None),
        P(("grp", "path"), None),
        P("grp", None),
        P("grp", None),
        P("grp"),
        P("grp"),
        P("path", None),
    )
    return jax.shard_map(
        per_device, mesh=mesh, in_specs=placed, out_specs=P(("grp", "path"), None), check_vma=False
    )
```

```python
import jax
import jax.numpy as jnp
from jax import lax
from jax.experimental import pallas as pl
from jax.experimental.pallas import tpu as pltpu
from jax.sharding import PartitionSpec as P

NB = 40
LANE = 128
RING = 4
DEPTH = 8
CHIPS = RING * DEPTH
PATHS = 2 * CHIPS
GROUP = 16
F32 = jnp.float32
BF16 = jnp.bfloat16
MESH = pl.DeviceIdType.MESH


def kernel(
    disc, sens, cash, index, exer, steps, jac, out,
    dv, cv, iv, ev, sv, s_own, s_in, d_in, xs, xp, r1, y2, r2, zb, rz, zr, zf, xf,
    jv, je, jp, jz, jr, jx, jb, wt, room, acc, pr, po, ob,
    ss_s, rs_s, ls, ss_1, rs_1, ss_2, rs_2, ss_z, rs_z, ss_g, rs_g,
    ss_a2, rs_a2, ss_a1, rs_a1, ss_j, ss_jx, rs_j, ss_ja, rs_ja, ss_p, rs_p, ss_o, rs_o, near_z,
):
    y = lax.axis_index("grp")
    me = lax.axis_index("path")
    j = lax.div(me, 2)
    c = lax.rem(me, 2)
    x = lax.div(j, DEPTH)
    z = lax.rem(j, DEPTH)
    sib = 1 - c
    params = sens.shape[0]
    width = params // NB
    half = params // 2
    jrows = jac.shape[0]
    pad = xp.shape[2] // 2
    trades = cash.shape[1]

    def at_chip(xx, zz, cc):
        return {"grp": y, "path": (xx * DEPTH + zz) * 2 + cc}

    def rdma(src, dst, ss, rs, dev):
        return pltpu.make_async_remote_copy(
            src_ref=src, dst_ref=dst, send_sem=ss, recv_sem=rs, device_id=dev, device_id_type=MESH
        )

    sent = []

    def send(*args):
        d = rdma(*args)
        d.start()
        sent.append((None, d))

    def send_if(cond, *args):
        d = rdma(*args)

        @pl.when(cond)
        def _():
            d.start()

        sent.append((cond, d))

    sibling = at_chip(x, z, sib)

    def on_x(k):
        return at_chip(lax.rem(x + k, RING), z, c)

    def on_y(k):
        return {"grp": lax.rem(y + k, RING), "path": me}

    def on_z(k):
        return at_chip(x, lax.rem(z + k, DEPTH), c)

    lines = ((x, on_x), (y, on_y))

    barrier = pltpu.get_barrier_semaphore()
    partners = [sibling] + [on(k) for on in (on_x, on_y) for k in (1, RING - 1)]
    partners += [on_z(k) for k in (1, DEPTH - 1, 2, DEPTH - 2)]
    for d in partners:
        pl.semaphore_signal(barrier, inc=1, device_id=d, device_id_type=MESH)

    fetched = [
        pltpu.make_async_copy(src, dst, ls.at[n])
        for n, (src, dst) in enumerate(
            (
                (disc, dv),
                (sens.at[pl.ds(pl.multiple_of(c * half, 16), half)], s_own),
                (cash, cv), (index, iv), (exer, ev), (steps, sv), (jac, jv),
            )
        )
    ]
    for f in fetched:
        f.start()

    first_cut = (half // 4 // 16 + 1) * 16
    cuts = (0, first_cut, half // 2, half // 2 + first_cut, half)

    def s_copy(q):
        n = cuts[q + 1] - cuts[q]
        return (
            sens.at[pl.ds(pl.multiple_of(sib * half + cuts[q], 16), n)],
            s_in.at[pl.ds(cuts[q], n)], ss_s.at[q], rs_s.at[q], sibling,
        )

    d_copy = (disc, d_in, ss_s.at[RING], rs_s.at[RING], sibling)

    xs[half : half + 8] = jnp.zeros((8, LANE), F32)
    for f in fetched[:2]:
        f.wait()
    third = half // 3

    @pl.loop(0, 3)
    def _(n):
        rws = pl.ds(pl.multiple_of(n * third, 16), third)
        xs[rws] = jnp.dot(s_own[rws], dv[...], preferred_element_type=F32)

    pl.semaphore_wait(barrier, len(partners))
    send(*d_copy)
    for q in range(RING):
        send(*s_copy(q))
    for n, k in enumerate((2, DEPTH - 2)):
        pl.semaphore_signal(near_z.at[n], inc=1, device_id=on_z(k), device_id_type=MESH)

    main = CHIPS * LANE
    more = (params - main) // CHIPS
    groups = pad // GROUP
    turn = lax.rem(z, RING) == y
    core = lax.div(x, 2)
    high = lax.div(z, RING)
    for f in fetched[2:]:
        f.wait()

    @pl.when(turn)
    def _():
        jp[...] = jnp.zeros(jp.shape, BF16)

        @pl.loop(0, DEPTH)
        def _(zz):
            for t in range(RING):
                col = pl.multiple_of((zz * RING + t) * LANE, LANE)
                jp[zz, t, 0:jrows] = jv[:, pl.ds(col, LANE)]

        je[...] = jnp.zeros(je.shape, F32)
        je[0:jrows, 0 : params - main] = jv[:, main:params].astype(F32)
        for t in range(CHIPS):
            packed = [
                je[r * GROUP : (r + 1) * GROUP, t * more : (t + 1) * more] for r in range(groups)
            ]
            packed.append(jnp.zeros((GROUP, LANE - groups * more), F32))
            jp[t // RING, t % RING, pad : pad + GROUP] = jnp.concatenate(packed, axis=1).astype(BF16)

        pltpu.make_async_copy(jp.at[z], jz.at[high], rs_j.at[2, high]).start()

    def j_line(k):
        zz = lax.rem(z + k, DEPTH)
        return jp.at[zz], jz.at[high], ss_j.at[k], rs_j.at[2, high], on_z(k)

    def j_depth(*steps_):
        @pl.when(turn)
        def _():
            for k in steps_:
                rdma(*j_line(k)).start()

    j_depth(2, 6, 1, 7)

    def part_rows(n, size):
        return pl.ds(pl.multiple_of(n * size, 8), size)

    class Scatter:
        def __init__(self, q):
            self.q = q
            self.i, self.on = lines[q % 2]
            self.nr, self.far, self.nl = (lax.rem(self.i + k, RING) for k in (1, 2, 3))
            self.right, self.left = self.on(1), self.on(3)

        def msg(self, n, h, k, dev):
            q = self.q
            return (
                xp.at[q, k, h * pad : (h + 1) * pad], r1.at[q, n],
                ss_1.at[q, n], rs_1.at[q, n], dev,
            )

        def first(self):
            send(*self.msg(0, 0, self.far, self.right))
            send(*self.msg(2, 1, self.far, self.left))
            send(*self.msg(3, 1, self.nr, self.right))
            send(*self.msg(1, 0, self.nl, self.left))

        def second(self):
            for h, n, k, dev in ((0, 0, self.nr, self.right), (1, 2, self.nl, self.left)):
                rdma(*self.msg(n, h, k, dev)).wait_recv()
                xp[self.q, k, h * pad : (h + 1) * pad] += r1[self.q, n]
                send(*self.msg(4 + h, h, k, dev))

        def result(self):
            for h, n in ((0, 1), (1, 3)):
                rdma(*self.msg(n, h, self.i, self.left)).wait_recv()
                rdma(*self.msg(4 + h, h, self.i, self.left)).wait_recv()
                rws = slice(h * pad, (h + 1) * pad)
                y2[self.q, rws] = xp[self.q, self.i, rws] + r1[self.q, n] + r1[self.q, 4 + h]

    one = [Scatter(q) for q in range(RING)]
    rdma(*d_copy).wait_recv()
    for q in range(RING):
        rdma(*s_copy(q)).wait_recv()
        xs[cuts[q] : cuts[q + 1]] += jnp.dot(
            s_in[cuts[q] : cuts[q + 1]], d_in[...], preferred_element_type=F32
        )
        for k in range(RING):
            for u in (0, 1):
                top = (8 * q + 2 * k + u) * jrows
                xp[q, k, u * pad : (u + 1) * pad] = xs[top : top + pad]
        one[q].first()

    for n in (0, 1):
        pl.semaphore_wait(near_z.at[n], 1)
    j_depth(4, 3, 5)
    one[0].second()
    one[1].second()
    one[2].second()
    one[3].second()

    def j_cross(e, k):
        xx = lax.rem(x + k, RING)
        two_ = pl.ds(2 * lax.rem(x, 2), 2)
        if e == 0:
            src = jz.at[:, xx, 0:pad]
            dst = jr.at[two_, y, pl.ds(pl.multiple_of(c * pad, 16), pad)]
        else:
            src = jz.at[:, xx, pad : pad + GROUP]
            dst = jx.at[two_, y, c]
        return src, dst, ss_jx.at[e, k], rs_j.at[e, 0], at_chip(xx, z, core)

    def both(f):
        f(0)
        f(1)

    def j_send(e):
        for k in (1, 3):
            rdma(*j_cross(e, k)).start()
        src, dst, ss, rs, dev = j_cross(e, 0)

        @pl.when(core == c)
        def _():
            pltpu.make_async_copy(src, dst, rs).start()

        @pl.when(core != c)
        def _():
            rdma(src, dst, ss, rs, dev).start()

    for n in (0, 1):
        pltpu.make_async_copy(jp.at[0], jz.at[n], rs_j.at[2, n]).wait()
    both(j_send)

    slots = cash.shape[0]
    forwards = lax.broadcasted_iota(jnp.int32, (LANE, trades), 0)
    late = forwards >= ev[...]
    weights = jnp.zeros((LANE, trades), F32)
    for s in range(slots):
        weights += jnp.where(late & (iv[s : s + 1] == forwards), cv[s : s + 1], 0.0)
    weights = weights * (1.0 / (disc.shape[0] * PATHS * RING))
    weights = weights.T
    w_hi = weights.astype(BF16)
    w_lo = (weights - w_hi.astype(F32)).astype(BF16)
    wt[...] = jnp.concatenate([w_hi, w_hi, w_lo], axis=1)
    reach = jnp.broadcast_to((sv[...] * width).astype(F32), (LANE, trades)).T.astype(jnp.int32)
    span = 4 * pad
    lane = lax.broadcasted_iota(jnp.int32, (trades, span), 1)
    lane = lane - jnp.where(lane >= 2 * pad, 2 * pad, 0)
    room[...] = (
        jnp.concatenate([reach] * (span // LANE) + [reach[:, : span % LANE]], axis=1)
        - lane + jnp.where(lane >= pad, pad - jrows, 0) - c * half
    )

    part = y2.shape[1] // RING

    def two(q, k):
        i, on = lines[1 - q % 2]
        return (
            y2.at[q, part_rows(lax.rem(i + k, RING), part)], r2.at[q, i],
            ss_2.at[q, k], rs_2.at[q], on(k),
        )

    for g in (0, 1):
        for q in (2 * g, 2 * g + 1):
            one[q].result()
            for k in (2, 1, 3):
                send(*two(q, k))
    both(lambda e: rdma(*j_cross(e, 2)).start())

    share = zr.shape[1]
    count = 2 * part // share
    spread = (4, 3, 5, 2, 6, 1, 7)

    def turn_of(g, d):
        return lax.rem(d + count * g, DEPTH)

    def reduces(g):
        return turn_of(g, z) < count

    def z_piece(g, d):
        return part_rows(jnp.minimum(turn_of(g, d), count - 1), share)

    for g in (0, 1):
        for p in (0, 1):
            q = 2 * g + p
            i, on = lines[1 - p]
            total = y2[q, part_rows(i, part)]
            three = r2.at[q, 0 : RING - 1]
            rdma(three, three, ss_2.at[q, 0], rs_2.at[q], sibling).wait_recv()
            for k in (1, 2, 3):
                total += r2[q, lax.rem(i + k, RING)]
            zb[g, p * part : (p + 1) * part] = total
        for k in spread:
            d = lax.rem(z + k, DEPTH)
            send_if(
                turn_of(g, d) < count,
                zb.at[g, z_piece(g, d)], rz.at[g, z], ss_z.at[g, k], rs_z.at[g], on_z(k),
            )


    def j_ring(half_, k, n, dev):
        ref = jr.at[pl.ds(2 * half_, 2), k]
        return ref, ref, ss_ja.at[0, n], rs_ja.at[0, n], dev

    def j_fan(k):
        ref = jx.at[:, y]
        return ref, ref, ss_ja.at[1, k], rs_ja.at[1, 0], on_y(k)

    yr, yl = on_y(1), on_y(3)
    ynr, yfar, ynl = (lax.rem(y + k, RING) for k in (1, 2, 3))

    def j_start():
        for e, whole in ((0, jr.at[:, y]), (1, jx.at[:, y])):
            pltpu.make_async_copy(whole, whole, rs_j.at[e, 0]).wait()
        for n, (hh, d) in enumerate(((0, yr), (1, yl), (1, yr), (0, yl))):
            send(*j_ring(hh, y, n, d))
        for k in (2, 1, 3):
            send(*j_fan(k))

    def j_forward():
        rdma(*j_ring(0, ynl, 0, yr)).wait_recv()
        send(*j_ring(0, ynl, 4, yr))
        rdma(*j_ring(1, ynr, 1, yl)).wait_recv()
        send(*j_ring(1, ynr, 5, yl))

    def j_finish():
        for hh, k, n, d in ((1, ynl, 2, yr), (0, ynr, 3, yl), (0, yfar, 4, yr), (1, yfar, 5, yl)):
            rdma(*j_ring(hh, k, n, d)).wait_recv()

    def j_unpack():
        three = jx.at[0 : RING - 1]
        rdma(three, three, ss_ja.at[1, 0], rs_ja.at[1, 0], sibling).wait_recv()

        @pl.loop(0, RING * RING)
        def _(n):
            q, k = lax.div(n, RING), lax.rem(n, RING)
            for u in (0, 1):
                tile = jx[q, k, u].astype(F32)
                for r in range(groups):
                    at = u * pad + r * GROUP
                    turned_ = tile if r == 0 else pltpu.roll(tile, LANE - r * more, 1)
                    jb[n, at : at + GROUP] = turned_.astype(BF16)

    j_start()

    for g in (0, 1):
        reducer = reduces(g)

        @pl.when(reducer)
        def _():
            total = zb[g, z_piece(g, z)]
            seven = rz.at[g, 0 : DEPTH - 1]
            rdma(seven, seven, ss_z.at[g, 0], rs_z.at[g], sibling).wait_recv()
            for k in range(1, DEPTH):
                total += rz[g, lax.rem(z + k, DEPTH)]
            zr[g] = total
            zf[g, z_piece(g, z)] = total

        for k in spread:
            send_if(
                reducer, zr.at[g], zf.at[g, z_piece(g, z)], ss_g.at[g, k], rs_g.at[g], on_z(k)
            )

    j_forward()

    def home(q, i):
        return xf.at[q, lines[q % 2][0], part_rows(i, part)]

    for g in (0, 1):
        for some, ref in ((reduces(g), zf.at[g, 0 : (count - 1) * share]), (~reduces(g), zf.at[g])):

            @pl.when(some)
            def _():
                rdma(ref, ref, ss_g.at[g, 0], rs_g.at[g], sibling).wait_recv()

        for p in (0, 1):
            q = 2 * g + p
            i, on = lines[1 - p]
            mine = zf.at[g, p * part : (p + 1) * part]
            for k in (2, 1, 3):
                send(mine, home(q, i), ss_a2.at[q, k], rs_a2.at[q], on(k))
            home(q, i)[...] = mine[...]

    j_unpack()

    class Gather:
        def __init__(self, q):
            self.q = q
            self.i, self.on = lines[q % 2]
            self.nr, self.far, self.nl = (lax.rem(self.i + k, RING) for k in (1, 2, 3))
            self.right, self.left = self.on(1), self.on(3)

        def msg(self, n, h, k, dev):
            ref = xf.at[self.q, k, h * pad : (h + 1) * pad]
            return ref, ref, ss_a1.at[self.q, n], rs_a1.at[self.q, n], dev

        def start(self):
            q = self.q
            three = xf.at[q, 0, 0 : (RING - 1) * part]
            rdma(three, three, ss_a2.at[q, 0], rs_a2.at[q], sibling).wait_recv()
            send(*self.msg(0, 0, self.i, self.right))
            send(*self.msg(1, 1, self.i, self.left))
            send(*self.msg(2, 1, self.i, self.right))
            send(*self.msg(3, 0, self.i, self.left))

        def forward(self):
            rdma(*self.msg(0, 0, self.nl, self.right)).wait_recv()
            send(*self.msg(4, 0, self.nl, self.right))
            rdma(*self.msg(1, 1, self.nr, self.left)).wait_recv()
            send(*self.msg(5, 1, self.nr, self.left))

    ring = [Gather(q) for q in range(RING)]
    for q in range(RING):
        ring[q].start()
    ring[0].forward()
    ring[1].forward()

    acc[...] = jnp.zeros(acc.shape, F32)

    second_lane = lax.broadcasted_iota(jnp.int32, (1, span), 1) >= 2 * pad

    def pair(*both_):
        values = jnp.concatenate([xf[q, k] for q, k in both_], axis=0)
        hi = values.astype(BF16)
        lo = (values - hi.astype(F32)).astype(BF16)
        vega = lax.dot_general(
            wt[...], jnp.concatenate([hi, lo, hi], axis=1), (((1,), (1,)), ((), ())),
            preferred_element_type=F32,
        )
        start = [(8 * q + 2 * k) * jrows for q, k in both_]
        masked = jnp.where(
            room[...] > jnp.where(second_lane, start[1], start[0]), vega, 0.0
        ).astype(BF16)
        columns = [
            jnp.concatenate([jr[q, k], jb[RING * q + k]], axis=1) for q, k in both_
        ]
        acc[...] += jnp.dot(
            masked, jnp.concatenate(columns, axis=0), preferred_element_type=F32
        )

    def landed(q, k, h, n):
        ref = xf.at[q, k, h * pad : (h + 1) * pad]
        rdma(ref, ref, ss_a1.at[q, n], rs_a1.at[q, n], sibling).wait_recv()

    def ring_place(q, step):
        return lax.rem(jnp.where(lax.rem(q, 2) == 0, x, y) + step, RING)

    j_finish()

    pair((0, x), (1, y))
    ring[2].forward()
    ring[3].forward()
    pair((2, x), (3, y))

    @pl.loop(0, RING)
    def _(q):
        nl, nr = ring_place(q, 3), ring_place(q, 1)
        landed(q, nl, 1, 2)
        landed(q, nr, 0, 3)
        pair((q, nl), (q, nr))

    far_x, far_y = ring[0].far, ring[1].far

    @pl.loop(0, 2)
    def _(g):
        for q, k in ((2 * g, far_x), (2 * g + 1, far_y)):
            landed(q, k, 0, 4)
            landed(q, k, 1, 5)
        pair((2 * g, far_x), (2 * g + 1, far_y))

    rows_c = pl.ds(pl.multiple_of(c * (trades // 2), 8), trades // 2)
    rows_sib = pl.ds(pl.multiple_of(sib * (trades // 2), 8), trades // 2)
    swap = (acc.at[rows_sib], pr, ss_p.at[0], rs_p.at[0], sibling)
    send(*swap)
    strip_rows = out.shape[0]
    rdma(*swap).wait_recv()
    total = acc[rows_c] + pr[...]
    po[...] = jnp.concatenate(
        [total[:, s * LANE : (s + 1) * LANE].reshape(CHIPS, strip_rows, LANE) for s in (0, 1)], axis=1
    ).astype(BF16)

    tile = ob.at[z * RING + x]

    def deliver(n, dst):
        rdma(po.at[n], tile, ss_o.at[0], rs_o.at[0], {"grp": y, "path": dst}).start()

    for k in (4, 3, 5, 2, 6, 1, 7, 0):
        zz = lax.rem(z + k, DEPTH)
        for side in (0, 1):
            for u in (0, 1):
                n = side * 2 * DEPTH + 2 * zz + u
                dst = c * CHIPS + n
                if k:
                    deliver(n, dst)
                else:
                    pl.when(dst != me)(lambda n=n, dst=dst: deliver(n, dst))

                    @pl.when(dst == me)
                    def _():
                        pltpu.make_async_copy(po.at[n], tile, rs_o.at[0]).start()

    for cond, d in sent:
        if cond is None:
            d.wait_send()
        else:
            pl.when(cond)(d.wait_send)

    def j_crossed(e):
        for k in (1, 2, 3):
            rdma(*j_cross(e, k)).wait_send()

        @pl.when(core != c)
        def _():
            rdma(*j_cross(e, 0)).wait_send()

    both(j_crossed)

    @pl.when(turn)
    def _():
        for k in range(1, DEPTH):
            rdma(*j_line(k)).wait_send()

    pltpu.make_async_copy(ob, ob, rs_o.at[0]).wait()

    rest = []
    for t in range(CHIPS):
        tile = ob[t].astype(F32)
        out[:, t * LANE : (t + 1) * LANE] = tile[0:strip_rows]
        rest.append(tile[strip_rows : 2 * strip_rows, 0:more])
    out[:, main:params] = jnp.concatenate(rest, axis=1)

    def po_sent(n):
        rdma(po.at[0:n], po.at[0:n], ss_o.at[0], rs_o.at[0], sibling).wait_send()

    pl.when(core == c)(lambda: po_sent(CHIPS - 1))
    pl.when(core != c)(lambda: po_sent(CHIPS))


def per_device(
    path_sens, discounts, cash_flows, flow_index, exercise_step, trade_steps, jacobian_inv
):
    paths_own, params = path_sens.shape
    trades = cash_flows.shape[0]
    jrows = jacobian_inv.shape[0]
    strip = trades // PATHS
    rest = params - CHIPS * LANE
    pad = -(-jrows // 16) * 16
    half = params // 2
    slots = cash_flows.shape[1]
    part = pad // 2
    share = 16
    vm = pltpu.VMEM
    dma = pltpu.SemaphoreType.DMA
    scratch = [
        vm((paths_own, LANE), BF16),
        vm((slots, trades), F32),
        vm((slots, trades), jnp.int32),
        vm((1, trades), jnp.int32),
        vm((1, trades), jnp.int32),
        vm((half, paths_own), BF16),
        vm((half, paths_own), BF16),
        vm((paths_own, LANE), BF16),
        vm((half + 8, LANE), F32),
        vm((RING, RING, 2 * pad, LANE), F32),
        vm((RING, 6, pad, LANE), F32),
        vm((RING, 2 * pad, LANE), F32),
        vm((RING, RING, part, LANE), F32),
        vm((2, 2 * part, LANE), F32),
        vm((2, DEPTH, share, LANE), F32),
        vm((2, share, LANE), F32),
        vm((2, 2 * part, LANE), F32),
        vm((RING, RING, 2 * pad, LANE), F32),
        vm((jrows, params), BF16),
        vm((pad, -(-rest // LANE) * LANE), F32),
        vm((DEPTH, RING, pad + GROUP, LANE), BF16),
        vm((2, RING, pad + GROUP, LANE), BF16),
        vm((RING, RING, 2 * pad, LANE), BF16),
        vm((RING, RING, 2, GROUP, LANE), BF16),
        vm((RING * RING, 2 * pad, LANE), BF16),
        vm((trades, 3 * LANE), BF16),
        vm((trades, 4 * pad), jnp.int32),
        vm((trades, 2 * LANE), F32),
        vm((trades // 2, 2 * LANE), F32),
        vm((CHIPS, 2 * strip, LANE), BF16),
        vm((CHIPS, 2 * strip, LANE), BF16),
        dma((RING + 1,)), dma((RING + 1,)), dma((7,)),
        dma((RING, 6)), dma((RING, 6)),
        dma((RING, RING)), dma((RING,)),
        dma((2, DEPTH)), dma((2,)),
        dma((2, DEPTH)), dma((2,)),
        dma((RING, RING)), dma((RING,)),
        dma((RING, 6)), dma((RING, 6)),
        dma((DEPTH,)), dma((2, RING)), dma((3, 2)),
        dma((2, 6)), dma((2, 6)),
        dma((2,)), dma((2,)),
        dma((1,)), dma((1,)),
        pltpu.SemaphoreType.REGULAR((2,)),
    ]
    vmem = pl.BlockSpec(memory_space=pltpu.VMEM)
    hbm = pl.BlockSpec(memory_space=pl.ANY)
    return pl.pallas_call(
        kernel,
        out_shape=jax.ShapeDtypeStruct((strip, params), F32),
        in_specs=[hbm] * 7,
        out_specs=vmem,
        scratch_shapes=scratch,
        compiler_params=pltpu.CompilerParams(
            collective_id=0, has_side_effects=True, vmem_limit_bytes=56 * 1024 * 1024
        ),
    )(
        discounts,
        path_sens.T,
        cash_flows.T,
        flow_index.T,
        exercise_step.reshape(1, trades),
        trade_steps.reshape(1, trades),
        jacobian_inv,
    )


def solution(mesh):
    placed = (
        P(("grp", "path"), None),
        P(("grp", "path"), None),
        P("grp", None),
        P("grp", None),
        P("grp"),
        P("grp"),
        P("path", None),
    )
    return jax.shard_map(
        per_device, mesh=mesh, in_specs=placed, out_specs=P(("grp", "path"), None), check_vma=False
    )
```

```python
import jax
import jax.numpy as jnp
from jax import lax
from jax.experimental import pallas as pl
from jax.experimental.pallas import tpu as pltpu
from jax.sharding import PartitionSpec as P

NB = 40
LANE = 128
RING = 4
DEPTH = 8
CHIPS = RING * DEPTH
PATHS = 2 * CHIPS
GROUP = 16
F32 = jnp.float32
BF16 = jnp.bfloat16
MESH = pl.DeviceIdType.MESH


def kernel(
    disc, sens, cash, index, exer, steps, jac, out,
    dv, cv, iv, ev, sv, s_own, s_in, d_in, xs, xp, r1, y2, r2, zb, rz, zr, zf, xf,
    jv, je, jp, jz, jr, jx, jb, wt, room, mk, acc, pr, po, ob,
    ss_s, rs_s, ls, ss_1, rs_1, ss_2, rs_2, ss_z, rs_z, ss_g, rs_g,
    ss_a2, rs_a2, ss_a1, rs_a1, ss_j, ss_jx, rs_j, ss_ja, rs_ja, ss_p, rs_p, ss_o, rs_o, near_z,
):
    y = lax.axis_index("grp")
    me = lax.axis_index("path")
    j = lax.div(me, 2)
    c = lax.rem(me, 2)
    x = lax.div(j, DEPTH)
    z = lax.rem(j, DEPTH)
    sib = 1 - c
    params = sens.shape[0]
    width = params // NB
    half = params // 2
    jrows = jac.shape[0]
    pad = xp.shape[2] // 2
    trades = cash.shape[1]

    def at_chip(xx, zz, cc):
        return {"grp": y, "path": (xx * DEPTH + zz) * 2 + cc}

    def rdma(src, dst, ss, rs, dev):
        return pltpu.make_async_remote_copy(
            src_ref=src, dst_ref=dst, send_sem=ss, recv_sem=rs, device_id=dev, device_id_type=MESH
        )

    sent = []

    def send(*args):
        d = rdma(*args)
        d.start()
        sent.append((None, d))

    def send_if(cond, *args):
        d = rdma(*args)

        @pl.when(cond)
        def _():
            d.start()

        sent.append((cond, d))

    sibling = at_chip(x, z, sib)

    def on_x(k):
        return at_chip(lax.rem(x + k, RING), z, c)

    def on_y(k):
        return {"grp": lax.rem(y + k, RING), "path": me}

    def on_z(k):
        return at_chip(x, lax.rem(z + k, DEPTH), c)

    lines = ((x, on_x), (y, on_y))

    barrier = pltpu.get_barrier_semaphore()
    partners = [sibling] + [on(k) for on in (on_x, on_y) for k in (1, RING - 1)]
    partners += [on_z(k) for k in (1, DEPTH - 1, 2, DEPTH - 2)]
    for d in partners:
        pl.semaphore_signal(barrier, inc=1, device_id=d, device_id_type=MESH)

    fetched = [
        pltpu.make_async_copy(src, dst, ls.at[n])
        for n, (src, dst) in enumerate(
            (
                (disc, dv),
                (sens.at[pl.ds(pl.multiple_of(c * half, 16), half)], s_own),
                (cash, cv), (index, iv), (exer, ev), (steps, sv), (jac, jv),
            )
        )
    ]
    for f in fetched:
        f.start()

    first_cut = (half // 4 // 16 + 1) * 16
    cuts = (0, first_cut, half // 2, half // 2 + first_cut, half)

    def s_copy(q):
        n = cuts[q + 1] - cuts[q]
        return (
            sens.at[pl.ds(pl.multiple_of(sib * half + cuts[q], 16), n)],
            s_in.at[pl.ds(cuts[q], n)], ss_s.at[q], rs_s.at[q], sibling,
        )

    d_copy = (disc, d_in, ss_s.at[RING], rs_s.at[RING], sibling)

    xs[half : half + 8] = jnp.zeros((8, LANE), F32)
    for f in fetched[:2]:
        f.wait()
    third = half // 3

    @pl.loop(0, 3)
    def _(n):
        rws = pl.ds(pl.multiple_of(n * third, 16), third)
        xs[rws] = jnp.dot(s_own[rws], dv[...], preferred_element_type=F32)

    pl.semaphore_wait(barrier, len(partners))
    send(*d_copy)
    for q in range(RING):
        send(*s_copy(q))
    for n, k in enumerate((2, DEPTH - 2)):
        pl.semaphore_signal(near_z.at[n], inc=1, device_id=on_z(k), device_id_type=MESH)

    main = CHIPS * LANE
    more = (params - main) // CHIPS
    groups = pad // GROUP
    turn = lax.rem(z, RING) == y
    core = lax.div(x, 2)
    high = lax.div(z, RING)
    for f in fetched[2:]:
        f.wait()

    @pl.when(turn)
    def _():
        jp[...] = jnp.zeros(jp.shape, BF16)

        @pl.loop(0, DEPTH)
        def _(zz):
            for t in range(RING):
                col = pl.multiple_of((zz * RING + t) * LANE, LANE)
                jp[zz, t, 0:jrows] = jv[:, pl.ds(col, LANE)]

        je[...] = jnp.zeros(je.shape, F32)
        je[0:jrows, 0 : params - main] = jv[:, main:params].astype(F32)
        for t in range(CHIPS):
            packed = [
                je[r * GROUP : (r + 1) * GROUP, t * more : (t + 1) * more] for r in range(groups)
            ]
            packed.append(jnp.zeros((GROUP, LANE - groups * more), F32))
            jp[t // RING, t % RING, pad : pad + GROUP] = jnp.concatenate(packed, axis=1).astype(BF16)

        pltpu.make_async_copy(jp.at[z], jz.at[high], rs_j.at[2, high]).start()

    def j_line(k):
        zz = lax.rem(z + k, DEPTH)
        return jp.at[zz], jz.at[high], ss_j.at[k], rs_j.at[2, high], on_z(k)

    def j_depth(*steps_):
        @pl.when(turn)
        def _():
            for k in steps_:
                rdma(*j_line(k)).start()

    j_depth(2, 6, 1, 7)

    def part_rows(n, size):
        return pl.ds(pl.multiple_of(n * size, 8), size)

    class Scatter:
        def __init__(self, q):
            self.q = q
            self.i, self.on = lines[q % 2]
            self.nr, self.far, self.nl = (lax.rem(self.i + k, RING) for k in (1, 2, 3))
            self.right, self.left = self.on(1), self.on(3)

        def msg(self, n, h, k, dev):
            q = self.q
            return (
                xp.at[q, k, h * pad : (h + 1) * pad], r1.at[q, n],
                ss_1.at[q, n], rs_1.at[q, n], dev,
            )

        def first(self):
            send(*self.msg(0, 0, self.far, self.right))
            send(*self.msg(2, 1, self.far, self.left))
            send(*self.msg(3, 1, self.nr, self.right))
            send(*self.msg(1, 0, self.nl, self.left))

        def second(self):
            for h, n, k, dev in ((0, 0, self.nr, self.right), (1, 2, self.nl, self.left)):
                rdma(*self.msg(n, h, k, dev)).wait_recv()
                xp[self.q, k, h * pad : (h + 1) * pad] += r1[self.q, n]
                send(*self.msg(4 + h, h, k, dev))

        def result(self):
            for h, n in ((0, 1), (1, 3)):
                rdma(*self.msg(n, h, self.i, self.left)).wait_recv()
                rdma(*self.msg(4 + h, h, self.i, self.left)).wait_recv()
                rws = slice(h * pad, (h + 1) * pad)
                y2[self.q, rws] = xp[self.q, self.i, rws] + r1[self.q, n] + r1[self.q, 4 + h]

    one = [Scatter(q) for q in range(RING)]
    rdma(*d_copy).wait_recv()
    for q in range(RING):
        rdma(*s_copy(q)).wait_recv()
        xs[cuts[q] : cuts[q + 1]] += jnp.dot(
            s_in[cuts[q] : cuts[q + 1]], d_in[...], preferred_element_type=F32
        )
        for k in range(RING):
            for u in (0, 1):
                top = (8 * q + 2 * k + u) * jrows
                xp[q, k, u * pad : (u + 1) * pad] = xs[top : top + pad]
        one[q].first()

    for n in (0, 1):
        pl.semaphore_wait(near_z.at[n], 1)
    j_depth(4, 3, 5)
    one[0].second()
    one[1].second()
    one[2].second()
    one[3].second()

    def j_cross(e, k):
        xx = lax.rem(x + k, RING)
        two_ = pl.ds(2 * lax.rem(x, 2), 2)
        if e == 0:
            src = jz.at[:, xx, 0:pad]
            dst = jr.at[two_, y, pl.ds(pl.multiple_of(c * pad, 16), pad)]
        else:
            src = jz.at[:, xx, pad : pad + GROUP]
            dst = jx.at[two_, y, c]
        return src, dst, ss_jx.at[e, k], rs_j.at[e, 0], at_chip(xx, z, core)

    def both(f):
        f(0)
        f(1)

    def j_send(e):
        for k in (1, 3):
            rdma(*j_cross(e, k)).start()
        src, dst, ss, rs, dev = j_cross(e, 0)

        @pl.when(core == c)
        def _():
            pltpu.make_async_copy(src, dst, rs).start()

        @pl.when(core != c)
        def _():
            rdma(src, dst, ss, rs, dev).start()

    for n in (0, 1):
        pltpu.make_async_copy(jp.at[0], jz.at[n], rs_j.at[2, n]).wait()
    both(j_send)

    slots = cash.shape[0]
    forwards = lax.broadcasted_iota(jnp.int32, (LANE, trades), 0)
    late = forwards >= ev[...]
    weights = jnp.zeros((LANE, trades), F32)
    for s in range(slots):
        weights += jnp.where(late & (iv[s : s + 1] == forwards), cv[s : s + 1], 0.0)
    weights = weights * (1.0 / (disc.shape[0] * PATHS * RING))
    weights = weights.T
    w_hi = weights.astype(BF16)
    w_lo = (weights - w_hi.astype(F32)).astype(BF16)
    wt[...] = jnp.concatenate([w_hi, w_hi, w_lo], axis=1)
    reach = jnp.broadcast_to((sv[...] * width).astype(F32), (LANE, trades)).T.astype(jnp.int32)
    span = 4 * pad
    lane = lax.broadcasted_iota(jnp.int32, (trades, span), 1)
    lane = lane - jnp.where(lane >= 2 * pad, 2 * pad, 0)
    room[...] = (
        jnp.concatenate([reach] * (span // LANE) + [reach[:, : span % LANE]], axis=1)
        - lane + jnp.where(lane >= pad, pad - jrows, 0) - c * half
    )

    part = y2.shape[1] // RING

    def two(q, k):
        i, on = lines[1 - q % 2]
        return (
            y2.at[q, part_rows(lax.rem(i + k, RING), part)], r2.at[q, i],
            ss_2.at[q, k], rs_2.at[q], on(k),
        )

    for g in (0, 1):
        for q in (2 * g, 2 * g + 1):
            one[q].result()
            for k in (2, 1, 3):
                send(*two(q, k))
    both(lambda e: rdma(*j_cross(e, 2)).start())

    share = zr.shape[1]
    count = zb.shape[1] // share
    spread = (4, 3, 5, 2, 6, 1, 7)

    def turn_of(g, d):
        return lax.rem(d + count, DEPTH)

    def reduces(g):
        return turn_of(g, z) < count

    def z_piece(g, d):
        return part_rows(jnp.minimum(turn_of(g, d), count - 1), share)

    for g in (0, 1):
        for p in (0, 1):
            q = 2 * g + p
            i, on = lines[1 - p]
            total = y2[q, part_rows(i, part)]
            three = r2.at[q, 0 : RING - 1]
            rdma(three, three, ss_2.at[q, 0], rs_2.at[q], sibling).wait_recv()
            for k in (1, 2, 3):
                total += r2[q, lax.rem(i + k, RING)]
            zb[g, p * part : (p + 1) * part] = total
        zb[g, 2 * part :] = jnp.zeros((zb.shape[1] - 2 * part, LANE), F32)
        for k in spread:
            d = lax.rem(z + k, DEPTH)
            send_if(
                turn_of(g, d) < count,
                zb.at[g, z_piece(g, d)], rz.at[g, z], ss_z.at[g, k], rs_z.at[g], on_z(k),
            )


    def j_ring(half_, k, n, dev):
        ref = jr.at[pl.ds(2 * half_, 2), k]
        return ref, ref, ss_ja.at[0, n], rs_ja.at[0, n], dev

    def j_fan(k):
        ref = jx.at[:, y]
        return ref, ref, ss_ja.at[1, k], rs_ja.at[1, 0], on_y(k)

    yr, yl = on_y(1), on_y(3)
    ynr, yfar, ynl = (lax.rem(y + k, RING) for k in (1, 2, 3))

    def j_start():
        for e, whole in ((0, jr.at[:, y]), (1, jx.at[:, y])):
            pltpu.make_async_copy(whole, whole, rs_j.at[e, 0]).wait()
        for n, (hh, d) in enumerate(((0, yr), (1, yl), (1, yr), (0, yl))):
            send(*j_ring(hh, y, n, d))
        for k in (2, 1, 3):
            send(*j_fan(k))

    def j_forward():
        rdma(*j_ring(0, ynl, 0, yr)).wait_recv()
        send(*j_ring(0, ynl, 4, yr))
        rdma(*j_ring(1, ynr, 1, yl)).wait_recv()
        send(*j_ring(1, ynr, 5, yl))

    def j_finish():
        for hh, k, n, d in ((1, ynl, 2, yr), (0, ynr, 3, yl), (0, yfar, 4, yr), (1, yfar, 5, yl)):
            rdma(*j_ring(hh, k, n, d)).wait_recv()

    def j_unpack():
        three = jx.at[0 : RING - 1]
        rdma(three, three, ss_ja.at[1, 0], rs_ja.at[1, 0], sibling).wait_recv()

        @pl.loop(0, RING * RING)
        def _(n):
            q, k = lax.div(n, RING), lax.rem(n, RING)
            for u in (0, 1):
                tile = jx[q, k, u].astype(F32)
                for r in range(groups):
                    at = u * pad + r * GROUP
                    turned_ = tile if r == 0 else pltpu.roll(tile, LANE - r * more, 1)
                    jb[n, at : at + GROUP] = turned_.astype(BF16)

    j_start()

    for g in (0, 1):
        reducer = reduces(g)

        @pl.when(reducer)
        def _():
            total = zb[g, z_piece(g, z)]
            seven = rz.at[g, 0 : DEPTH - 1]
            rdma(seven, seven, ss_z.at[g, 0], rs_z.at[g], sibling).wait_recv()
            for k in range(1, DEPTH):
                total += rz[g, lax.rem(z + k, DEPTH)]
            zr[g] = total
            zf[g, z_piece(g, z)] = total

        for k in spread:
            send_if(
                reducer, zr.at[g], zf.at[g, z_piece(g, z)], ss_g.at[g, k], rs_g.at[g], on_z(k)
            )

    j_forward()

    def home(q, i):
        return xf.at[q, lines[q % 2][0], part_rows(i, part)]

    for g in (0, 1):
        for some, ref in ((reduces(g), zf.at[g, 0 : (count - 1) * share]), (~reduces(g), zf.at[g])):

            @pl.when(some)
            def _():
                rdma(ref, ref, ss_g.at[g, 0], rs_g.at[g], sibling).wait_recv()

        for p in (0, 1):
            q = 2 * g + p
            i, on = lines[1 - p]
            mine = zf.at[g, p * part : (p + 1) * part]
            for k in (2, 1, 3):
                send(mine, home(q, i), ss_a2.at[q, k], rs_a2.at[q], on(k))
            home(q, i)[...] = mine[...]

    def all_left():
        while sent:
            cond, d = sent.pop()
            if cond is None:
                d.wait_send()
            else:
                pl.when(cond)(d.wait_send)

    later = sent[-4 * (RING - 1) - 2:]
    del sent[-len(later) :]
    all_left()
    sent.extend(later)
    j_unpack()

    class Gather:
        def __init__(self, q):
            self.q = q
            self.i, self.on = lines[q % 2]
            self.nr, self.far, self.nl = (lax.rem(self.i + k, RING) for k in (1, 2, 3))
            self.right, self.left = self.on(1), self.on(3)

        def msg(self, n, h, k, dev):
            ref = xf.at[self.q, k, h * pad : (h + 1) * pad]
            return ref, ref, ss_a1.at[self.q, n], rs_a1.at[self.q, n], dev

        def start(self):
            q = self.q
            three = xf.at[q, 0, 0 : (RING - 1) * part]
            rdma(three, three, ss_a2.at[q, 0], rs_a2.at[q], sibling).wait_recv()
            send(*self.msg(0, 0, self.i, self.right))
            send(*self.msg(1, 1, self.i, self.left))
            send(*self.msg(2, 1, self.i, self.right))
            send(*self.msg(3, 0, self.i, self.left))

        def forward(self):
            rdma(*self.msg(0, 0, self.nl, self.right)).wait_recv()
            send(*self.msg(4, 0, self.nl, self.right))
            rdma(*self.msg(1, 1, self.nr, self.left)).wait_recv()
            send(*self.msg(5, 1, self.nr, self.left))

    ring = [Gather(q) for q in range(RING)]
    for q in range(RING):
        ring[q].start()

    acc[...] = jnp.zeros(acc.shape, F32)

    second_lane = lax.broadcasted_iota(jnp.int32, (1, span), 1) >= 2 * pad

    def mask(*both_):
        values = jnp.concatenate([xf[q, k] for q, k in both_], axis=0)
        hi = values.astype(BF16)
        lo = (values - hi.astype(F32)).astype(BF16)
        vega = lax.dot_general(
            wt[...], jnp.concatenate([hi, lo, hi], axis=1), (((1,), (1,)), ((), ())),
            preferred_element_type=F32,
        )
        start = [(8 * q + 2 * k) * jrows for q, k in both_]
        keep = room[...] > jnp.where(second_lane, start[1], start[0])
        return jnp.where(keep, vega, 0.0).astype(BF16)

    def add(masked, *both_):
        columns = [
            jnp.concatenate([jr[q, k], jb[RING * q + k]], axis=1) for q, k in both_
        ]
        acc[...] += jnp.dot(
            masked, jnp.concatenate(columns, axis=0), preferred_element_type=F32
        )

    def pair(*both_):
        add(mask(*both_), *both_)

    def landed(q, k, h, n):
        ref = xf.at[q, k, h * pad : (h + 1) * pad]
        rdma(ref, ref, ss_a1.at[q, n], rs_a1.at[q, n], sibling).wait_recv()

    def ring_place(q, step):
        return lax.rem(jnp.where(lax.rem(q, 2) == 0, x, y) + step, RING)

    mine = lambda g: ((2 * g, x), (2 * g + 1, y))

    @pl.loop(0, 2)
    def _(g):
        mk[g] = mask(*mine(g))

    for r in ring:
        r.forward()
    j_finish()

    @pl.loop(0, 2)
    def _(g):
        add(mk[g], *mine(g))

    @pl.loop(0, RING)
    def _(q):
        nl, nr = ring_place(q, 3), ring_place(q, 1)
        landed(q, nl, 1, 2)
        landed(q, nr, 0, 3)
        pair((q, nl), (q, nr))

    far_x, far_y = ring[0].far, ring[1].far

    @pl.loop(0, 2)
    def _(g):
        for q, k in ((2 * g, far_x), (2 * g + 1, far_y)):
            landed(q, k, 0, 4)
            landed(q, k, 1, 5)
        pair((2 * g, far_x), (2 * g + 1, far_y))

    rows_c = pl.ds(pl.multiple_of(c * (trades // 2), 8), trades // 2)
    rows_sib = pl.ds(pl.multiple_of(sib * (trades // 2), 8), trades // 2)
    swap = (acc.at[rows_sib], pr, ss_p.at[0], rs_p.at[0], sibling)
    send(*swap)
    strip_rows = out.shape[0]
    rdma(*swap).wait_recv()
    total = acc[rows_c] + pr[...]
    po[...] = jnp.concatenate(
        [total[:, s * LANE : (s + 1) * LANE].reshape(CHIPS, strip_rows, LANE) for s in (0, 1)], axis=1
    ).astype(BF16)

    tile = ob.at[z * RING + x]

    def deliver(n, dst):
        rdma(po.at[n], tile, ss_o.at[0], rs_o.at[0], {"grp": y, "path": dst}).start()

    for k in (4, 3, 5, 2, 6, 1, 7, 0):
        zz = lax.rem(z + k, DEPTH)
        for side in (0, 1):
            for u in (0, 1):
                n = side * 2 * DEPTH + 2 * zz + u
                dst = c * CHIPS + n
                if k:
                    deliver(n, dst)
                else:
                    pl.when(dst != me)(lambda n=n, dst=dst: deliver(n, dst))

                    @pl.when(dst == me)
                    def _():
                        pltpu.make_async_copy(po.at[n], tile, rs_o.at[0]).start()

    all_left()

    def j_crossed(e):
        for k in (1, 2, 3):
            rdma(*j_cross(e, k)).wait_send()

        @pl.when(core != c)
        def _():
            rdma(*j_cross(e, 0)).wait_send()

    both(j_crossed)

    @pl.when(turn)
    def _():
        for k in range(1, DEPTH):
            rdma(*j_line(k)).wait_send()

    pltpu.make_async_copy(ob, ob, rs_o.at[0]).wait()

    rest = []
    for t in range(CHIPS):
        tile = ob[t].astype(F32)
        out[:, t * LANE : (t + 1) * LANE] = tile[0:strip_rows]
        rest.append(tile[strip_rows : 2 * strip_rows, 0:more])
    out[:, main:params] = jnp.concatenate(rest, axis=1)

    def po_sent(n):
        rdma(po.at[0:n], po.at[0:n], ss_o.at[0], rs_o.at[0], sibling).wait_send()

    pl.when(core == c)(lambda: po_sent(CHIPS - 1))
    pl.when(core != c)(lambda: po_sent(CHIPS))


def per_device(
    path_sens, discounts, cash_flows, flow_index, exercise_step, trade_steps, jacobian_inv
):
    paths_own, params = path_sens.shape
    trades = cash_flows.shape[0]
    jrows = jacobian_inv.shape[0]
    strip = trades // PATHS
    rest = params - CHIPS * LANE
    pad = -(-jrows // 16) * 16
    half = params // 2
    slots = cash_flows.shape[1]
    part = pad // 2
    share = 24
    vm = pltpu.VMEM
    dma = pltpu.SemaphoreType.DMA
    scratch = [
        vm((paths_own, LANE), BF16),
        vm((slots, trades), F32),
        vm((slots, trades), jnp.int32),
        vm((1, trades), jnp.int32),
        vm((1, trades), jnp.int32),
        vm((half, paths_own), BF16),
        vm((half, paths_own), BF16),
        vm((paths_own, LANE), BF16),
        vm((half + 8, LANE), F32),
        vm((RING, RING, 2 * pad, LANE), F32),
        vm((RING, 6, pad, LANE), F32),
        vm((RING, 2 * pad, LANE), F32),
        vm((RING, RING, part, LANE), F32),
        vm((2, RING * share, LANE), F32),
        vm((2, DEPTH, share, LANE), F32),
        vm((2, share, LANE), F32),
        vm((2, RING * share, LANE), F32),
        vm((RING, RING, 2 * pad, LANE), F32),
        vm((jrows, params), BF16),
        vm((pad, -(-rest // LANE) * LANE), F32),
        vm((DEPTH, RING, pad + GROUP, LANE), BF16),
        vm((2, RING, pad + GROUP, LANE), BF16),
        vm((RING, RING, 2 * pad, LANE), BF16),
        vm((RING, RING, 2, GROUP, LANE), BF16),
        vm((RING * RING, 2 * pad, LANE), BF16),
        vm((trades, 3 * LANE), BF16),
        vm((trades, 4 * pad), jnp.int32),
        vm((2, trades, 4 * pad), BF16),
        vm((trades, 2 * LANE), F32),
        vm((trades // 2, 2 * LANE), F32),
        vm((CHIPS, 2 * strip, LANE), BF16),
        vm((CHIPS, 2 * strip, LANE), BF16),
        dma((RING + 1,)), dma((RING + 1,)), dma((7,)),
        dma((RING, 6)), dma((RING, 6)),
        dma((RING, RING)), dma((RING,)),
        dma((2, DEPTH)), dma((2,)),
        dma((2, DEPTH)), dma((2,)),
        dma((RING, RING)), dma((RING,)),
        dma((RING, 6)), dma((RING, 6)),
        dma((DEPTH,)), dma((2, RING)), dma((3, 2)),
        dma((2, 6)), dma((2, 6)),
        dma((2,)), dma((2,)),
        dma((1,)), dma((1,)),
        pltpu.SemaphoreType.REGULAR((2,)),
    ]
    vmem = pl.BlockSpec(memory_space=pltpu.VMEM)
    hbm = pl.BlockSpec(memory_space=pl.ANY)
    return pl.pallas_call(
        kernel,
        out_shape=jax.ShapeDtypeStruct((strip, params), F32),
        in_specs=[hbm] * 7,
        out_specs=vmem,
        scratch_shapes=scratch,
        compiler_params=pltpu.CompilerParams(
            collective_id=0, has_side_effects=True, vmem_limit_bytes=56 * 1024 * 1024
        ),
    )(
        discounts,
        path_sens.T,
        cash_flows.T,
        flow_index.T,
        exercise_step.reshape(1, trades),
        trade_steps.reshape(1, trades),
        jacobian_inv,
    )


def solution(mesh):
    placed = (
        P(("grp", "path"), None),
        P(("grp", "path"), None),
        P("grp", None),
        P("grp", None),
        P("grp"),
        P("grp"),
        P("path", None),
    )
    return jax.shard_map(
        per_device, mesh=mesh, in_specs=placed, out_specs=P(("grp", "path"), None), check_vma=False
    )
```

```python
import jax
import jax.numpy as jnp
from jax import lax
from jax.experimental import pallas as pl
from jax.experimental.pallas import tpu as pltpu
from jax.sharding import PartitionSpec as P

NB = 40
LANE = 128
RING = 4
DEPTH = 8
CHIPS = RING * DEPTH
PATHS = 2 * CHIPS
GROUP = 16
F32 = jnp.float32
BF16 = jnp.bfloat16
MESH = pl.DeviceIdType.MESH


def kernel(
    disc, sens, cash, index, exer, steps, jac, out,
    dv, cv, iv, ev, sv, s_own, s_in, d_in, xs, xp, r1, y2, r2, zb, rz, zr, zf, xf,
    jv, je, jp, jz, jr, jx, jb, wt, room, mk, acc, pr, po, ob,
    ss_s, rs_s, ls, ss_1, rs_1, ss_2, rs_2, ss_z, rs_z, ss_g, rs_g,
    ss_a2, rs_a2, ss_a1, rs_a1, ss_j, ss_jx, rs_j, ss_ja, rs_ja, ss_p, rs_p, ss_o, rs_o, near_z,
):
    y = lax.axis_index("grp")
    me = lax.axis_index("path")
    j = lax.div(me, 2)
    c = lax.rem(me, 2)
    x = lax.div(j, DEPTH)
    z = lax.rem(j, DEPTH)
    sib = 1 - c
    params = sens.shape[0]
    width = params // NB
    half = params // 2
    jrows = jac.shape[0]
    pad = xp.shape[2] // 2
    trades = cash.shape[1]

    def at_chip(xx, zz, cc):
        return {"grp": y, "path": (xx * DEPTH + zz) * 2 + cc}

    def rdma(src, dst, ss, rs, dev):
        return pltpu.make_async_remote_copy(
            src_ref=src, dst_ref=dst, send_sem=ss, recv_sem=rs, device_id=dev, device_id_type=MESH
        )

    sent = []

    def send(*args):
        d = rdma(*args)
        d.start()
        sent.append((None, d))

    def send_if(cond, *args):
        d = rdma(*args)

        @pl.when(cond)
        def _():
            d.start()

        sent.append((cond, d))

    sibling = at_chip(x, z, sib)

    def on_x(k):
        return at_chip(lax.rem(x + k, RING), z, c)

    def on_y(k):
        return {"grp": lax.rem(y + k, RING), "path": me}

    def on_z(k):
        return at_chip(x, lax.rem(z + k, DEPTH), c)

    lines = ((x, on_x), (y, on_y))

    barrier = pltpu.get_barrier_semaphore()
    partners = [sibling] + [on(k) for on in (on_x, on_y) for k in (1, RING - 1)]
    partners += [on_z(k) for k in (1, DEPTH - 1, 2, DEPTH - 2)]
    for d in partners:
        pl.semaphore_signal(barrier, inc=1, device_id=d, device_id_type=MESH)

    fetched = [
        pltpu.make_async_copy(src, dst, ls.at[n])
        for n, (src, dst) in enumerate(
            (
                (disc, dv),
                (sens.at[pl.ds(pl.multiple_of(c * half, 16), half)], s_own),
                (cash, cv), (index, iv), (exer, ev), (steps, sv), (jac, jv),
            )
        )
    ]
    for f in fetched:
        f.start()

    first_cut = (half // 4 // 16 + 1) * 16
    cuts = (0, first_cut, half // 2, half // 2 + first_cut, half)

    def s_copy(q):
        n = cuts[q + 1] - cuts[q]
        return (
            sens.at[pl.ds(pl.multiple_of(sib * half + cuts[q], 16), n)],
            s_in.at[pl.ds(cuts[q], n)], ss_s.at[q], rs_s.at[q], sibling,
        )

    d_copy = (disc, d_in, ss_s.at[RING], rs_s.at[RING], sibling)

    xs[half : half + 8] = jnp.zeros((8, LANE), F32)
    for f in fetched[:2]:
        f.wait()
    third = half // 3

    @pl.loop(0, 3)
    def _(n):
        rws = pl.ds(pl.multiple_of(n * third, 16), third)
        xs[rws] = jnp.dot(s_own[rws], dv[...], preferred_element_type=F32)

    pl.semaphore_wait(barrier, len(partners))
    send(*d_copy)
    for q in (0, 1):
        send(*s_copy(q))
    for n, k in enumerate((2, DEPTH - 2)):
        pl.semaphore_signal(near_z.at[n], inc=1, device_id=on_z(k), device_id_type=MESH)

    main = CHIPS * LANE
    more = (params - main) // CHIPS
    groups = pad // GROUP
    turn = lax.rem(z, RING) == y
    core = lax.div(x, 2)
    high = lax.div(z, RING)
    for f in fetched[2:]:
        f.wait()

    @pl.when(turn)
    def _():
        jp[...] = jnp.zeros(jp.shape, BF16)

        @pl.loop(0, DEPTH)
        def _(zz):
            for t in range(RING):
                col = pl.multiple_of((zz * RING + t) * LANE, LANE)
                jp[zz, t, 0:jrows] = jv[:, pl.ds(col, LANE)]

        je[...] = jnp.zeros(je.shape, F32)
        je[0:jrows, 0 : params - main] = jv[:, main:params].astype(F32)
        for t in range(CHIPS):
            packed = [
                je[r * GROUP : (r + 1) * GROUP, t * more : (t + 1) * more] for r in range(groups)
            ]
            packed.append(jnp.zeros((GROUP, LANE - groups * more), F32))
            jp[t // RING, t % RING, pad : pad + GROUP] = jnp.concatenate(packed, axis=1).astype(BF16)

        pltpu.make_async_copy(jp.at[z], jz.at[high], rs_j.at[2, high]).start()

    def j_line(k):
        zz = lax.rem(z + k, DEPTH)
        return jp.at[zz], jz.at[high], ss_j.at[k], rs_j.at[2, high], on_z(k)

    def j_depth(*steps_):
        @pl.when(turn)
        def _():
            for k in steps_:
                rdma(*j_line(k)).start()

    j_depth(2, 6, 1, 7)

    def part_rows(n, size):
        return pl.ds(pl.multiple_of(n * size, 8), size)

    class Scatter:
        def __init__(self, q):
            self.q = q
            self.i, self.on = lines[q % 2]
            self.nr, self.far, self.nl = (lax.rem(self.i + k, RING) for k in (1, 2, 3))
            self.right, self.left = self.on(1), self.on(3)

        def msg(self, n, h, k, dev):
            q = self.q
            return (
                xp.at[q, k, h * pad : (h + 1) * pad], r1.at[q, n],
                ss_1.at[q, n], rs_1.at[q, n], dev,
            )

        def first(self):
            send(*self.msg(0, 0, self.far, self.right))
            send(*self.msg(2, 1, self.far, self.left))

        def near(self):
            send(*self.msg(3, 1, self.nr, self.right))
            send(*self.msg(1, 0, self.nl, self.left))

        def second(self):
            for h, n, k, dev in ((0, 0, self.nr, self.right), (1, 2, self.nl, self.left)):
                rdma(*self.msg(n, h, k, dev)).wait_recv()
                xp[self.q, k, h * pad : (h + 1) * pad] += r1[self.q, n]
                send(*self.msg(4 + h, h, k, dev))

        def result(self):
            for h, n in ((0, 1), (1, 3)):
                rdma(*self.msg(n, h, self.i, self.left)).wait_recv()
                rdma(*self.msg(4 + h, h, self.i, self.left)).wait_recv()
                rws = slice(h * pad, (h + 1) * pad)
                y2[self.q, rws] = xp[self.q, self.i, rws] + r1[self.q, n] + r1[self.q, 4 + h]

    one = [Scatter(q) for q in range(RING)]
    rdma(*d_copy).wait_recv()
    for q in range(RING):
        rdma(*s_copy(q)).wait_recv()
        if q < 2:
            send(*s_copy(q + 2))
        xs[cuts[q] : cuts[q + 1]] += jnp.dot(
            s_in[cuts[q] : cuts[q + 1]], d_in[...], preferred_element_type=F32
        )
        for k in range(RING):
            for u in (0, 1):
                top = (8 * q + 2 * k + u) * jrows
                xp[q, k, u * pad : (u + 1) * pad] = xs[top : top + pad]
        one[q].first()
    for r in one:
        r.near()

    for n in (0, 1):
        pl.semaphore_wait(near_z.at[n], 1)
    j_depth(4, 3, 5)
    one[0].second()
    one[1].second()
    one[2].second()
    one[3].second()

    def j_cross(e, k):
        xx = lax.rem(x + k, RING)
        two_ = pl.ds(2 * lax.rem(x, 2), 2)
        if e == 0:
            src = jz.at[:, xx, 0:pad]
            dst = jr.at[two_, y, pl.ds(pl.multiple_of(c * pad, 16), pad)]
        else:
            src = jz.at[:, xx, pad : pad + GROUP]
            dst = jx.at[two_, y, c]
        return src, dst, ss_jx.at[e, k], rs_j.at[e, 0], at_chip(xx, z, core)

    def both(f):
        f(0)
        f(1)

    def j_send(e):
        for k in (1, 3):
            rdma(*j_cross(e, k)).start()
        src, dst, ss, rs, dev = j_cross(e, 0)

        @pl.when(core == c)
        def _():
            pltpu.make_async_copy(src, dst, rs).start()

        @pl.when(core != c)
        def _():
            rdma(src, dst, ss, rs, dev).start()

    for n in (0, 1):
        pltpu.make_async_copy(jp.at[0], jz.at[n], rs_j.at[2, n]).wait()
    both(j_send)

    slots = cash.shape[0]
    forwards = lax.broadcasted_iota(jnp.int32, (LANE, trades), 0)
    late = forwards >= ev[...]
    weights = jnp.zeros((LANE, trades), F32)
    for s in range(slots):
        weights += jnp.where(late & (iv[s : s + 1] == forwards), cv[s : s + 1], 0.0)
    weights = weights * (1.0 / (disc.shape[0] * PATHS * RING))
    weights = weights.T
    w_hi = weights.astype(BF16)
    w_lo = (weights - w_hi.astype(F32)).astype(BF16)
    wt[...] = jnp.concatenate([w_hi, w_hi, w_lo], axis=1)
    reach = jnp.broadcast_to((sv[...] * width).astype(F32), (LANE, trades)).T.astype(jnp.int32)
    span = 4 * pad
    lane = lax.broadcasted_iota(jnp.int32, (trades, span), 1)
    lane = lane - jnp.where(lane >= 2 * pad, 2 * pad, 0)
    room[...] = (
        jnp.concatenate([reach] * (span // LANE) + [reach[:, : span % LANE]], axis=1)
        - lane + jnp.where(lane >= pad, pad - jrows, 0) - c * half
    )

    part = y2.shape[1] // RING

    def two(q, k):
        i, on = lines[1 - q % 2]
        return (
            y2.at[q, part_rows(lax.rem(i + k, RING), part)], r2.at[q, i],
            ss_2.at[q, k], rs_2.at[q], on(k),
        )

    for g in (0, 1):
        for q in (2 * g, 2 * g + 1):
            one[q].result()
            for k in (2, 1, 3):
                send(*two(q, k))
    both(lambda e: rdma(*j_cross(e, 2)).start())

    share = zr.shape[1]
    count = 2 * part // share
    spread = (4, 3, 5, 2, 6, 1, 7)

    def turn_of(g, d):
        return lax.rem(d + count * g, DEPTH)

    def reduces(g):
        return turn_of(g, z) < count

    def z_piece(g, d):
        return part_rows(jnp.minimum(turn_of(g, d), count - 1), share)

    for g in (0, 1):
        for p in (0, 1):
            q = 2 * g + p
            i, on = lines[1 - p]
            total = y2[q, part_rows(i, part)]
            three = r2.at[q, 0 : RING - 1]
            rdma(three, three, ss_2.at[q, 0], rs_2.at[q], sibling).wait_recv()
            for k in (1, 2, 3):
                total += r2[q, lax.rem(i + k, RING)]
            zb[g, p * part : (p + 1) * part] = total
        for k in spread:
            d = lax.rem(z + k, DEPTH)
            send_if(
                turn_of(g, d) < count,
                zb.at[g, z_piece(g, d)], rz.at[g, z], ss_z.at[g, k], rs_z.at[g], on_z(k),
            )


    def j_ring(half_, k, n, dev):
        ref = jr.at[pl.ds(2 * half_, 2), k]
        return ref, ref, ss_ja.at[0, n], rs_ja.at[0, n], dev

    def j_fan(k):
        ref = jx.at[:, y]
        return ref, ref, ss_ja.at[1, k], rs_ja.at[1, 0], on_y(k)

    yr, yl = on_y(1), on_y(3)
    ynr, yfar, ynl = (lax.rem(y + k, RING) for k in (1, 2, 3))

    def j_start():
        for e, whole in ((0, jr.at[:, y]), (1, jx.at[:, y])):
            pltpu.make_async_copy(whole, whole, rs_j.at[e, 0]).wait()
        for n, (hh, d) in enumerate(((0, yr), (1, yl), (1, yr), (0, yl))):
            send(*j_ring(hh, y, n, d))
        for k in (2, 1, 3):
            send(*j_fan(k))

    def j_forward():
        rdma(*j_ring(0, ynl, 0, yr)).wait_recv()
        send(*j_ring(0, ynl, 4, yr))
        rdma(*j_ring(1, ynr, 1, yl)).wait_recv()
        send(*j_ring(1, ynr, 5, yl))

    def j_finish():
        for hh, k, n, d in ((1, ynl, 2, yr), (0, ynr, 3, yl), (0, yfar, 4, yr), (1, yfar, 5, yl)):
            rdma(*j_ring(hh, k, n, d)).wait_recv()

    def j_unpack():
        three = jx.at[0 : RING - 1]
        rdma(three, three, ss_ja.at[1, 0], rs_ja.at[1, 0], sibling).wait_recv()

        @pl.loop(0, RING * RING)
        def _(n):
            q, k = lax.div(n, RING), lax.rem(n, RING)
            for u in (0, 1):
                tile = jx[q, k, u].astype(F32)
                for r in range(groups):
                    at = u * pad + r * GROUP
                    turned_ = tile if r == 0 else pltpu.roll(tile, LANE - r * more, 1)
                    jb[n, at : at + GROUP] = turned_.astype(BF16)

    j_start()

    for g in (0, 1):
        reducer = reduces(g)

        @pl.when(reducer)
        def _():
            total = zb[g, z_piece(g, z)]
            seven = rz.at[g, 0 : DEPTH - 1]
            rdma(seven, seven, ss_z.at[g, 0], rs_z.at[g], sibling).wait_recv()
            for k in range(1, DEPTH):
                total += rz[g, lax.rem(z + k, DEPTH)]
            zr[g] = total
            zf[g, z_piece(g, z)] = total

        for k in spread:
            send_if(
                reducer, zr.at[g], zf.at[g, z_piece(g, z)], ss_g.at[g, k], rs_g.at[g], on_z(k)
            )

    j_forward()

    def home(q, i):
        return xf.at[q, lines[q % 2][0], part_rows(i, part)]

    for g in (0, 1):
        for some, ref in ((reduces(g), zf.at[g, 0 : (count - 1) * share]), (~reduces(g), zf.at[g])):

            @pl.when(some)
            def _():
                rdma(ref, ref, ss_g.at[g, 0], rs_g.at[g], sibling).wait_recv()

        for p in (0, 1):
            q = 2 * g + p
            i, on = lines[1 - p]
            mine = zf.at[g, p * part : (p + 1) * part]
            for k in (2, 1, 3):
                send(mine, home(q, i), ss_a2.at[q, k], rs_a2.at[q], on(k))
            home(q, i)[...] = mine[...]

    def all_left():
        while sent:
            cond, d = sent.pop()
            if cond is None:
                d.wait_send()
            else:
                pl.when(cond)(d.wait_send)

    later = sent[-4 * (RING - 1) - 2:]
    del sent[-len(later) :]
    all_left()
    sent.extend(later)
    j_unpack()

    class Gather:
        def __init__(self, q):
            self.q = q
            self.i, self.on = lines[q % 2]
            self.nr, self.far, self.nl = (lax.rem(self.i + k, RING) for k in (1, 2, 3))
            self.right, self.left = self.on(1), self.on(3)

        def msg(self, n, h, k, dev):
            ref = xf.at[self.q, k, h * pad : (h + 1) * pad]
            return ref, ref, ss_a1.at[self.q, n], rs_a1.at[self.q, n], dev

        def start(self):
            q = self.q
            three = xf.at[q, 0, 0 : (RING - 1) * part]
            rdma(three, three, ss_a2.at[q, 0], rs_a2.at[q], sibling).wait_recv()
            send(*self.msg(0, 0, self.i, self.right))
            send(*self.msg(1, 1, self.i, self.left))

        def rest(self):
            send(*self.msg(2, 1, self.i, self.right))
            send(*self.msg(3, 0, self.i, self.left))

        def forward(self):
            rdma(*self.msg(0, 0, self.nl, self.right)).wait_recv()
            send(*self.msg(4, 0, self.nl, self.right))
            rdma(*self.msg(1, 1, self.nr, self.left)).wait_recv()
            send(*self.msg(5, 1, self.nr, self.left))

    ring = [Gather(q) for q in range(RING)]
    for q in range(RING):
        ring[q].start()

    acc[...] = jnp.zeros(acc.shape, F32)

    second_lane = lax.broadcasted_iota(jnp.int32, (1, span), 1) >= 2 * pad

    def mask(*both_):
        values = jnp.concatenate([xf[q, k] for q, k in both_], axis=0)
        hi = values.astype(BF16)
        lo = (values - hi.astype(F32)).astype(BF16)
        vega = lax.dot_general(
            wt[...], jnp.concatenate([hi, lo, hi], axis=1), (((1,), (1,)), ((), ())),
            preferred_element_type=F32,
        )
        start = [(8 * q + 2 * k) * jrows for q, k in both_]
        keep = room[...] > jnp.where(second_lane, start[1], start[0])
        return jnp.where(keep, vega, 0.0).astype(BF16)

    def add(masked, *both_):
        columns = [
            jnp.concatenate([jr[q, k], jb[RING * q + k]], axis=1) for q, k in both_
        ]
        acc[...] += jnp.dot(
            masked, jnp.concatenate(columns, axis=0), preferred_element_type=F32
        )

    def pair(*both_):
        add(mask(*both_), *both_)

    def landed(q, k, h, n):
        ref = xf.at[q, k, h * pad : (h + 1) * pad]
        rdma(ref, ref, ss_a1.at[q, n], rs_a1.at[q, n], sibling).wait_recv()

    def ring_place(q, step):
        return lax.rem(jnp.where(lax.rem(q, 2) == 0, x, y) + step, RING)

    mine = lambda g: ((2 * g, x), (2 * g + 1, y))

    @pl.loop(0, 2)
    def _(g):
        mk[g] = mask(*mine(g))

    for r in ring:
        r.rest()
    for r in ring:
        r.forward()
    j_finish()

    @pl.loop(0, 2)
    def _(g):
        add(mk[g], *mine(g))

    @pl.loop(0, RING)
    def _(q):
        nl, nr = ring_place(q, 3), ring_place(q, 1)
        landed(q, nl, 1, 2)
        landed(q, nr, 0, 3)
        pair((q, nl), (q, nr))

    far_x, far_y = ring[0].far, ring[1].far

    @pl.loop(0, 2)
    def _(g):
        for q, k in ((2 * g, far_x), (2 * g + 1, far_y)):
            landed(q, k, 0, 4)
            landed(q, k, 1, 5)
        pair((2 * g, far_x), (2 * g + 1, far_y))

    rows_c = pl.ds(pl.multiple_of(c * (trades // 2), 8), trades // 2)
    rows_sib = pl.ds(pl.multiple_of(sib * (trades // 2), 8), trades // 2)
    swap = (acc.at[rows_sib], pr, ss_p.at[0], rs_p.at[0], sibling)
    send(*swap)
    strip_rows = out.shape[0]
    rdma(*swap).wait_recv()
    total = acc[rows_c] + pr[...]
    po[...] = jnp.concatenate(
        [total[:, s * LANE : (s + 1) * LANE].reshape(CHIPS, strip_rows, LANE) for s in (0, 1)], axis=1
    ).astype(BF16)

    tile = ob.at[z * RING + x]

    def deliver(n, dst):
        rdma(po.at[n], tile, ss_o.at[0], rs_o.at[0], {"grp": y, "path": dst}).start()

    for k in (4, 3, 5, 2, 6, 1, 7, 0):
        zz = lax.rem(z + k, DEPTH)
        for side in (0, 1):
            for u in (0, 1):
                n = side * 2 * DEPTH + 2 * zz + u
                dst = c * CHIPS + n
                if k:
                    deliver(n, dst)
                else:
                    pl.when(dst != me)(lambda n=n, dst=dst: deliver(n, dst))

                    @pl.when(dst == me)
                    def _():
                        pltpu.make_async_copy(po.at[n], tile, rs_o.at[0]).start()

    all_left()

    def j_crossed(e):
        for k in (1, 2, 3):
            rdma(*j_cross(e, k)).wait_send()

        @pl.when(core != c)
        def _():
            rdma(*j_cross(e, 0)).wait_send()

    both(j_crossed)

    @pl.when(turn)
    def _():
        for k in range(1, DEPTH):
            rdma(*j_line(k)).wait_send()

    pltpu.make_async_copy(ob, ob, rs_o.at[0]).wait()

    rest = []
    for t in range(CHIPS):
        tile = ob[t].astype(F32)
        out[:, t * LANE : (t + 1) * LANE] = tile[0:strip_rows]
        rest.append(tile[strip_rows : 2 * strip_rows, 0:more])
    out[:, main:params] = jnp.concatenate(rest, axis=1)

    def po_sent(n):
        rdma(po.at[0:n], po.at[0:n], ss_o.at[0], rs_o.at[0], sibling).wait_send()

    pl.when(core == c)(lambda: po_sent(CHIPS - 1))
    pl.when(core != c)(lambda: po_sent(CHIPS))


def per_device(
    path_sens, discounts, cash_flows, flow_index, exercise_step, trade_steps, jacobian_inv
):
    paths_own, params = path_sens.shape
    trades = cash_flows.shape[0]
    jrows = jacobian_inv.shape[0]
    strip = trades // PATHS
    rest = params - CHIPS * LANE
    pad = -(-jrows // 16) * 16
    half = params // 2
    slots = cash_flows.shape[1]
    part = pad // 2
    share = 16
    vm = pltpu.VMEM
    dma = pltpu.SemaphoreType.DMA
    scratch = [
        vm((paths_own, LANE), BF16),
        vm((slots, trades), F32),
        vm((slots, trades), jnp.int32),
        vm((1, trades), jnp.int32),
        vm((1, trades), jnp.int32),
        vm((half, paths_own), BF16),
        vm((half, paths_own), BF16),
        vm((paths_own, LANE), BF16),
        vm((half + 8, LANE), F32),
        vm((RING, RING, 2 * pad, LANE), F32),
        vm((RING, 6, pad, LANE), F32),
        vm((RING, 2 * pad, LANE), F32),
        vm((RING, RING, part, LANE), F32),
        vm((2, 2 * part, LANE), F32),
        vm((2, DEPTH, share, LANE), F32),
        vm((2, share, LANE), F32),
        vm((2, 2 * part, LANE), F32),
        vm((RING, RING, 2 * pad, LANE), F32),
        vm((jrows, params), BF16),
        vm((pad, -(-rest // LANE) * LANE), F32),
        vm((DEPTH, RING, pad + GROUP, LANE), BF16),
        vm((2, RING, pad + GROUP, LANE), BF16),
        vm((RING, RING, 2 * pad, LANE), BF16),
        vm((RING, RING, 2, GROUP, LANE), BF16),
        vm((RING * RING, 2 * pad, LANE), BF16),
        vm((trades, 3 * LANE), BF16),
        vm((trades, 4 * pad), jnp.int32),
        vm((2, trades, 4 * pad), BF16),
        vm((trades, 2 * LANE), F32),
        vm((trades // 2, 2 * LANE), F32),
        vm((CHIPS, 2 * strip, LANE), BF16),
        vm((CHIPS, 2 * strip, LANE), BF16),
        dma((RING + 1,)), dma((RING + 1,)), dma((7,)),
        dma((RING, 6)), dma((RING, 6)),
        dma((RING, RING)), dma((RING,)),
        dma((2, DEPTH)), dma((2,)),
        dma((2, DEPTH)), dma((2,)),
        dma((RING, RING)), dma((RING,)),
        dma((RING, 6)), dma((RING, 6)),
        dma((DEPTH,)), dma((2, RING)), dma((3, 2)),
        dma((2, 6)), dma((2, 6)),
        dma((2,)), dma((2,)),
        dma((1,)), dma((1,)),
        pltpu.SemaphoreType.REGULAR((2,)),
    ]
    vmem = pl.BlockSpec(memory_space=pltpu.VMEM)
    hbm = pl.BlockSpec(memory_space=pl.ANY)
    return pl.pallas_call(
        kernel,
        out_shape=jax.ShapeDtypeStruct((strip, params), F32),
        in_specs=[hbm] * 7,
        out_specs=vmem,
        scratch_shapes=scratch,
        compiler_params=pltpu.CompilerParams(
            collective_id=0, has_side_effects=True, vmem_limit_bytes=56 * 1024 * 1024
        ),
    )(
        discounts,
        path_sens.T,
        cash_flows.T,
        flow_index.T,
        exercise_step.reshape(1, trades),
        trade_steps.reshape(1, trades),
        jacobian_inv,
    )


def solution(mesh):
    placed = (
        P(("grp", "path"), None),
        P(("grp", "path"), None),
        P("grp", None),
        P("grp", None),
        P("grp"),
        P("grp"),
        P("path", None),
    )
    return jax.shard_map(
        per_device, mesh=mesh, in_specs=placed, out_specs=P(("grp", "path"), None), check_vma=False
    )
```

```python
import jax
import jax.numpy as jnp
from jax import lax
from jax.experimental import pallas as pl
from jax.experimental.pallas import tpu as pltpu
from jax.sharding import PartitionSpec as P

NB = 40
LANE = 128
RING = 4
DEPTH = 8
CHIPS = RING * DEPTH
PATHS = 2 * CHIPS
GROUP = 16
F32 = jnp.float32
BF16 = jnp.bfloat16
MESH = pl.DeviceIdType.MESH


def kernel(
    disc, sens, cash, index, exer, steps, jac, out,
    dv, cv, iv, ev, sv, s_own, s_in, d_in, xs, xp, r1, y2, r2, zb, rz, zr, zf, xf,
    jv, je, jp, jz, jr, jx, jb, wt, room, mk, acc, pr, po, ob,
    ss_s, rs_s, ls, ss_1, rs_1, ss_2, rs_2, ss_z, rs_z, ss_g, rs_g,
    ss_a2, rs_a2, ss_a1, rs_a1, ss_j, ss_jx, rs_j, ss_ja, rs_ja, ss_p, rs_p, ss_o, rs_o, near_z,
):
    y = lax.axis_index("grp")
    me = lax.axis_index("path")
    j = lax.div(me, 2)
    c = lax.rem(me, 2)
    x = lax.div(j, DEPTH)
    z = lax.rem(j, DEPTH)
    sib = 1 - c
    params = sens.shape[0]
    width = params // NB
    half = params // 2
    jrows = jac.shape[0]
    pad = xp.shape[2] // 2
    trades = cash.shape[1]

    def at_chip(xx, zz, cc):
        return {"grp": y, "path": (xx * DEPTH + zz) * 2 + cc}

    def rdma(src, dst, ss, rs, dev):
        return pltpu.make_async_remote_copy(
            src_ref=src, dst_ref=dst, send_sem=ss, recv_sem=rs, device_id=dev, device_id_type=MESH
        )

    sent = []

    def send(*args):
        d = rdma(*args)
        d.start()
        sent.append((None, d))

    def send_if(cond, *args):
        d = rdma(*args)

        @pl.when(cond)
        def _():
            d.start()

        sent.append((cond, d))

    sibling = at_chip(x, z, sib)

    def on_x(k):
        return at_chip(lax.rem(x + k, RING), z, c)

    def on_y(k):
        return {"grp": lax.rem(y + k, RING), "path": me}

    def on_z(k):
        return at_chip(x, lax.rem(z + k, DEPTH), c)

    lines = ((x, on_x), (y, on_y))

    barrier = pltpu.get_barrier_semaphore()
    partners = [sibling] + [on(k) for on in (on_x, on_y) for k in (1, RING - 1)]
    partners += [on_z(k) for k in (1, DEPTH - 1, 2, DEPTH - 2)]
    for d in partners:
        pl.semaphore_signal(barrier, inc=1, device_id=d, device_id_type=MESH)

    fetched = [
        pltpu.make_async_copy(src, dst, ls.at[n])
        for n, (src, dst) in enumerate(
            (
                (disc, dv),
                (sens.at[pl.ds(pl.multiple_of(c * half, 16), half)], s_own),
                (cash, cv), (index, iv), (exer, ev), (steps, sv), (jac, jv),
            )
        )
    ]
    for f in fetched:
        f.start()

    first_cut = (half // 4 // 16 + 1) * 16
    cuts = (0, first_cut, half // 2, half // 2 + first_cut, half)

    def s_copy(q):
        n = cuts[q + 1] - cuts[q]
        return (
            sens.at[pl.ds(pl.multiple_of(sib * half + cuts[q], 16), n)],
            s_in.at[pl.ds(cuts[q], n)], ss_s.at[q], rs_s.at[q], sibling,
        )

    d_copy = (disc, d_in, ss_s.at[RING], rs_s.at[RING], sibling)

    xs[half : half + 8] = jnp.zeros((8, LANE), F32)
    for f in fetched[:2]:
        f.wait()
    third = half // 3

    @pl.loop(0, 3)
    def _(n):
        rws = pl.ds(pl.multiple_of(n * third, 16), third)
        xs[rws] = jnp.dot(s_own[rws], dv[...], preferred_element_type=F32)

    pl.semaphore_wait(barrier, len(partners))
    send(*d_copy)
    for q in (0, 1):
        send(*s_copy(q))
    for n, k in enumerate((2, DEPTH - 2)):
        pl.semaphore_signal(near_z.at[n], inc=1, device_id=on_z(k), device_id_type=MESH)

    main = CHIPS * LANE
    more = (params - main) // CHIPS
    groups = pad // GROUP
    turn = lax.rem(z, RING) == y
    core = lax.div(x, 2)
    high = lax.div(z, RING)
    for f in fetched[2:]:
        f.wait()

    @pl.when(turn)
    def _():
        jp[...] = jnp.zeros(jp.shape, BF16)

        @pl.loop(0, DEPTH)
        def _(zz):
            for t in range(RING):
                col = pl.multiple_of((zz * RING + t) * LANE, LANE)
                jp[zz, t, 0:jrows] = jv[:, pl.ds(col, LANE)]

        je[...] = jnp.zeros(je.shape, F32)
        je[0:jrows, 0 : params - main] = jv[:, main:params].astype(F32)
        for t in range(CHIPS):
            packed = [
                je[r * GROUP : (r + 1) * GROUP, t * more : (t + 1) * more] for r in range(groups)
            ]
            packed.append(jnp.zeros((GROUP, LANE - groups * more), F32))
            jp[t // RING, t % RING, pad : pad + GROUP] = jnp.concatenate(packed, axis=1).astype(BF16)

        pltpu.make_async_copy(jp.at[z], jz.at[high], rs_j.at[2, high]).start()

    def j_line(k):
        zz = lax.rem(z + k, DEPTH)
        return jp.at[zz], jz.at[high], ss_j.at[k], rs_j.at[2, high], on_z(k)

    def j_depth(*steps_):
        @pl.when(turn)
        def _():
            for k in steps_:
                rdma(*j_line(k)).start()

    j_depth(2, 6, 1, 7)

    def part_rows(n, size):
        return pl.ds(pl.multiple_of(n * size, 8), size)

    class Scatter:
        def __init__(self, q):
            self.q = q
            self.i, self.on = lines[q % 2]
            self.nr, self.far, self.nl = (lax.rem(self.i + k, RING) for k in (1, 2, 3))
            self.right, self.left = self.on(1), self.on(3)

        def msg(self, n, h, k, dev):
            q = self.q
            return (
                xp.at[q, k, h * pad : (h + 1) * pad], r1.at[q, n],
                ss_1.at[q, n], rs_1.at[q, n], dev,
            )

        def first(self):
            send(*self.msg(0, 0, self.far, self.right))
            send(*self.msg(2, 1, self.far, self.left))

        def near(self):
            send(*self.msg(3, 1, self.nr, self.right))
            send(*self.msg(1, 0, self.nl, self.left))

        def second(self):
            for h, n, k, dev in ((0, 0, self.nr, self.right), (1, 2, self.nl, self.left)):
                rdma(*self.msg(n, h, k, dev)).wait_recv()
                xp[self.q, k, h * pad : (h + 1) * pad] += r1[self.q, n]
                send(*self.msg(4 + h, h, k, dev))

        def result(self):
            for h, n in ((0, 1), (1, 3)):
                rdma(*self.msg(n, h, self.i, self.left)).wait_recv()
                rdma(*self.msg(4 + h, h, self.i, self.left)).wait_recv()
                rws = slice(h * pad, (h + 1) * pad)
                y2[self.q, rws] = xp[self.q, self.i, rws] + r1[self.q, n] + r1[self.q, 4 + h]

    one = [Scatter(q) for q in range(RING)]
    rdma(*d_copy).wait_recv()
    for q in range(RING):
        rdma(*s_copy(q)).wait_recv()
        if q < 2:
            send(*s_copy(q + 2))
        xs[cuts[q] : cuts[q + 1]] += jnp.dot(
            s_in[cuts[q] : cuts[q + 1]], d_in[...], preferred_element_type=F32
        )
        for k in range(RING):
            for u in (0, 1):
                top = (8 * q + 2 * k + u) * jrows
                xp[q, k, u * pad : (u + 1) * pad] = xs[top : top + pad]
        one[q].first()
    for r in one:
        r.near()

    for n in (0, 1):
        pl.semaphore_wait(near_z.at[n], 1)
    j_depth(4, 3, 5)
    one[0].second()
    one[1].second()
    one[2].second()
    one[3].second()

    def j_cross(e, k):
        xx = lax.rem(x + k, RING)
        two_ = pl.ds(2 * lax.rem(x, 2), 2)
        if e == 0:
            src = jz.at[:, xx, 0:pad]
            dst = jr.at[two_, y, pl.ds(pl.multiple_of(c * pad, 16), pad)]
        else:
            src = jz.at[:, xx, pad : pad + GROUP]
            dst = jx.at[two_, y, c]
        return src, dst, ss_jx.at[e, k], rs_j.at[e, 0], at_chip(xx, z, core)

    def both(f):
        f(0)
        f(1)

    def j_send(e):
        for k in (2, 1, 3):
            rdma(*j_cross(e, k)).start()
        src, dst, ss, rs, dev = j_cross(e, 0)

        @pl.when(core == c)
        def _():
            pltpu.make_async_copy(src, dst, rs).start()

        @pl.when(core != c)
        def _():
            rdma(src, dst, ss, rs, dev).start()


    slots = cash.shape[0]
    forwards = lax.broadcasted_iota(jnp.int32, (LANE, trades), 0)
    late = forwards >= ev[...]
    weights = jnp.zeros((LANE, trades), F32)
    for s in range(slots):
        weights += jnp.where(late & (iv[s : s + 1] == forwards), cv[s : s + 1], 0.0)
    weights = weights * (1.0 / (disc.shape[0] * PATHS * RING))
    weights = weights.T
    w_hi = weights.astype(BF16)
    w_lo = (weights - w_hi.astype(F32)).astype(BF16)
    wt[...] = jnp.concatenate([w_hi, w_hi, w_lo], axis=1)
    reach = jnp.broadcast_to((sv[...] * width).astype(F32), (LANE, trades)).T.astype(jnp.int32)
    span = 4 * pad
    lane = lax.broadcasted_iota(jnp.int32, (trades, span), 1)
    lane = lane - jnp.where(lane >= 2 * pad, 2 * pad, 0)
    room[...] = (
        jnp.concatenate([reach] * (span // LANE) + [reach[:, : span % LANE]], axis=1)
        - lane + jnp.where(lane >= pad, pad - jrows, 0) - c * half
    )

    part = y2.shape[1] // RING

    def two(q, k):
        i, on = lines[1 - q % 2]
        return (
            y2.at[q, part_rows(lax.rem(i + k, RING), part)], r2.at[q, i],
            ss_2.at[q, k], rs_2.at[q], on(k),
        )

    for g in (0, 1):
        for q in (2 * g, 2 * g + 1):
            one[q].result()
            for k in (2, 1, 3):
                send(*two(q, k))
    for n in (0, 1):
        pltpu.make_async_copy(jp.at[0], jz.at[n], rs_j.at[2, n]).wait()
    both(j_send)

    share = zr.shape[1]
    count = 2 * part // share
    spread = (4, 3, 5, 2, 6, 1, 7)

    def turn_of(g, d):
        return lax.rem(d + count * g, DEPTH)

    def reduces(g):
        return turn_of(g, z) < count

    def z_piece(g, d):
        return part_rows(jnp.minimum(turn_of(g, d), count - 1), share)

    for g in (0, 1):
        for p in (0, 1):
            q = 2 * g + p
            i, on = lines[1 - p]
            total = y2[q, part_rows(i, part)]
            three = r2.at[q, 0 : RING - 1]
            rdma(three, three, ss_2.at[q, 0], rs_2.at[q], sibling).wait_recv()
            for k in (1, 2, 3):
                total += r2[q, lax.rem(i + k, RING)]
            zb[g, p * part : (p + 1) * part] = total
        for k in spread:
            d = lax.rem(z + k, DEPTH)
            send_if(
                turn_of(g, d) < count,
                zb.at[g, z_piece(g, d)], rz.at[g, z], ss_z.at[g, k], rs_z.at[g], on_z(k),
            )


    def j_ring(half_, k, n, dev):
        ref = jr.at[pl.ds(2 * half_, 2), k]
        return ref, ref, ss_ja.at[0, n], rs_ja.at[0, n], dev

    def j_fan(k):
        ref = jx.at[:, y]
        return ref, ref, ss_ja.at[1, k], rs_ja.at[1, 0], on_y(k)

    yr, yl = on_y(1), on_y(3)
    ynr, yfar, ynl = (lax.rem(y + k, RING) for k in (1, 2, 3))

    def j_start():
        for e, whole in ((0, jr.at[:, y]), (1, jx.at[:, y])):
            pltpu.make_async_copy(whole, whole, rs_j.at[e, 0]).wait()
        for n, (hh, d) in enumerate(((0, yr), (1, yl), (1, yr), (0, yl))):
            send(*j_ring(hh, y, n, d))
        for k in (2, 1, 3):
            send(*j_fan(k))

    def j_forward():
        rdma(*j_ring(0, ynl, 0, yr)).wait_recv()
        send(*j_ring(0, ynl, 4, yr))
        rdma(*j_ring(1, ynr, 1, yl)).wait_recv()
        send(*j_ring(1, ynr, 5, yl))

    def j_finish():
        for hh, k, n, d in ((1, ynl, 2, yr), (0, ynr, 3, yl), (0, yfar, 4, yr), (1, yfar, 5, yl)):
            rdma(*j_ring(hh, k, n, d)).wait_recv()

    def j_unpack():
        three = jx.at[0 : RING - 1]
        rdma(three, three, ss_ja.at[1, 0], rs_ja.at[1, 0], sibling).wait_recv()

        @pl.loop(0, RING * RING)
        def _(n):
            q, k = lax.div(n, RING), lax.rem(n, RING)
            for u in (0, 1):
                tile = jx[q, k, u].astype(F32)
                for r in range(groups):
                    at = u * pad + r * GROUP
                    turned_ = tile if r == 0 else pltpu.roll(tile, LANE - r * more, 1)
                    jb[n, at : at + GROUP] = turned_.astype(BF16)

    j_start()

    for g in (0, 1):
        reducer = reduces(g)

        @pl.when(reducer)
        def _():
            total = zb[g, z_piece(g, z)]
            seven = rz.at[g, 0 : DEPTH - 1]
            rdma(seven, seven, ss_z.at[g, 0], rs_z.at[g], sibling).wait_recv()
            for k in range(1, DEPTH):
                total += rz[g, lax.rem(z + k, DEPTH)]
            zr[g] = total
            zf[g, z_piece(g, z)] = total

        for k in spread:
            send_if(
                reducer, zr.at[g], zf.at[g, z_piece(g, z)], ss_g.at[g, k], rs_g.at[g], on_z(k)
            )


    def home(q, i):
        return xf.at[q, lines[q % 2][0], part_rows(i, part)]

    for g in (0, 1):
        for some, ref in ((reduces(g), zf.at[g, 0 : (count - 1) * share]), (~reduces(g), zf.at[g])):

            @pl.when(some)
            def _():
                rdma(ref, ref, ss_g.at[g, 0], rs_g.at[g], sibling).wait_recv()

        for p in (0, 1):
            q = 2 * g + p
            i, on = lines[1 - p]
            mine = zf.at[g, p * part : (p + 1) * part]
            for k in (2, 1, 3):
                send(mine, home(q, i), ss_a2.at[q, k], rs_a2.at[q], on(k))
            home(q, i)[...] = mine[...]

    def all_left():
        while sent:
            cond, d = sent.pop()
            if cond is None:
                d.wait_send()
            else:
                pl.when(cond)(d.wait_send)

    later = sent[-4 * (RING - 1):]
    del sent[-len(later) :]
    all_left()
    sent.extend(later)
    j_forward()
    j_unpack()

    class Gather:
        def __init__(self, q):
            self.q = q
            self.i, self.on = lines[q % 2]
            self.nr, self.far, self.nl = (lax.rem(self.i + k, RING) for k in (1, 2, 3))
            self.right, self.left = self.on(1), self.on(3)

        def msg(self, n, h, k, dev):
            ref = xf.at[self.q, k, h * pad : (h + 1) * pad]
            return ref, ref, ss_a1.at[self.q, n], rs_a1.at[self.q, n], dev

        def start(self):
            q = self.q
            three = xf.at[q, 0, 0 : (RING - 1) * part]
            rdma(three, three, ss_a2.at[q, 0], rs_a2.at[q], sibling).wait_recv()
            send(*self.msg(0, 0, self.i, self.right))
            send(*self.msg(1, 1, self.i, self.left))

        def rest(self):
            send(*self.msg(2, 1, self.i, self.right))
            send(*self.msg(3, 0, self.i, self.left))

        def forward(self):
            rdma(*self.msg(0, 0, self.nl, self.right)).wait_recv()
            send(*self.msg(4, 0, self.nl, self.right))
            rdma(*self.msg(1, 1, self.nr, self.left)).wait_recv()
            send(*self.msg(5, 1, self.nr, self.left))

    ring = [Gather(q) for q in range(RING)]
    for q in range(RING):
        ring[q].start()

    acc[...] = jnp.zeros(acc.shape, F32)

    second_lane = lax.broadcasted_iota(jnp.int32, (1, span), 1) >= 2 * pad

    def mask(*both_):
        values = jnp.concatenate([xf[q, k] for q, k in both_], axis=0)
        hi = values.astype(BF16)
        lo = (values - hi.astype(F32)).astype(BF16)
        vega = lax.dot_general(
            wt[...], jnp.concatenate([hi, lo, hi], axis=1), (((1,), (1,)), ((), ())),
            preferred_element_type=F32,
        )
        start = [(8 * q + 2 * k) * jrows for q, k in both_]
        keep = room[...] > jnp.where(second_lane, start[1], start[0])
        return jnp.where(keep, vega, 0.0).astype(BF16)

    def add(masked, *both_):
        columns = [
            jnp.concatenate([jr[q, k], jb[RING * q + k]], axis=1) for q, k in both_
        ]
        acc[...] += jnp.dot(
            masked, jnp.concatenate(columns, axis=0), preferred_element_type=F32
        )

    def pair(*both_):
        add(mask(*both_), *both_)

    def landed(q, k, h, n):
        ref = xf.at[q, k, h * pad : (h + 1) * pad]
        rdma(ref, ref, ss_a1.at[q, n], rs_a1.at[q, n], sibling).wait_recv()

    def ring_place(q, step):
        return lax.rem(jnp.where(lax.rem(q, 2) == 0, x, y) + step, RING)

    mine = lambda g: ((2 * g, x), (2 * g + 1, y))

    @pl.loop(0, 2)
    def _(g):
        mk[g] = mask(*mine(g))

    for r in ring:
        r.rest()
    for r in ring:
        r.forward()
    j_finish()

    @pl.loop(0, 2)
    def _(g):
        add(mk[g], *mine(g))

    @pl.loop(0, RING)
    def _(q):
        nl, nr = ring_place(q, 3), ring_place(q, 1)
        landed(q, nl, 1, 2)
        landed(q, nr, 0, 3)
        pair((q, nl), (q, nr))

    far_x, far_y = ring[0].far, ring[1].far

    @pl.loop(0, 2)
    def _(g):
        for q, k in ((2 * g, far_x), (2 * g + 1, far_y)):
            landed(q, k, 0, 4)
            landed(q, k, 1, 5)
        pair((2 * g, far_x), (2 * g + 1, far_y))

    rows_c = pl.ds(pl.multiple_of(c * (trades // 2), 8), trades // 2)
    rows_sib = pl.ds(pl.multiple_of(sib * (trades // 2), 8), trades // 2)
    swap = (acc.at[rows_sib], pr, ss_p.at[0], rs_p.at[0], sibling)
    send(*swap)
    strip_rows = out.shape[0]
    rdma(*swap).wait_recv()
    total = acc[rows_c] + pr[...]
    po[...] = jnp.concatenate(
        [total[:, s * LANE : (s + 1) * LANE].reshape(CHIPS, strip_rows, LANE) for s in (0, 1)], axis=1
    ).astype(BF16)

    tile = ob.at[z * RING + x]

    def deliver(n, dst):
        rdma(po.at[n], tile, ss_o.at[0], rs_o.at[0], {"grp": y, "path": dst}).start()

    for k in (4, 3, 5, 2, 6, 1, 7, 0):
        zz = lax.rem(z + k, DEPTH)
        for side in (0, 1):
            for u in (0, 1):
                n = side * 2 * DEPTH + 2 * zz + u
                dst = c * CHIPS + n
                if k:
                    deliver(n, dst)
                else:
                    pl.when(dst != me)(lambda n=n, dst=dst: deliver(n, dst))

                    @pl.when(dst == me)
                    def _():
                        pltpu.make_async_copy(po.at[n], tile, rs_o.at[0]).start()

    all_left()

    def j_crossed(e):
        for k in (1, 2, 3):
            rdma(*j_cross(e, k)).wait_send()

        @pl.when(core != c)
        def _():
            rdma(*j_cross(e, 0)).wait_send()

    both(j_crossed)

    @pl.when(turn)
    def _():
        for k in range(1, DEPTH):
            rdma(*j_line(k)).wait_send()

    pltpu.make_async_copy(ob, ob, rs_o.at[0]).wait()

    rest = []
    for t in range(CHIPS):
        tile = ob[t].astype(F32)
        out[:, t * LANE : (t + 1) * LANE] = tile[0:strip_rows]
        rest.append(tile[strip_rows : 2 * strip_rows, 0:more])
    out[:, main:params] = jnp.concatenate(rest, axis=1)

    def po_sent(n):
        rdma(po.at[0:n], po.at[0:n], ss_o.at[0], rs_o.at[0], sibling).wait_send()

    pl.when(core == c)(lambda: po_sent(CHIPS - 1))
    pl.when(core != c)(lambda: po_sent(CHIPS))


def per_device(
    path_sens, discounts, cash_flows, flow_index, exercise_step, trade_steps, jacobian_inv
):
    paths_own, params = path_sens.shape
    trades = cash_flows.shape[0]
    jrows = jacobian_inv.shape[0]
    strip = trades // PATHS
    rest = params - CHIPS * LANE
    pad = -(-jrows // 16) * 16
    half = params // 2
    slots = cash_flows.shape[1]
    part = pad // 2
    share = 16
    vm = pltpu.VMEM
    dma = pltpu.SemaphoreType.DMA
    scratch = [
        vm((paths_own, LANE), BF16),
        vm((slots, trades), F32),
        vm((slots, trades), jnp.int32),
        vm((1, trades), jnp.int32),
        vm((1, trades), jnp.int32),
        vm((half, paths_own), BF16),
        vm((half, paths_own), BF16),
        vm((paths_own, LANE), BF16),
        vm((half + 8, LANE), F32),
        vm((RING, RING, 2 * pad, LANE), F32),
        vm((RING, 6, pad, LANE), F32),
        vm((RING, 2 * pad, LANE), F32),
        vm((RING, RING, part, LANE), F32),
        vm((2, 2 * part, LANE), F32),
        vm((2, DEPTH, share, LANE), F32),
        vm((2, share, LANE), F32),
        vm((2, 2 * part, LANE), F32),
        vm((RING, RING, 2 * pad, LANE), F32),
        vm((jrows, params), BF16),
        vm((pad, -(-rest // LANE) * LANE), F32),
        vm((DEPTH, RING, pad + GROUP, LANE), BF16),
        vm((2, RING, pad + GROUP, LANE), BF16),
        vm((RING, RING, 2 * pad, LANE), BF16),
        vm((RING, RING, 2, GROUP, LANE), BF16),
        vm((RING * RING, 2 * pad, LANE), BF16),
        vm((trades, 3 * LANE), BF16),
        vm((trades, 4 * pad), jnp.int32),
        vm((2, trades, 4 * pad), BF16),
        vm((trades, 2 * LANE), F32),
        vm((trades // 2, 2 * LANE), F32),
        vm((CHIPS, 2 * strip, LANE), BF16),
        vm((CHIPS, 2 * strip, LANE), BF16),
        dma((RING + 1,)), dma((RING + 1,)), dma((7,)),
        dma((RING, 6)), dma((RING, 6)),
        dma((RING, RING)), dma((RING,)),
        dma((2, DEPTH)), dma((2,)),
        dma((2, DEPTH)), dma((2,)),
        dma((RING, RING)), dma((RING,)),
        dma((RING, 6)), dma((RING, 6)),
        dma((DEPTH,)), dma((2, RING)), dma((3, 2)),
        dma((2, 6)), dma((2, 6)),
        dma((2,)), dma((2,)),
        dma((1,)), dma((1,)),
        pltpu.SemaphoreType.REGULAR((2,)),
    ]
    vmem = pl.BlockSpec(memory_space=pltpu.VMEM)
    hbm = pl.BlockSpec(memory_space=pl.ANY)
    return pl.pallas_call(
        kernel,
        out_shape=jax.ShapeDtypeStruct((strip, params), F32),
        in_specs=[hbm] * 7,
        out_specs=vmem,
        scratch_shapes=scratch,
        compiler_params=pltpu.CompilerParams(
            collective_id=0, has_side_effects=True, vmem_limit_bytes=56 * 1024 * 1024
        ),
    )(
        discounts,
        path_sens.T,
        cash_flows.T,
        flow_index.T,
        exercise_step.reshape(1, trades),
        trade_steps.reshape(1, trades),
        jacobian_inv,
    )


def solution(mesh):
    placed = (
        P(("grp", "path"), None),
        P(("grp", "path"), None),
        P("grp", None),
        P("grp", None),
        P("grp"),
        P("grp"),
        P("path", None),
    )
    return jax.shard_map(
        per_device, mesh=mesh, in_specs=placed, out_specs=P(("grp", "path"), None), check_vma=False
    )
```

```python
import jax
import jax.numpy as jnp
from jax import lax
from jax.experimental import pallas as pl
from jax.experimental.pallas import tpu as pltpu
from jax.sharding import PartitionSpec as P

NB = 40
LANE = 128
RING = 4
DEPTH = 8
CHIPS = RING * DEPTH
PATHS = 2 * CHIPS
GROUP = 16
F32 = jnp.float32
BF16 = jnp.bfloat16
MESH = pl.DeviceIdType.MESH


def kernel(
    disc, sens, cash, index, exer, steps, jac, out,
    dv, cv, iv, ev, sv, s_own, s_in, d_in, xs, xp, r1, y2, r2, zb, rz, zr, zf, xf,
    jv, je, jp, jz, jr, jx, jb, wt, room, mk, acc, pr, po, ob,
    ss_s, rs_s, ls, ss_1, rs_1, ss_2, rs_2, ss_z, rs_z, ss_g, rs_g,
    ss_a2, rs_a2, ss_a1, rs_a1, ss_j, ss_jx, rs_j, ss_ja, rs_ja, ss_p, rs_p, ss_o, rs_o, near_z,
):
    y = lax.axis_index("grp")
    me = lax.axis_index("path")
    j = lax.div(me, 2)
    c = lax.rem(me, 2)
    x = lax.div(j, DEPTH)
    z = lax.rem(j, DEPTH)
    sib = 1 - c
    params = sens.shape[0]
    width = params // NB
    half = params // 2
    jrows = jac.shape[0]
    pad = xp.shape[2] // 2
    trades = cash.shape[1]

    def at_chip(xx, zz, cc):
        return {"grp": y, "path": (xx * DEPTH + zz) * 2 + cc}

    def rdma(src, dst, ss, rs, dev):
        return pltpu.make_async_remote_copy(
            src_ref=src, dst_ref=dst, send_sem=ss, recv_sem=rs, device_id=dev, device_id_type=MESH
        )

    sent = []

    def send(*args):
        d = rdma(*args)
        d.start()
        sent.append((None, d))

    def send_if(cond, *args):
        d = rdma(*args)

        @pl.when(cond)
        def _():
            d.start()

        sent.append((cond, d))

    sibling = at_chip(x, z, sib)

    def on_x(k):
        return at_chip(lax.rem(x + k, RING), z, c)

    def on_y(k):
        return {"grp": lax.rem(y + k, RING), "path": me}

    def on_z(k):
        return at_chip(x, lax.rem(z + k, DEPTH), c)

    lines = ((x, on_x), (y, on_y))

    barrier = pltpu.get_barrier_semaphore()
    partners = [sibling] + [on(k) for on in (on_x, on_y) for k in (1, RING - 1)]
    partners += [on_z(k) for k in (1, DEPTH - 1, 2, DEPTH - 2)]
    for d in partners:
        pl.semaphore_signal(barrier, inc=1, device_id=d, device_id_type=MESH)

    fetched = [
        pltpu.make_async_copy(src, dst, ls.at[n])
        for n, (src, dst) in enumerate(
            (
                (disc, dv),
                (sens.at[pl.ds(pl.multiple_of(c * half, 16), half)], s_own),
                (cash, cv), (index, iv), (exer, ev), (steps, sv), (jac, jv),
            )
        )
    ]
    for f in fetched:
        f.start()

    first_cut = (half // 4 // 16 + 1) * 16
    cuts = (0, first_cut, half // 2, half // 2 + first_cut, half)

    def s_copy(q):
        n = cuts[q + 1] - cuts[q]
        return (
            sens.at[pl.ds(pl.multiple_of(sib * half + cuts[q], 16), n)],
            s_in.at[pl.ds(cuts[q], n)], ss_s.at[q], rs_s.at[q], sibling,
        )

    d_copy = (disc, d_in, ss_s.at[RING], rs_s.at[RING], sibling)

    xs[half : half + 8] = jnp.zeros((8, LANE), F32)
    for f in fetched[:2]:
        f.wait()
    third = half // 3

    @pl.loop(0, 3)
    def _(n):
        rws = pl.ds(pl.multiple_of(n * third, 16), third)
        xs[rws] = jnp.dot(s_own[rws], dv[...], preferred_element_type=F32)

    pl.semaphore_wait(barrier, len(partners))
    send(*d_copy)
    leading = [rdma(*s_copy(q)) for q in (0, 1)]
    for d in leading:
        d.start()
    for n, k in enumerate((2, DEPTH - 2)):
        pl.semaphore_signal(near_z.at[n], inc=1, device_id=on_z(k), device_id_type=MESH)

    main = CHIPS * LANE
    more = (params - main) // CHIPS
    groups = pad // GROUP
    turn = lax.rem(z, RING) == y
    core = lax.div(x, 2)
    high = lax.div(z, RING)
    for f in fetched[2:]:
        f.wait()

    @pl.when(turn)
    def _():
        jp[...] = jnp.zeros(jp.shape, BF16)

        @pl.loop(0, DEPTH)
        def _(zz):
            for t in range(RING):
                col = pl.multiple_of((zz * RING + t) * LANE, LANE)
                jp[zz, t, 0:jrows] = jv[:, pl.ds(col, LANE)]

        je[...] = jnp.zeros(je.shape, F32)
        je[0:jrows, 0 : params - main] = jv[:, main:params].astype(F32)
        for t in range(CHIPS):
            packed = [
                je[r * GROUP : (r + 1) * GROUP, t * more : (t + 1) * more] for r in range(groups)
            ]
            packed.append(jnp.zeros((GROUP, LANE - groups * more), F32))
            jp[t // RING, t % RING, pad : pad + GROUP] = jnp.concatenate(packed, axis=1).astype(BF16)

        pltpu.make_async_copy(jp.at[z], jz.at[high], rs_j.at[2, high]).start()

    def j_line(k):
        zz = lax.rem(z + k, DEPTH)
        return jp.at[zz], jz.at[high], ss_j.at[k], rs_j.at[2, high], on_z(k)

    def j_depth(*steps_):
        @pl.when(turn)
        def _():
            for k in steps_:
                rdma(*j_line(k)).start()

    j_depth(2, 6, 1, 7)

    def part_rows(n, size):
        return pl.ds(pl.multiple_of(n * size, 8), size)

    class Scatter:
        def __init__(self, q):
            self.q = q
            self.i, self.on = lines[q % 2]
            self.nr, self.far, self.nl = (lax.rem(self.i + k, RING) for k in (1, 2, 3))
            self.right, self.left = self.on(1), self.on(3)

        def msg(self, n, h, k, dev):
            q = self.q
            return (
                xp.at[q, k, h * pad : (h + 1) * pad], r1.at[q, n],
                ss_1.at[q, n], rs_1.at[q, n], dev,
            )

        def first(self):
            send(*self.msg(0, 0, self.far, self.right))
            send(*self.msg(2, 1, self.far, self.left))

        def near(self):
            send(*self.msg(3, 1, self.nr, self.right))
            send(*self.msg(1, 0, self.nl, self.left))

        def second(self):
            for h, n, k, dev in ((0, 0, self.nr, self.right), (1, 2, self.nl, self.left)):
                rdma(*self.msg(n, h, k, dev)).wait_recv()
                xp[self.q, k, h * pad : (h + 1) * pad] += r1[self.q, n]
                send(*self.msg(4 + h, h, k, dev))

        def result(self):
            for h, n in ((0, 1), (1, 3)):
                rdma(*self.msg(n, h, self.i, self.left)).wait_recv()
                rdma(*self.msg(4 + h, h, self.i, self.left)).wait_recv()
                rws = slice(h * pad, (h + 1) * pad)
                y2[self.q, rws] = xp[self.q, self.i, rws] + r1[self.q, n] + r1[self.q, 4 + h]

    one = [Scatter(q) for q in range(RING)]
    for q, d in enumerate(leading):
        d.wait_send()
        send(*s_copy(q + 2))
    rdma(*d_copy).wait_recv()
    for q in range(RING):
        rdma(*s_copy(q)).wait_recv()
        xs[cuts[q] : cuts[q + 1]] += jnp.dot(
            s_in[cuts[q] : cuts[q + 1]], d_in[...], preferred_element_type=F32
        )
        for k in range(RING):
            for u in (0, 1):
                top = (8 * q + 2 * k + u) * jrows
                xp[q, k, u * pad : (u + 1) * pad] = xs[top : top + pad]
        one[q].first()
    for r in one:
        r.near()

    for n in (0, 1):
        pl.semaphore_wait(near_z.at[n], 1)
    j_depth(4, 3, 5)
    one[0].second()
    one[1].second()
    one[2].second()
    one[3].second()

    def j_cross(e, k):
        xx = lax.rem(x + k, RING)
        two_ = pl.ds(2 * lax.rem(x, 2), 2)
        if e == 0:
            src = jz.at[:, xx, 0:pad]
            dst = jr.at[two_, y, pl.ds(pl.multiple_of(c * pad, 16), pad)]
        else:
            src = jz.at[:, xx, pad : pad + GROUP]
            dst = jx.at[two_, y, c]
        return src, dst, ss_jx.at[e, k], rs_j.at[e, 0], at_chip(xx, z, core)

    def both(f):
        f(0)
        f(1)

    def j_send(e):
        for k in (2, 1, 3):
            rdma(*j_cross(e, k)).start()
        src, dst, ss, rs, dev = j_cross(e, 0)

        @pl.when(core == c)
        def _():
            pltpu.make_async_copy(src, dst, rs).start()

        @pl.when(core != c)
        def _():
            rdma(src, dst, ss, rs, dev).start()


    part = y2.shape[1] // RING

    def two(q, k):
        i, on = lines[1 - q % 2]
        return (
            y2.at[q, part_rows(lax.rem(i + k, RING), part)], r2.at[q, i],
            ss_2.at[q, k], rs_2.at[q], on(k),
        )

    for g in (0, 1):
        for q in (2 * g, 2 * g + 1):
            one[q].result()
            for k in (2, 1, 3):
                send(*two(q, k))
    for n in (0, 1):
        pltpu.make_async_copy(jp.at[0], jz.at[n], rs_j.at[2, n]).wait()
    both(j_send)

    share = zr.shape[1]
    count = 2 * part // share
    spread = (4, 3, 5, 2, 6, 1, 7)

    def turn_of(g, d):
        return lax.rem(d + count * g, DEPTH)

    def reduces(g):
        return turn_of(g, z) < count

    def z_piece(g, d):
        return part_rows(jnp.minimum(turn_of(g, d), count - 1), share)

    for g in (0, 1):
        for p in (0, 1):
            q = 2 * g + p
            i, on = lines[1 - p]
            total = y2[q, part_rows(i, part)]
            three = r2.at[q, 0 : RING - 1]
            rdma(three, three, ss_2.at[q, 0], rs_2.at[q], sibling).wait_recv()
            for k in (1, 2, 3):
                total += r2[q, lax.rem(i + k, RING)]
            zb[g, p * part : (p + 1) * part] = total
        for k in spread:
            d = lax.rem(z + k, DEPTH)
            send_if(
                turn_of(g, d) < count,
                zb.at[g, z_piece(g, d)], rz.at[g, z], ss_z.at[g, k], rs_z.at[g], on_z(k),
            )


    def j_ring(half_, k, n, dev):
        ref = jr.at[pl.ds(2 * half_, 2), k]
        return ref, ref, ss_ja.at[0, n], rs_ja.at[0, n], dev

    def j_fan(k):
        ref = jx.at[:, y]
        return ref, ref, ss_ja.at[1, k], rs_ja.at[1, 0], on_y(k)

    yr, yl = on_y(1), on_y(3)
    ynr, yfar, ynl = (lax.rem(y + k, RING) for k in (1, 2, 3))

    def j_start():
        for e, whole in ((0, jr.at[:, y]), (1, jx.at[:, y])):
            pltpu.make_async_copy(whole, whole, rs_j.at[e, 0]).wait()
        for n, (hh, d) in enumerate(((0, yr), (1, yl), (1, yr), (0, yl))):
            send(*j_ring(hh, y, n, d))
        for k in (2, 1, 3):
            send(*j_fan(k))

    def j_forward():
        rdma(*j_ring(0, ynl, 0, yr)).wait_recv()
        send(*j_ring(0, ynl, 4, yr))
        rdma(*j_ring(1, ynr, 1, yl)).wait_recv()
        send(*j_ring(1, ynr, 5, yl))

    def j_finish():
        for hh, k, n, d in ((1, ynl, 2, yr), (0, ynr, 3, yl), (0, yfar, 4, yr), (1, yfar, 5, yl)):
            rdma(*j_ring(hh, k, n, d)).wait_recv()

    def j_unpack():
        three = jx.at[0 : RING - 1]
        rdma(three, three, ss_ja.at[1, 0], rs_ja.at[1, 0], sibling).wait_recv()

        @pl.loop(0, RING * RING)
        def _(n):
            q, k = lax.div(n, RING), lax.rem(n, RING)
            for u in (0, 1):
                tile = jx[q, k, u].astype(F32)
                for r in range(groups):
                    at = u * pad + r * GROUP
                    turned_ = tile if r == 0 else pltpu.roll(tile, LANE - r * more, 1)
                    jb[n, at : at + GROUP] = turned_.astype(BF16)

    j_start()

    for g in (0, 1):
        reducer = reduces(g)

        @pl.when(reducer)
        def _():
            total = zb[g, z_piece(g, z)]
            seven = rz.at[g, 0 : DEPTH - 1]
            rdma(seven, seven, ss_z.at[g, 0], rs_z.at[g], sibling).wait_recv()
            for k in range(1, DEPTH):
                total += rz[g, lax.rem(z + k, DEPTH)]
            zr[g] = total
            zf[g, z_piece(g, z)] = total

        for k in spread:
            send_if(
                reducer, zr.at[g], zf.at[g, z_piece(g, z)], ss_g.at[g, k], rs_g.at[g], on_z(k)
            )


    slots = cash.shape[0]
    forwards = lax.broadcasted_iota(jnp.int32, (LANE, trades), 0)
    late = forwards >= ev[...]
    weights = jnp.zeros((LANE, trades), F32)
    for s in range(slots):
        weights += jnp.where(late & (iv[s : s + 1] == forwards), cv[s : s + 1], 0.0)
    weights = weights * (1.0 / (disc.shape[0] * PATHS * RING))
    weights = weights.T
    w_hi = weights.astype(BF16)
    w_lo = (weights - w_hi.astype(F32)).astype(BF16)
    wt[...] = jnp.concatenate([w_hi, w_hi, w_lo], axis=1)
    reach = jnp.broadcast_to((sv[...] * width).astype(F32), (LANE, trades)).T.astype(jnp.int32)
    span = 4 * pad
    lane = lax.broadcasted_iota(jnp.int32, (trades, span), 1)
    lane = lane - jnp.where(lane >= 2 * pad, 2 * pad, 0)
    room[...] = (
        jnp.concatenate([reach] * (span // LANE) + [reach[:, : span % LANE]], axis=1)
        - lane + jnp.where(lane >= pad, pad - jrows, 0) - c * half
    )

    def home(q, i):
        return xf.at[q, lines[q % 2][0], part_rows(i, part)]

    for g in (0, 1):
        for some, ref in ((reduces(g), zf.at[g, 0 : (count - 1) * share]), (~reduces(g), zf.at[g])):

            @pl.when(some)
            def _():
                rdma(ref, ref, ss_g.at[g, 0], rs_g.at[g], sibling).wait_recv()

        for p in (0, 1):
            q = 2 * g + p
            i, on = lines[1 - p]
            mine = zf.at[g, p * part : (p + 1) * part]
            for k in (2, 1, 3):
                send(mine, home(q, i), ss_a2.at[q, k], rs_a2.at[q], on(k))
            home(q, i)[...] = mine[...]

    def all_left():
        while sent:
            cond, d = sent.pop()
            if cond is None:
                d.wait_send()
            else:
                pl.when(cond)(d.wait_send)

    later = sent[-4 * (RING - 1):]
    del sent[-len(later) :]
    all_left()
    sent.extend(later)
    j_forward()
    j_unpack()

    class Gather:
        def __init__(self, q):
            self.q = q
            self.i, self.on = lines[q % 2]
            self.nr, self.far, self.nl = (lax.rem(self.i + k, RING) for k in (1, 2, 3))
            self.right, self.left = self.on(1), self.on(3)

        def msg(self, n, h, k, dev):
            ref = xf.at[self.q, k, h * pad : (h + 1) * pad]
            return ref, ref, ss_a1.at[self.q, n], rs_a1.at[self.q, n], dev

        def start(self):
            q = self.q
            three = xf.at[q, 0, 0 : (RING - 1) * part]
            rdma(three, three, ss_a2.at[q, 0], rs_a2.at[q], sibling).wait_recv()
            send(*self.msg(0, 0, self.i, self.right))
            send(*self.msg(1, 1, self.i, self.left))
            send(*self.msg(2, 1, self.i, self.right))
            send(*self.msg(3, 0, self.i, self.left))

        def forward(self):
            rdma(*self.msg(0, 0, self.nl, self.right)).wait_recv()
            send(*self.msg(4, 0, self.nl, self.right))
            rdma(*self.msg(1, 1, self.nr, self.left)).wait_recv()
            send(*self.msg(5, 1, self.nr, self.left))

    ring = [Gather(q) for q in range(RING)]
    for q in range(RING):
        ring[q].start()

    acc[...] = jnp.zeros(acc.shape, F32)

    second_lane = lax.broadcasted_iota(jnp.int32, (1, span), 1) >= 2 * pad

    def mask(*both_):
        values = jnp.concatenate([xf[q, k] for q, k in both_], axis=0)
        hi = values.astype(BF16)
        lo = (values - hi.astype(F32)).astype(BF16)
        vega = lax.dot_general(
            wt[...], jnp.concatenate([hi, lo, hi], axis=1), (((1,), (1,)), ((), ())),
            preferred_element_type=F32,
        )
        start = [(8 * q + 2 * k) * jrows for q, k in both_]
        keep = room[...] > jnp.where(second_lane, start[1], start[0])
        return jnp.where(keep, vega, 0.0).astype(BF16)

    def add(masked, *both_):
        columns = [
            jnp.concatenate([jr[q, k], jb[RING * q + k]], axis=1) for q, k in both_
        ]
        acc[...] += jnp.dot(
            masked, jnp.concatenate(columns, axis=0), preferred_element_type=F32
        )

    def pair(*both_):
        add(mask(*both_), *both_)

    def landed(q, k, h, n):
        ref = xf.at[q, k, h * pad : (h + 1) * pad]
        rdma(ref, ref, ss_a1.at[q, n], rs_a1.at[q, n], sibling).wait_recv()

    def ring_place(q, step):
        return lax.rem(jnp.where(lax.rem(q, 2) == 0, x, y) + step, RING)

    mine = lambda g: ((2 * g, x), (2 * g + 1, y))

    @pl.loop(0, 2)
    def _(g):
        mk[g] = mask(*mine(g))

    for r in ring:
        r.forward()
    j_finish()

    @pl.loop(0, 2)
    def _(g):
        add(mk[g], *mine(g))

    @pl.loop(0, RING)
    def _(q):
        nl, nr = ring_place(q, 3), ring_place(q, 1)
        landed(q, nl, 1, 2)
        landed(q, nr, 0, 3)
        pair((q, nl), (q, nr))

    far_x, far_y = ring[0].far, ring[1].far

    @pl.loop(0, 2)
    def _(g):
        for q, k in ((2 * g, far_x), (2 * g + 1, far_y)):
            landed(q, k, 0, 4)
            landed(q, k, 1, 5)
        pair((2 * g, far_x), (2 * g + 1, far_y))

    rows_c = pl.ds(pl.multiple_of(c * (trades // 2), 8), trades // 2)
    rows_sib = pl.ds(pl.multiple_of(sib * (trades // 2), 8), trades // 2)
    swap = (acc.at[rows_sib], pr, ss_p.at[0], rs_p.at[0], sibling)
    send(*swap)
    strip_rows = out.shape[0]
    rdma(*swap).wait_recv()
    total = acc[rows_c] + pr[...]
    po[...] = jnp.concatenate(
        [total[:, s * LANE : (s + 1) * LANE].reshape(CHIPS, strip_rows, LANE) for s in (0, 1)], axis=1
    ).astype(BF16)

    tile = ob.at[z * RING + x]

    def deliver(n, dst):
        rdma(po.at[n], tile, ss_o.at[0], rs_o.at[0], {"grp": y, "path": dst}).start()

    for k in (4, 3, 5, 2, 6, 1, 7, 0):
        zz = lax.rem(z + k, DEPTH)
        for side in (0, 1):
            for u in (0, 1):
                n = side * 2 * DEPTH + 2 * zz + u
                dst = c * CHIPS + n
                if k:
                    deliver(n, dst)
                else:
                    pl.when(dst != me)(lambda n=n, dst=dst: deliver(n, dst))

                    @pl.when(dst == me)
                    def _():
                        pltpu.make_async_copy(po.at[n], tile, rs_o.at[0]).start()

    all_left()

    def j_crossed(e):
        for k in (1, 2, 3):
            rdma(*j_cross(e, k)).wait_send()

        @pl.when(core != c)
        def _():
            rdma(*j_cross(e, 0)).wait_send()

    both(j_crossed)

    @pl.when(turn)
    def _():
        for k in range(1, DEPTH):
            rdma(*j_line(k)).wait_send()

    pltpu.make_async_copy(ob, ob, rs_o.at[0]).wait()

    rest = []
    for t in range(CHIPS):
        tile = ob[t].astype(F32)
        out[:, t * LANE : (t + 1) * LANE] = tile[0:strip_rows]
        rest.append(tile[strip_rows : 2 * strip_rows, 0:more])
    out[:, main:params] = jnp.concatenate(rest, axis=1)

    def po_sent(n):
        rdma(po.at[0:n], po.at[0:n], ss_o.at[0], rs_o.at[0], sibling).wait_send()

    pl.when(core == c)(lambda: po_sent(CHIPS - 1))
    pl.when(core != c)(lambda: po_sent(CHIPS))


def per_device(
    path_sens, discounts, cash_flows, flow_index, exercise_step, trade_steps, jacobian_inv
):
    paths_own, params = path_sens.shape
    trades = cash_flows.shape[0]
    jrows = jacobian_inv.shape[0]
    strip = trades // PATHS
    rest = params - CHIPS * LANE
    pad = -(-jrows // 16) * 16
    half = params // 2
    slots = cash_flows.shape[1]
    part = pad // 2
    share = 16
    vm = pltpu.VMEM
    dma = pltpu.SemaphoreType.DMA
    scratch = [
        vm((paths_own, LANE), BF16),
        vm((slots, trades), F32),
        vm((slots, trades), jnp.int32),
        vm((1, trades), jnp.int32),
        vm((1, trades), jnp.int32),
        vm((half, paths_own), BF16),
        vm((half, paths_own), BF16),
        vm((paths_own, LANE), BF16),
        vm((half + 8, LANE), F32),
        vm((RING, RING, 2 * pad, LANE), F32),
        vm((RING, 6, pad, LANE), F32),
        vm((RING, 2 * pad, LANE), F32),
        vm((RING, RING, part, LANE), F32),
        vm((2, 2 * part, LANE), F32),
        vm((2, DEPTH, share, LANE), F32),
        vm((2, share, LANE), F32),
        vm((2, 2 * part, LANE), F32),
        vm((RING, RING, 2 * pad, LANE), F32),
        vm((jrows, params), BF16),
        vm((pad, -(-rest // LANE) * LANE), F32),
        vm((DEPTH, RING, pad + GROUP, LANE), BF16),
        vm((2, RING, pad + GROUP, LANE), BF16),
        vm((RING, RING, 2 * pad, LANE), BF16),
        vm((RING, RING, 2, GROUP, LANE), BF16),
        vm((RING * RING, 2 * pad, LANE), BF16),
        vm((trades, 3 * LANE), BF16),
        vm((trades, 4 * pad), jnp.int32),
        vm((2, trades, 4 * pad), BF16),
        vm((trades, 2 * LANE), F32),
        vm((trades // 2, 2 * LANE), F32),
        vm((CHIPS, 2 * strip, LANE), BF16),
        vm((CHIPS, 2 * strip, LANE), BF16),
        dma((RING + 1,)), dma((RING + 1,)), dma((7,)),
        dma((RING, 6)), dma((RING, 6)),
        dma((RING, RING)), dma((RING,)),
        dma((2, DEPTH)), dma((2,)),
        dma((2, DEPTH)), dma((2,)),
        dma((RING, RING)), dma((RING,)),
        dma((RING, 6)), dma((RING, 6)),
        dma((DEPTH,)), dma((2, RING)), dma((3, 2)),
        dma((2, 6)), dma((2, 6)),
        dma((2,)), dma((2,)),
        dma((1,)), dma((1,)),
        pltpu.SemaphoreType.REGULAR((2,)),
    ]
    vmem = pl.BlockSpec(memory_space=pltpu.VMEM)
    hbm = pl.BlockSpec(memory_space=pl.ANY)
    return pl.pallas_call(
        kernel,
        out_shape=jax.ShapeDtypeStruct((strip, params), F32),
        in_specs=[hbm] * 7,
        out_specs=vmem,
        scratch_shapes=scratch,
        compiler_params=pltpu.CompilerParams(
            collective_id=0, has_side_effects=True, vmem_limit_bytes=56 * 1024 * 1024
        ),
    )(
        discounts,
        path_sens.T,
        cash_flows.T,
        flow_index.T,
        exercise_step.reshape(1, trades),
        trade_steps.reshape(1, trades),
        jacobian_inv,
    )


def solution(mesh):
    placed = (
        P(("grp", "path"), None),
        P(("grp", "path"), None),
        P("grp", None),
        P("grp", None),
        P("grp"),
        P("grp"),
        P("path", None),
    )
    return jax.shard_map(
        per_device, mesh=mesh, in_specs=placed, out_specs=P(("grp", "path"), None), check_vma=False
    )
```

```python
import jax
import jax.numpy as jnp
from jax import lax
from jax.experimental import pallas as pl
from jax.experimental.pallas import tpu as pltpu
from jax.sharding import PartitionSpec as P

NB = 40
LANE = 128
RING = 4
DEPTH = 8
CHIPS = RING * DEPTH
PATHS = 2 * CHIPS
GROUP = 16
F32 = jnp.float32
BF16 = jnp.bfloat16
MESH = pl.DeviceIdType.MESH


def kernel(
    disc, sens, cash, index, exer, steps, jac, out,
    dv, cv, iv, ev, sv, s_own, s_in, d_in, xs, xp, r1, y2, r2, zb, rz, zr, zf, xf,
    jv, je, jp, jz, jr, jx, jb, wt, room, mk, acc, pr, po, ob,
    ss_s, rs_s, ls, ss_1, rs_1, ss_2, rs_2, ss_z, rs_z, ss_g, rs_g,
    ss_a2, rs_a2, ss_a1, rs_a1, ss_j, ss_jx, rs_j, ss_ja, rs_ja, ss_p, rs_p, ss_o, rs_o, near_z,
):
    y = lax.axis_index("grp")
    me = lax.axis_index("path")
    j = lax.div(me, 2)
    c = lax.rem(me, 2)
    x = lax.div(j, DEPTH)
    z = lax.rem(j, DEPTH)
    sib = 1 - c
    params = sens.shape[0]
    width = params // NB
    half = params // 2
    jrows = jac.shape[0]
    pad = xp.shape[2] // 2
    trades = cash.shape[1]

    def at_chip(xx, zz, cc):
        return {"grp": y, "path": (xx * DEPTH + zz) * 2 + cc}

    def rdma(src, dst, ss, rs, dev):
        return pltpu.make_async_remote_copy(
            src_ref=src, dst_ref=dst, send_sem=ss, recv_sem=rs, device_id=dev, device_id_type=MESH
        )

    sent = []

    def send(*args):
        d = rdma(*args)
        d.start()
        sent.append((None, d))

    def send_if(cond, *args):
        d = rdma(*args)

        @pl.when(cond)
        def _():
            d.start()

        sent.append((cond, d))

    sibling = at_chip(x, z, sib)

    def on_x(k):
        return at_chip(lax.rem(x + k, RING), z, c)

    def on_y(k):
        return {"grp": lax.rem(y + k, RING), "path": me}

    def on_z(k):
        return at_chip(x, lax.rem(z + k, DEPTH), c)

    lines = ((x, on_x), (y, on_y))

    barrier = pltpu.get_barrier_semaphore()
    partners = [sibling] + [on(k) for on in (on_x, on_y) for k in (1, RING - 1)]
    partners += [on_z(k) for k in (1, DEPTH - 1, 2, DEPTH - 2)]
    for d in partners:
        pl.semaphore_signal(barrier, inc=1, device_id=d, device_id_type=MESH)

    fetched = [
        pltpu.make_async_copy(src, dst, ls.at[n])
        for n, (src, dst) in enumerate(
            (
                (disc, dv),
                (sens.at[pl.ds(pl.multiple_of(c * half, 16), half)], s_own),
                (cash, cv), (index, iv), (exer, ev), (steps, sv), (jac, jv),
            )
        )
    ]
    for f in fetched:
        f.start()

    first_cut = (half // 4 // 16 + 1) * 16
    cuts = (0, first_cut, half // 2, half // 2 + first_cut, half)

    def s_copy(q):
        n = cuts[q + 1] - cuts[q]
        return (
            sens.at[pl.ds(pl.multiple_of(sib * half + cuts[q], 16), n)],
            s_in.at[pl.ds(cuts[q], n)], ss_s.at[q], rs_s.at[q], sibling,
        )

    d_copy = (disc, d_in, ss_s.at[RING], rs_s.at[RING], sibling)

    xs[half : half + 8] = jnp.zeros((8, LANE), F32)
    for f in fetched[:2]:
        f.wait()
    third = half // 3

    @pl.loop(0, 3)
    def _(n):
        rws = pl.ds(pl.multiple_of(n * third, 16), third)
        xs[rws] = jnp.dot(s_own[rws], dv[...], preferred_element_type=F32)

    pl.semaphore_wait(barrier, len(partners))
    send(*d_copy)
    leading = [rdma(*s_copy(q)) for q in (0, 1)]
    for d in leading:
        d.start()
    for n, k in enumerate((2, DEPTH - 2)):
        pl.semaphore_signal(near_z.at[n], inc=1, device_id=on_z(k), device_id_type=MESH)

    main = CHIPS * LANE
    more = (params - main) // CHIPS
    groups = pad // GROUP
    turn = lax.rem(z, RING) == y
    core = lax.div(x, 2)
    high = lax.div(z, RING)
    for f in fetched[2:]:
        f.wait()

    @pl.when(turn)
    def _():
        jp[...] = jnp.zeros(jp.shape, BF16)

        @pl.loop(0, DEPTH)
        def _(zz):
            for t in range(RING):
                col = pl.multiple_of((zz * RING + t) * LANE, LANE)
                jp[zz, t, 0:jrows] = jv[:, pl.ds(col, LANE)]

        je[...] = jnp.zeros(je.shape, F32)
        je[0:jrows, 0 : params - main] = jv[:, main:params].astype(F32)
        for t in range(CHIPS):
            packed = [
                je[r * GROUP : (r + 1) * GROUP, t * more : (t + 1) * more] for r in range(groups)
            ]
            packed.append(jnp.zeros((GROUP, LANE - groups * more), F32))
            jp[t // RING, t % RING, pad : pad + GROUP] = jnp.concatenate(packed, axis=1).astype(BF16)

        pltpu.make_async_copy(jp.at[z], jz.at[high], rs_j.at[2, high]).start()

    def j_line(k):
        zz = lax.rem(z + k, DEPTH)
        return jp.at[zz], jz.at[high], ss_j.at[k], rs_j.at[2, high], on_z(k)

    def j_depth(*steps_):
        @pl.when(turn)
        def _():
            for k in steps_:
                rdma(*j_line(k)).start()

    j_depth(2, 6, 1, 7)

    def part_rows(n, size):
        return pl.ds(pl.multiple_of(n * size, 8), size)

    class Scatter:
        def __init__(self, q):
            self.q = q
            self.i, self.on = lines[q % 2]
            self.nr, self.far, self.nl = (lax.rem(self.i + k, RING) for k in (1, 2, 3))
            self.right, self.left = self.on(1), self.on(3)

        def msg(self, n, h, k, dev):
            q = self.q
            return (
                xp.at[q, k, h * pad : (h + 1) * pad], r1.at[q, n],
                ss_1.at[q, n], rs_1.at[q, n], dev,
            )

        def first(self):
            send(*self.msg(0, 0, self.far, self.right))
            send(*self.msg(2, 1, self.far, self.left))

        def near(self):
            send(*self.msg(3, 1, self.nr, self.right))
            send(*self.msg(1, 0, self.nl, self.left))

        def second(self):
            for h, n, k, dev in ((0, 0, self.nr, self.right), (1, 2, self.nl, self.left)):
                rdma(*self.msg(n, h, k, dev)).wait_recv()
                xp[self.q, k, h * pad : (h + 1) * pad] += r1[self.q, n]
                send(*self.msg(4 + h, h, k, dev))

        def result(self):
            for h, n in ((0, 1), (1, 3)):
                rdma(*self.msg(n, h, self.i, self.left)).wait_recv()
                rdma(*self.msg(4 + h, h, self.i, self.left)).wait_recv()
                rws = slice(h * pad, (h + 1) * pad)
                y2[self.q, rws] = xp[self.q, self.i, rws] + r1[self.q, n] + r1[self.q, 4 + h]

    one = [Scatter(q) for q in range(RING)]
    for q, d in enumerate(leading):
        d.wait_send()
        send(*s_copy(q + 2))
    rdma(*d_copy).wait_recv()
    for q in range(RING):
        rdma(*s_copy(q)).wait_recv()
        xs[cuts[q] : cuts[q + 1]] += jnp.dot(
            s_in[cuts[q] : cuts[q + 1]], d_in[...], preferred_element_type=F32
        )
        for k in range(RING):
            for u in (0, 1):
                top = (8 * q + 2 * k + u) * jrows
                xp[q, k, u * pad : (u + 1) * pad] = xs[top : top + pad]
        one[q].first()
        if q % 2:
            one[q - 1].near()
            one[q].near()

    for n in (0, 1):
        pl.semaphore_wait(near_z.at[n], 1)
    j_depth(4, 3, 5)
    one[0].second()
    one[1].second()
    one[2].second()
    one[3].second()

    def j_cross(e, k):
        xx = lax.rem(x + k, RING)
        two_ = pl.ds(2 * lax.rem(x, 2), 2)
        if e == 0:
            src = jz.at[:, xx, 0:pad]
            dst = jr.at[two_, y, pl.ds(pl.multiple_of(c * pad, 16), pad)]
        else:
            src = jz.at[:, xx, pad : pad + GROUP]
            dst = jx.at[two_, y, c]
        return src, dst, ss_jx.at[e, k], rs_j.at[e, 0], at_chip(xx, z, core)

    def both(f):
        f(0)
        f(1)

    def j_send(e):
        for k in (2, 1, 3):
            rdma(*j_cross(e, k)).start()
        src, dst, ss, rs, dev = j_cross(e, 0)

        @pl.when(core == c)
        def _():
            pltpu.make_async_copy(src, dst, rs).start()

        @pl.when(core != c)
        def _():
            rdma(src, dst, ss, rs, dev).start()


    part = y2.shape[1] // RING

    def two(q, k):
        i, on = lines[1 - q % 2]
        return (
            y2.at[q, part_rows(lax.rem(i + k, RING), part)], r2.at[q, i],
            ss_2.at[q, k], rs_2.at[q], on(k),
        )

    for g in (0, 1):
        for q in (2 * g, 2 * g + 1):
            one[q].result()
            for k in (2, 1, 3):
                send(*two(q, k))
    for n in (0, 1):
        pltpu.make_async_copy(jp.at[0], jz.at[n], rs_j.at[2, n]).wait()
    both(j_send)

    share = zr.shape[1]
    count = 2 * part // share
    spread = (4, 3, 5, 2, 6, 1, 7)

    def turn_of(g, d):
        return lax.rem(d + count * g, DEPTH)

    def reduces(g):
        return turn_of(g, z) < count

    def z_piece(g, d):
        return part_rows(jnp.minimum(turn_of(g, d), count - 1), share)

    for g in (0, 1):
        for p in (0, 1):
            q = 2 * g + p
            i, on = lines[1 - p]
            total = y2[q, part_rows(i, part)]
            three = r2.at[q, 0 : RING - 1]
            rdma(three, three, ss_2.at[q, 0], rs_2.at[q], sibling).wait_recv()
            for k in (1, 2, 3):
                total += r2[q, lax.rem(i + k, RING)]
            zb[g, p * part : (p + 1) * part] = total
        for k in spread:
            d = lax.rem(z + k, DEPTH)
            send_if(
                turn_of(g, d) < count,
                zb.at[g, z_piece(g, d)], rz.at[g, z], ss_z.at[g, k], rs_z.at[g], on_z(k),
            )


    def j_ring(half_, k, n, dev):
        ref = jr.at[pl.ds(2 * half_, 2), k]
        return ref, ref, ss_ja.at[0, n], rs_ja.at[0, n], dev

    def j_fan(k):
        ref = jx.at[:, y]
        return ref, ref, ss_ja.at[1, k], rs_ja.at[1, 0], on_y(k)

    yr, yl = on_y(1), on_y(3)
    ynr, yfar, ynl = (lax.rem(y + k, RING) for k in (1, 2, 3))

    def j_start():
        for e, whole in ((0, jr.at[:, y]), (1, jx.at[:, y])):
            pltpu.make_async_copy(whole, whole, rs_j.at[e, 0]).wait()
        for n, (hh, d) in enumerate(((0, yr), (1, yl), (1, yr), (0, yl))):
            send(*j_ring(hh, y, n, d))
        for k in (2, 1, 3):
            send(*j_fan(k))

    def j_forward():
        rdma(*j_ring(0, ynl, 0, yr)).wait_recv()
        send(*j_ring(0, ynl, 4, yr))
        rdma(*j_ring(1, ynr, 1, yl)).wait_recv()
        send(*j_ring(1, ynr, 5, yl))

    def j_finish():
        for hh, k, n, d in ((1, ynl, 2, yr), (0, ynr, 3, yl), (0, yfar, 4, yr), (1, yfar, 5, yl)):
            rdma(*j_ring(hh, k, n, d)).wait_recv()

    def j_unpack():
        three = jx.at[0 : RING - 1]
        rdma(three, three, ss_ja.at[1, 0], rs_ja.at[1, 0], sibling).wait_recv()

        @pl.loop(0, RING * RING)
        def _(n):
            q, k = lax.div(n, RING), lax.rem(n, RING)
            for u in (0, 1):
                tile = jx[q, k, u].astype(F32)
                for r in range(groups):
                    at = u * pad + r * GROUP
                    turned_ = tile if r == 0 else pltpu.roll(tile, LANE - r * more, 1)
                    jb[n, at : at + GROUP] = turned_.astype(BF16)

    j_start()

    for g in (0, 1):
        reducer = reduces(g)

        @pl.when(reducer)
        def _():
            total = zb[g, z_piece(g, z)]
            seven = rz.at[g, 0 : DEPTH - 1]
            rdma(seven, seven, ss_z.at[g, 0], rs_z.at[g], sibling).wait_recv()
            for k in range(1, DEPTH):
                total += rz[g, lax.rem(z + k, DEPTH)]
            zr[g] = total
            zf[g, z_piece(g, z)] = total

        for k in spread:
            send_if(
                reducer, zr.at[g], zf.at[g, z_piece(g, z)], ss_g.at[g, k], rs_g.at[g], on_z(k)
            )


    slots = cash.shape[0]
    forwards = lax.broadcasted_iota(jnp.int32, (LANE, trades), 0)
    late = forwards >= ev[...]
    weights = jnp.zeros((LANE, trades), F32)
    for s in range(slots):
        weights += jnp.where(late & (iv[s : s + 1] == forwards), cv[s : s + 1], 0.0)
    weights = weights * (1.0 / (disc.shape[0] * PATHS * RING))
    weights = weights.T
    w_hi = weights.astype(BF16)
    w_lo = (weights - w_hi.astype(F32)).astype(BF16)
    wt[...] = jnp.concatenate([w_hi, w_hi, w_lo], axis=1)
    reach = jnp.broadcast_to((sv[...] * width).astype(F32), (LANE, trades)).T.astype(jnp.int32)
    span = 4 * pad
    lane = lax.broadcasted_iota(jnp.int32, (trades, span), 1)
    lane = lane - jnp.where(lane >= 2 * pad, 2 * pad, 0)
    room[...] = (
        jnp.concatenate([reach] * (span // LANE) + [reach[:, : span % LANE]], axis=1)
        - lane + jnp.where(lane >= pad, pad - jrows, 0) - c * half
    )

    def home(q, i):
        return xf.at[q, lines[q % 2][0], part_rows(i, part)]

    for g in (0, 1):
        for some, ref in ((reduces(g), zf.at[g, 0 : (count - 1) * share]), (~reduces(g), zf.at[g])):

            @pl.when(some)
            def _():
                rdma(ref, ref, ss_g.at[g, 0], rs_g.at[g], sibling).wait_recv()

        for p in (0, 1):
            q = 2 * g + p
            i, on = lines[1 - p]
            mine = zf.at[g, p * part : (p + 1) * part]
            for k in (2, 1, 3):
                send(mine, home(q, i), ss_a2.at[q, k], rs_a2.at[q], on(k))
            home(q, i)[...] = mine[...]

    def all_left():
        while sent:
            cond, d = sent.pop()
            if cond is None:
                d.wait_send()
            else:
                pl.when(cond)(d.wait_send)

    later = sent[-4 * (RING - 1):]
    del sent[-len(later) :]
    all_left()
    sent.extend(later)
    j_forward()
    j_unpack()

    class Gather:
        def __init__(self, q):
            self.q = q
            self.i, self.on = lines[q % 2]
            self.nr, self.far, self.nl = (lax.rem(self.i + k, RING) for k in (1, 2, 3))
            self.right, self.left = self.on(1), self.on(3)

        def msg(self, n, h, k, dev):
            ref = xf.at[self.q, k, h * pad : (h + 1) * pad]
            return ref, ref, ss_a1.at[self.q, n], rs_a1.at[self.q, n], dev

        def start(self):
            q = self.q
            three = xf.at[q, 0, 0 : (RING - 1) * part]
            rdma(three, three, ss_a2.at[q, 0], rs_a2.at[q], sibling).wait_recv()
            send(*self.msg(0, 0, self.i, self.right))
            send(*self.msg(1, 1, self.i, self.left))
            send(*self.msg(2, 1, self.i, self.right))
            send(*self.msg(3, 0, self.i, self.left))

        def forward(self):
            rdma(*self.msg(0, 0, self.nl, self.right)).wait_recv()
            send(*self.msg(4, 0, self.nl, self.right))
            rdma(*self.msg(1, 1, self.nr, self.left)).wait_recv()
            send(*self.msg(5, 1, self.nr, self.left))

    ring = [Gather(q) for q in range(RING)]
    for q in range(RING):
        ring[q].start()

    acc[...] = jnp.zeros(acc.shape, F32)

    second_lane = lax.broadcasted_iota(jnp.int32, (1, span), 1) >= 2 * pad

    def mask(*both_):
        values = jnp.concatenate([xf[q, k] for q, k in both_], axis=0)
        hi = values.astype(BF16)
        lo = (values - hi.astype(F32)).astype(BF16)
        vega = lax.dot_general(
            wt[...], jnp.concatenate([hi, lo, hi], axis=1), (((1,), (1,)), ((), ())),
            preferred_element_type=F32,
        )
        start = [(8 * q + 2 * k) * jrows for q, k in both_]
        keep = room[...] > jnp.where(second_lane, start[1], start[0])
        return jnp.where(keep, vega, 0.0).astype(BF16)

    def add(masked, *both_):
        columns = [
            jnp.concatenate([jr[q, k], jb[RING * q + k]], axis=1) for q, k in both_
        ]
        acc[...] += jnp.dot(
            masked, jnp.concatenate(columns, axis=0), preferred_element_type=F32
        )

    def pair(*both_):
        add(mask(*both_), *both_)

    def landed(q, k, h, n):
        ref = xf.at[q, k, h * pad : (h + 1) * pad]
        rdma(ref, ref, ss_a1.at[q, n], rs_a1.at[q, n], sibling).wait_recv()

    def ring_place(q, step):
        return lax.rem(jnp.where(lax.rem(q, 2) == 0, x, y) + step, RING)

    mine = lambda g: ((2 * g, x), (2 * g + 1, y))

    @pl.loop(0, 2)
    def _(g):
        mk[g] = mask(*mine(g))

    for r in ring:
        r.forward()
    j_finish()

    @pl.loop(0, 2)
    def _(g):
        add(mk[g], *mine(g))

    @pl.loop(0, RING)
    def _(q):
        nl, nr = ring_place(q, 3), ring_place(q, 1)
        landed(q, nl, 1, 2)
        landed(q, nr, 0, 3)
        pair((q, nl), (q, nr))

    far_x, far_y = ring[0].far, ring[1].far

    @pl.loop(0, 2)
    def _(g):
        for q, k in ((2 * g, far_x), (2 * g + 1, far_y)):
            landed(q, k, 0, 4)
            landed(q, k, 1, 5)
        pair((2 * g, far_x), (2 * g + 1, far_y))

    strip_rows = out.shape[0]
    side_rows = trades // 4

    def side_of(half_, side):
        return pl.ds(pl.multiple_of((2 * half_ + side) * side_rows, 8), side_rows)

    swaps = [
        (acc.at[side_of(sib, n)], pr.at[n], ss_p.at[n], rs_p.at[n], sibling) for n in (0, 1)
    ]
    for swap in swaps:
        send(*swap)

    tile = ob.at[z * RING + x]

    def deliver(n, dst):
        rdma(po.at[n], tile, ss_o.at[0], rs_o.at[0], {"grp": y, "path": dst}).start()

    for side in (0, 1):
        rdma(*swaps[side]).wait_recv()
        total = acc[side_of(c, side)] + pr[side]
        po[side * 2 * DEPTH : (side + 1) * 2 * DEPTH] = jnp.concatenate(
            [
                total[:, h * LANE : (h + 1) * LANE].reshape(2 * DEPTH, strip_rows, LANE)
                for h in (0, 1)
            ],
            axis=1,
        ).astype(BF16)
        for k in (4, 3, 5, 2, 6, 1, 7, 0):
            zz = lax.rem(z + k, DEPTH)
            for u in (0, 1):
                n = side * 2 * DEPTH + 2 * zz + u
                dst = c * CHIPS + n
                if k:
                    deliver(n, dst)
                else:
                    pl.when(dst != me)(lambda n=n, dst=dst: deliver(n, dst))

                    @pl.when(dst == me)
                    def _():
                        pltpu.make_async_copy(po.at[n], tile, rs_o.at[0]).start()

    all_left()

    def j_crossed(e):
        for k in (1, 2, 3):
            rdma(*j_cross(e, k)).wait_send()

        @pl.when(core != c)
        def _():
            rdma(*j_cross(e, 0)).wait_send()

    both(j_crossed)

    @pl.when(turn)
    def _():
        for k in range(1, DEPTH):
            rdma(*j_line(k)).wait_send()

    pltpu.make_async_copy(ob, ob, rs_o.at[0]).wait()

    rest = []
    for t in range(CHIPS):
        tile = ob[t].astype(F32)
        out[:, t * LANE : (t + 1) * LANE] = tile[0:strip_rows]
        rest.append(tile[strip_rows : 2 * strip_rows, 0:more])
    out[:, main:params] = jnp.concatenate(rest, axis=1)

    def po_sent(n):
        rdma(po.at[0:n], po.at[0:n], ss_o.at[0], rs_o.at[0], sibling).wait_send()

    pl.when(core == c)(lambda: po_sent(CHIPS - 1))
    pl.when(core != c)(lambda: po_sent(CHIPS))


def per_device(
    path_sens, discounts, cash_flows, flow_index, exercise_step, trade_steps, jacobian_inv
):
    paths_own, params = path_sens.shape
    trades = cash_flows.shape[0]
    jrows = jacobian_inv.shape[0]
    strip = trades // PATHS
    rest = params - CHIPS * LANE
    pad = -(-jrows // 16) * 16
    half = params // 2
    slots = cash_flows.shape[1]
    part = pad // 2
    share = 16
    vm = pltpu.VMEM
    dma = pltpu.SemaphoreType.DMA
    scratch = [
        vm((paths_own, LANE), BF16),
        vm((slots, trades), F32),
        vm((slots, trades), jnp.int32),
        vm((1, trades), jnp.int32),
        vm((1, trades), jnp.int32),
        vm((half, paths_own), BF16),
        vm((half, paths_own), BF16),
        vm((paths_own, LANE), BF16),
        vm((half + 8, LANE), F32),
        vm((RING, RING, 2 * pad, LANE), F32),
        vm((RING, 6, pad, LANE), F32),
        vm((RING, 2 * pad, LANE), F32),
        vm((RING, RING, part, LANE), F32),
        vm((2, 2 * part, LANE), F32),
        vm((2, DEPTH, share, LANE), F32),
        vm((2, share, LANE), F32),
        vm((2, 2 * part, LANE), F32),
        vm((RING, RING, 2 * pad, LANE), F32),
        vm((jrows, params), BF16),
        vm((pad, -(-rest // LANE) * LANE), F32),
        vm((DEPTH, RING, pad + GROUP, LANE), BF16),
        vm((2, RING, pad + GROUP, LANE), BF16),
        vm((RING, RING, 2 * pad, LANE), BF16),
        vm((RING, RING, 2, GROUP, LANE), BF16),
        vm((RING * RING, 2 * pad, LANE), BF16),
        vm((trades, 3 * LANE), BF16),
        vm((trades, 4 * pad), jnp.int32),
        vm((2, trades, 4 * pad), BF16),
        vm((trades, 2 * LANE), F32),
        vm((2, trades // 4, 2 * LANE), F32),
        vm((CHIPS, 2 * strip, LANE), BF16),
        vm((CHIPS, 2 * strip, LANE), BF16),
        dma((RING + 1,)), dma((RING + 1,)), dma((7,)),
        dma((RING, 6)), dma((RING, 6)),
        dma((RING, RING)), dma((RING,)),
        dma((2, DEPTH)), dma((2,)),
        dma((2, DEPTH)), dma((2,)),
        dma((RING, RING)), dma((RING,)),
        dma((RING, 6)), dma((RING, 6)),
        dma((DEPTH,)), dma((2, RING)), dma((3, 2)),
        dma((2, 6)), dma((2, 6)),
        dma((2,)), dma((2,)),
        dma((1,)), dma((1,)),
        pltpu.SemaphoreType.REGULAR((2,)),
    ]
    vmem = pl.BlockSpec(memory_space=pltpu.VMEM)
    hbm = pl.BlockSpec(memory_space=pl.ANY)
    return pl.pallas_call(
        kernel,
        out_shape=jax.ShapeDtypeStruct((strip, params), F32),
        in_specs=[hbm] * 7,
        out_specs=vmem,
        scratch_shapes=scratch,
        compiler_params=pltpu.CompilerParams(
            collective_id=0, has_side_effects=True, vmem_limit_bytes=56 * 1024 * 1024
        ),
    )(
        discounts,
        path_sens.T,
        cash_flows.T,
        flow_index.T,
        exercise_step.reshape(1, trades),
        trade_steps.reshape(1, trades),
        jacobian_inv,
    )


def solution(mesh):
    placed = (
        P(("grp", "path"), None),
        P(("grp", "path"), None),
        P("grp", None),
        P("grp", None),
        P("grp"),
        P("grp"),
        P("path", None),
    )
    return jax.shard_map(
        per_device, mesh=mesh, in_specs=placed, out_specs=P(("grp", "path"), None), check_vma=False
    )
```

```python
import jax
import jax.numpy as jnp
from jax import lax
from jax.experimental import pallas as pl
from jax.experimental.pallas import tpu as pltpu
from jax.sharding import PartitionSpec as P

NB = 40
LANE = 128
RING = 4
DEPTH = 8
CHIPS = RING * DEPTH
PATHS = 2 * CHIPS
GROUP = 16
F32 = jnp.float32
BF16 = jnp.bfloat16
MESH = pl.DeviceIdType.MESH


def kernel(
    disc, sens, cash, index, exer, steps, jac, out,
    dv, cv, iv, ev, sv, s_own, s_in, d_in, xs, xp, r1, y2, r2, zb, rz, zr, zf, xf,
    jv, je, jp, jz, jr, jx, jb, wt, room, mk, acc, pr, po, ob,
    ss_s, rs_s, ls, ss_1, rs_1, ss_2, rs_2, ss_z, rs_z, ss_g, rs_g,
    ss_a2, rs_a2, ss_a1, rs_a1, ss_j, ss_jx, rs_j, ss_ja, rs_ja, ss_p, rs_p, ss_o, rs_o, near_z,
):
    y = lax.axis_index("grp")
    me = lax.axis_index("path")
    j = lax.div(me, 2)
    c = lax.rem(me, 2)
    x = lax.div(j, DEPTH)
    z = lax.rem(j, DEPTH)
    sib = 1 - c
    params = sens.shape[0]
    width = params // NB
    half = params // 2
    jrows = jac.shape[0]
    pad = xp.shape[2] // 2
    trades = cash.shape[1]

    def at_chip(xx, zz, cc):
        return {"grp": y, "path": (xx * DEPTH + zz) * 2 + cc}

    def rdma(src, dst, ss, rs, dev):
        return pltpu.make_async_remote_copy(
            src_ref=src, dst_ref=dst, send_sem=ss, recv_sem=rs, device_id=dev, device_id_type=MESH
        )

    sent = []

    def send(*args):
        d = rdma(*args)
        d.start()
        sent.append((None, d))

    def send_if(cond, *args):
        d = rdma(*args)

        @pl.when(cond)
        def _():
            d.start()

        sent.append((cond, d))

    sibling = at_chip(x, z, sib)

    def on_x(k):
        return at_chip(lax.rem(x + k, RING), z, c)

    def on_y(k):
        return {"grp": lax.rem(y + k, RING), "path": me}

    def on_z(k):
        return at_chip(x, lax.rem(z + k, DEPTH), c)

    lines = ((x, on_x), (y, on_y))

    barrier = pltpu.get_barrier_semaphore()
    partners = [sibling] + [on(k) for on in (on_x, on_y) for k in (1, RING - 1)]
    partners += [on_z(k) for k in (1, DEPTH - 1, 2, DEPTH - 2)]
    for d in partners:
        pl.semaphore_signal(barrier, inc=1, device_id=d, device_id_type=MESH)

    fetched = [
        pltpu.make_async_copy(src, dst, ls.at[n])
        for n, (src, dst) in enumerate(
            (
                (disc, dv),
                (sens.at[pl.ds(pl.multiple_of(c * half, 16), half)], s_own),
                (cash, cv), (index, iv), (exer, ev), (steps, sv), (jac, jv),
            )
        )
    ]
    for f in fetched:
        f.start()

    first_cut = (half // 4 // 16 + 1) * 16
    cuts = (0, first_cut, half // 2, half // 2 + first_cut, half)

    def s_copy(q):
        n = cuts[q + 1] - cuts[q]
        return (
            sens.at[pl.ds(pl.multiple_of(sib * half + cuts[q], 16), n)],
            s_in.at[pl.ds(cuts[q], n)], ss_s.at[q], rs_s.at[q], sibling,
        )

    d_copy = (disc, d_in, ss_s.at[RING], rs_s.at[RING], sibling)

    xs[half : half + 8] = jnp.zeros((8, LANE), F32)
    for f in fetched[:2]:
        f.wait()
    third = half // 3

    @pl.loop(0, 3)
    def _(n):
        rws = pl.ds(pl.multiple_of(n * third, 16), third)
        xs[rws] = jnp.dot(s_own[rws], dv[...], preferred_element_type=F32)

    pl.semaphore_wait(barrier, len(partners))
    send(*d_copy)
    leading = [rdma(*s_copy(q)) for q in (0, 1)]
    for d in leading:
        d.start()
    for n, k in enumerate((2, DEPTH - 2)):
        pl.semaphore_signal(near_z.at[n], inc=1, device_id=on_z(k), device_id_type=MESH)

    main = CHIPS * LANE
    more = (params - main) // CHIPS
    groups = pad // GROUP
    turn = lax.rem(z, RING) == y
    core = lax.div(x, 2)
    high = lax.div(z, RING)
    for f in fetched[2:]:
        f.wait()

    @pl.when(turn)
    def _():
        jp[...] = jnp.zeros(jp.shape, BF16)

        @pl.loop(0, DEPTH)
        def _(zz):
            for t in range(RING):
                col = pl.multiple_of((zz * RING + t) * LANE, LANE)
                jp[zz, t, 0:jrows] = jv[:, pl.ds(col, LANE)]

        je[...] = jnp.zeros(je.shape, F32)
        je[0:jrows, 0 : params - main] = jv[:, main:params].astype(F32)
        for t in range(CHIPS):
            packed = [
                je[r * GROUP : (r + 1) * GROUP, t * more : (t + 1) * more] for r in range(groups)
            ]
            packed.append(jnp.zeros((GROUP, LANE - groups * more), F32))
            jp[t // RING, t % RING, pad : pad + GROUP] = jnp.concatenate(packed, axis=1).astype(BF16)

        pltpu.make_async_copy(jp.at[z], jz.at[high], rs_j.at[2, high]).start()

    def j_line(k):
        zz = lax.rem(z + k, DEPTH)
        return jp.at[zz], jz.at[high], ss_j.at[k], rs_j.at[2, high], on_z(k)

    def j_depth(*steps_):
        @pl.when(turn)
        def _():
            for k in steps_:
                rdma(*j_line(k)).start()

    j_depth(2, 6, 1, 7)

    def part_rows(n, size):
        return pl.ds(pl.multiple_of(n * size, 8), size)

    class Scatter:
        def __init__(self, q):
            self.q = q
            self.i, self.on = lines[q % 2]
            self.nr, self.far, self.nl = (lax.rem(self.i + k, RING) for k in (1, 2, 3))
            self.right, self.left = self.on(1), self.on(3)

        def msg(self, n, h, k, dev):
            q = self.q
            return (
                xp.at[q, k, h * pad : (h + 1) * pad], r1.at[q, n],
                ss_1.at[q, n], rs_1.at[q, n], dev,
            )

        def first(self):
            send(*self.msg(0, 0, self.far, self.right))
            send(*self.msg(2, 1, self.far, self.left))

        def near(self):
            send(*self.msg(3, 1, self.nr, self.right))
            send(*self.msg(1, 0, self.nl, self.left))

        def second(self):
            for h, n, k, dev in ((0, 0, self.nr, self.right), (1, 2, self.nl, self.left)):
                rdma(*self.msg(n, h, k, dev)).wait_recv()
                xp[self.q, k, h * pad : (h + 1) * pad] += r1[self.q, n]
                send(*self.msg(4 + h, h, k, dev))

        def result(self):
            for h, n in ((0, 1), (1, 3)):
                rdma(*self.msg(n, h, self.i, self.left)).wait_recv()
                rdma(*self.msg(4 + h, h, self.i, self.left)).wait_recv()
                rws = slice(h * pad, (h + 1) * pad)
                y2[self.q, rws] = xp[self.q, self.i, rws] + r1[self.q, n] + r1[self.q, 4 + h]

    one = [Scatter(q) for q in range(RING)]
    for q, d in enumerate(leading):
        d.wait_send()
        send(*s_copy(q + 2))
    rdma(*d_copy).wait_recv()
    for q in range(RING):
        rdma(*s_copy(q)).wait_recv()
        xs[cuts[q] : cuts[q + 1]] += jnp.dot(
            s_in[cuts[q] : cuts[q + 1]], d_in[...], preferred_element_type=F32
        )
        for k in range(RING):
            for u in (0, 1):
                top = (8 * q + 2 * k + u) * jrows
                xp[q, k, u * pad : (u + 1) * pad] = xs[top : top + pad]
        one[q].first()
    for r in one:
        r.near()

    for n in (0, 1):
        pl.semaphore_wait(near_z.at[n], 1)
    j_depth(4, 3, 5)
    one[0].second()
    one[1].second()
    one[2].second()
    one[3].second()

    def j_cross(e, k):
        xx = lax.rem(x + k, RING)
        two_ = pl.ds(2 * lax.rem(x, 2), 2)
        if e == 0:
            src = jz.at[:, xx, 0:pad]
            dst = jr.at[two_, y, pl.ds(pl.multiple_of(c * pad, 16), pad)]
        else:
            src = jz.at[:, xx, pad : pad + GROUP]
            dst = jx.at[two_, y, c]
        return src, dst, ss_jx.at[e, k], rs_j.at[e, 0], at_chip(xx, z, core)

    def both(f):
        f(0)
        f(1)

    def j_send(e):
        for k in (2, 1, 3):
            rdma(*j_cross(e, k)).start()
        src, dst, ss, rs, dev = j_cross(e, 0)

        @pl.when(core == c)
        def _():
            pltpu.make_async_copy(src, dst, rs).start()

        @pl.when(core != c)
        def _():
            rdma(src, dst, ss, rs, dev).start()


    part = y2.shape[1] // RING

    def two(q, k):
        i, on = lines[1 - q % 2]
        return (
            y2.at[q, part_rows(lax.rem(i + k, RING), part)], r2.at[q, i],
            ss_2.at[q, k], rs_2.at[q], on(k),
        )

    for g in (0, 1):
        for q in (2 * g, 2 * g + 1):
            one[q].result()
            for k in (2, 1, 3):
                send(*two(q, k))
    for n in (0, 1):
        pltpu.make_async_copy(jp.at[0], jz.at[n], rs_j.at[2, n]).wait()
    both(j_send)

    share = zr.shape[1]
    count = 2 * part // share
    spread = (4, 3, 5, 2, 6, 1, 7)

    def turn_of(g, d):
        return lax.rem(d + count * g, DEPTH)

    def reduces(g):
        return turn_of(g, z) < count

    def z_piece(g, d):
        return part_rows(jnp.minimum(turn_of(g, d), count - 1), share)

    for g in (0, 1):
        for p in (0, 1):
            q = 2 * g + p
            i, on = lines[1 - p]
            total = y2[q, part_rows(i, part)]
            three = r2.at[q, 0 : RING - 1]
            rdma(three, three, ss_2.at[q, 0], rs_2.at[q], sibling).wait_recv()
            for k in (1, 2, 3):
                total += r2[q, lax.rem(i + k, RING)]
            zb[g, p * part : (p + 1) * part] = total
        for k in spread:
            d = lax.rem(z + k, DEPTH)
            send_if(
                turn_of(g, d) < count,
                zb.at[g, z_piece(g, d)], rz.at[g, z], ss_z.at[g, k], rs_z.at[g], on_z(k),
            )


    def j_ring(half_, k, n, dev):
        ref = jr.at[pl.ds(2 * half_, 2), k]
        return ref, ref, ss_ja.at[0, n], rs_ja.at[0, n], dev

    def j_fan(k):
        ref = jx.at[:, y]
        return ref, ref, ss_ja.at[1, k], rs_ja.at[1, 0], on_y(k)

    yr, yl = on_y(1), on_y(3)
    ynr, yfar, ynl = (lax.rem(y + k, RING) for k in (1, 2, 3))

    def j_start():
        for e, whole in ((0, jr.at[:, y]), (1, jx.at[:, y])):
            pltpu.make_async_copy(whole, whole, rs_j.at[e, 0]).wait()
        for n, (hh, d) in enumerate(((0, yr), (1, yl), (1, yr), (0, yl))):
            send(*j_ring(hh, y, n, d))
        for k in (2, 1, 3):
            send(*j_fan(k))

    def j_forward():
        rdma(*j_ring(0, ynl, 0, yr)).wait_recv()
        send(*j_ring(0, ynl, 4, yr))
        rdma(*j_ring(1, ynr, 1, yl)).wait_recv()
        send(*j_ring(1, ynr, 5, yl))

    def j_finish():
        for hh, k, n, d in ((1, ynl, 2, yr), (0, ynr, 3, yl), (0, yfar, 4, yr), (1, yfar, 5, yl)):
            rdma(*j_ring(hh, k, n, d)).wait_recv()

    def j_unpack():
        three = jx.at[0 : RING - 1]
        rdma(three, three, ss_ja.at[1, 0], rs_ja.at[1, 0], sibling).wait_recv()

        @pl.loop(0, RING * RING)
        def _(n):
            q, k = lax.div(n, RING), lax.rem(n, RING)
            for u in (0, 1):
                tile = jx[q, k, u].astype(F32)
                for r in range(groups):
                    at = u * pad + r * GROUP
                    turned_ = tile if r == 0 else pltpu.roll(tile, LANE - r * more, 1)
                    jb[n, at : at + GROUP] = turned_.astype(BF16)

    j_start()

    for g in (0, 1):
        reducer = reduces(g)

        @pl.when(reducer)
        def _():
            total = zb[g, z_piece(g, z)]
            seven = rz.at[g, 0 : DEPTH - 1]
            rdma(seven, seven, ss_z.at[g, 0], rs_z.at[g], sibling).wait_recv()
            for k in range(1, DEPTH):
                total += rz[g, lax.rem(z + k, DEPTH)]
            zr[g] = total
            zf[g, z_piece(g, z)] = total

        for k in spread:
            send_if(
                reducer, zr.at[g], zf.at[g, z_piece(g, z)], ss_g.at[g, k], rs_g.at[g], on_z(k)
            )


    slots = cash.shape[0]
    forwards = lax.broadcasted_iota(jnp.int32, (LANE, trades), 0)
    late = forwards >= ev[...]
    weights = jnp.zeros((LANE, trades), F32)
    for s in range(slots):
        weights += jnp.where(late & (iv[s : s + 1] == forwards), cv[s : s + 1], 0.0)
    weights = weights * (1.0 / (disc.shape[0] * PATHS * RING))
    weights = weights.T
    w_hi = weights.astype(BF16)
    w_lo = (weights - w_hi.astype(F32)).astype(BF16)
    wt[...] = jnp.concatenate([w_hi, w_hi, w_lo], axis=1)
    reach = jnp.broadcast_to((sv[...] * width).astype(F32), (LANE, trades)).T.astype(jnp.int32)
    span = room.shape[1]
    lane = lax.broadcasted_iota(jnp.int32, (trades, span), 1)
    lane = lax.rem(lane, 2 * pad)
    room[...] = (
        jnp.concatenate([reach] * (span // LANE), axis=1)
        - lane + jnp.where(lane >= pad, pad - jrows, 0) - c * half
    )

    def home(q, i):
        return xf.at[q, lines[q % 2][0], part_rows(i, part)]

    for g in (0, 1):
        for some, ref in ((reduces(g), zf.at[g, 0 : (count - 1) * share]), (~reduces(g), zf.at[g])):

            @pl.when(some)
            def _():
                rdma(ref, ref, ss_g.at[g, 0], rs_g.at[g], sibling).wait_recv()

        for p in (0, 1):
            q = 2 * g + p
            i, on = lines[1 - p]
            mine = zf.at[g, p * part : (p + 1) * part]
            for k in (2, 1, 3):
                send(mine, home(q, i), ss_a2.at[q, k], rs_a2.at[q], on(k))
            home(q, i)[...] = mine[...]

    def all_left():
        while sent:
            cond, d = sent.pop()
            if cond is None:
                d.wait_send()
            else:
                pl.when(cond)(d.wait_send)

    later = sent[-4 * (RING - 1):]
    del sent[-len(later) :]
    all_left()
    sent.extend(later)
    j_forward()
    j_unpack()

    class Gather:
        def __init__(self, q):
            self.q = q
            self.i, self.on = lines[q % 2]
            self.nr, self.far, self.nl = (lax.rem(self.i + k, RING) for k in (1, 2, 3))
            self.right, self.left = self.on(1), self.on(3)

        def msg(self, n, h, k, dev):
            ref = xf.at[self.q, k, h * pad : (h + 1) * pad]
            return ref, ref, ss_a1.at[self.q, n], rs_a1.at[self.q, n], dev

        def start(self):
            q = self.q
            three = xf.at[q, 0, 0 : (RING - 1) * part]
            rdma(three, three, ss_a2.at[q, 0], rs_a2.at[q], sibling).wait_recv()
            send(*self.msg(0, 0, self.i, self.right))
            send(*self.msg(1, 1, self.i, self.left))
            send(*self.msg(2, 1, self.i, self.right))
            send(*self.msg(3, 0, self.i, self.left))

        def forward(self):
            rdma(*self.msg(0, 0, self.nl, self.right)).wait_recv()
            send(*self.msg(4, 0, self.nl, self.right))
            rdma(*self.msg(1, 1, self.nr, self.left)).wait_recv()
            send(*self.msg(5, 1, self.nr, self.left))

    ring = [Gather(q) for q in range(RING)]
    for q in range(RING):
        ring[q].start()

    acc[...] = jnp.zeros(acc.shape, F32)


    def mask(*both_):
        values = jnp.concatenate([xf[q, k] for q, k in both_], axis=0)
        hi = values.astype(BF16)
        lo = (values - hi.astype(F32)).astype(BF16)
        vega = lax.dot_general(
            wt[...], jnp.concatenate([hi, lo, hi], axis=1), (((1,), (1,)), ((), ())),
            preferred_element_type=F32,
        )
        wide_ = len(both_) * 2 * pad
        lanes = lax.broadcasted_iota(jnp.int32, (1, wide_), 1)
        start = jnp.zeros((1, wide_), jnp.int32)
        for n, (q, k) in enumerate(both_):
            start = jnp.where(lanes >= n * 2 * pad, (8 * q + 2 * k) * jrows, start)
        keep = room[:, 0:wide_] > start
        return jnp.where(keep, vega, 0.0).astype(BF16)

    def add(masked, *both_):
        columns = [
            jnp.concatenate([jr[q, k], jb[RING * q + k]], axis=1) for q, k in both_
        ]
        acc[...] += jnp.dot(
            masked, jnp.concatenate(columns, axis=0), preferred_element_type=F32
        )

    def pair(*both_):
        add(mask(*both_), *both_)

    def landed(q, k, h, n):
        ref = xf.at[q, k, h * pad : (h + 1) * pad]
        rdma(ref, ref, ss_a1.at[q, n], rs_a1.at[q, n], sibling).wait_recv()

    mine = lambda g: ((2 * g, x), (2 * g + 1, y))

    @pl.loop(0, 2)
    def _(g):
        mk[g] = mask(*mine(g))

    for r in ring:
        r.forward()
    j_finish()

    @pl.loop(0, 2)
    def _(g):
        add(mk[g], *mine(g))

    @pl.loop(0, 2)
    def _(g):
        blocks = []
        for p in (0, 1):
            q = 2 * g + p
            landed(q, ring[p].nl, 1, 2)
            landed(q, ring[p].nr, 0, 3)
            blocks += [(q, ring[p].nl), (q, ring[p].nr)]
        pair(*blocks)

    far_x, far_y = ring[0].far, ring[1].far

    @pl.loop(0, 2)
    def _(g):
        for q, k in ((2 * g, far_x), (2 * g + 1, far_y)):
            landed(q, k, 0, 4)
            landed(q, k, 1, 5)
        pair((2 * g, far_x), (2 * g + 1, far_y))

    rows_c = pl.ds(pl.multiple_of(c * (trades // 2), 8), trades // 2)
    rows_sib = pl.ds(pl.multiple_of(sib * (trades // 2), 8), trades // 2)
    swap = (acc.at[rows_sib], pr, ss_p.at[0], rs_p.at[0], sibling)
    send(*swap)
    strip_rows = out.shape[0]
    rdma(*swap).wait_recv()
    total = acc[rows_c] + pr[...]
    po[...] = jnp.concatenate(
        [total[:, s * LANE : (s + 1) * LANE].reshape(CHIPS, strip_rows, LANE) for s in (0, 1)], axis=1
    ).astype(BF16)

    tile = ob.at[z * RING + x]

    def deliver(n, dst):
        rdma(po.at[n], tile, ss_o.at[0], rs_o.at[0], {"grp": y, "path": dst}).start()

    for k in (4, 3, 5, 2, 6, 1, 7, 0):
        zz = lax.rem(z + k, DEPTH)
        for side in (0, 1):
            for u in (0, 1):
                n = side * 2 * DEPTH + 2 * zz + u
                dst = c * CHIPS + n
                if k:
                    deliver(n, dst)
                else:
                    pl.when(dst != me)(lambda n=n, dst=dst: deliver(n, dst))

                    @pl.when(dst == me)
                    def _():
                        pltpu.make_async_copy(po.at[n], tile, rs_o.at[0]).start()

    all_left()

    def j_crossed(e):
        for k in (1, 2, 3):
            rdma(*j_cross(e, k)).wait_send()

        @pl.when(core != c)
        def _():
            rdma(*j_cross(e, 0)).wait_send()

    both(j_crossed)

    @pl.when(turn)
    def _():
        for k in range(1, DEPTH):
            rdma(*j_line(k)).wait_send()

    pltpu.make_async_copy(ob, ob, rs_o.at[0]).wait()

    rest = []
    for t in range(CHIPS):
        tile = ob[t].astype(F32)
        out[:, t * LANE : (t + 1) * LANE] = tile[0:strip_rows]
        rest.append(tile[strip_rows : 2 * strip_rows, 0:more])
    out[:, main:params] = jnp.concatenate(rest, axis=1)

    def po_sent(n):
        rdma(po.at[0:n], po.at[0:n], ss_o.at[0], rs_o.at[0], sibling).wait_send()

    pl.when(core == c)(lambda: po_sent(CHIPS - 1))
    pl.when(core != c)(lambda: po_sent(CHIPS))


def per_device(
    path_sens, discounts, cash_flows, flow_index, exercise_step, trade_steps, jacobian_inv
):
    paths_own, params = path_sens.shape
    trades = cash_flows.shape[0]
    jrows = jacobian_inv.shape[0]
    strip = trades // PATHS
    rest = params - CHIPS * LANE
    pad = -(-jrows // 16) * 16
    half = params // 2
    slots = cash_flows.shape[1]
    part = pad // 2
    share = 16
    vm = pltpu.VMEM
    dma = pltpu.SemaphoreType.DMA
    scratch = [
        vm((paths_own, LANE), BF16),
        vm((slots, trades), F32),
        vm((slots, trades), jnp.int32),
        vm((1, trades), jnp.int32),
        vm((1, trades), jnp.int32),
        vm((half, paths_own), BF16),
        vm((half, paths_own), BF16),
        vm((paths_own, LANE), BF16),
        vm((half + 8, LANE), F32),
        vm((RING, RING, 2 * pad, LANE), F32),
        vm((RING, 6, pad, LANE), F32),
        vm((RING, 2 * pad, LANE), F32),
        vm((RING, RING, part, LANE), F32),
        vm((2, 2 * part, LANE), F32),
        vm((2, DEPTH, share, LANE), F32),
        vm((2, share, LANE), F32),
        vm((2, 2 * part, LANE), F32),
        vm((RING, RING, 2 * pad, LANE), F32),
        vm((jrows, params), BF16),
        vm((pad, -(-rest // LANE) * LANE), F32),
        vm((DEPTH, RING, pad + GROUP, LANE), BF16),
        vm((2, RING, pad + GROUP, LANE), BF16),
        vm((RING, RING, 2 * pad, LANE), BF16),
        vm((RING, RING, 2, GROUP, LANE), BF16),
        vm((RING * RING, 2 * pad, LANE), BF16),
        vm((trades, 3 * LANE), BF16),
        vm((trades, 8 * pad), jnp.int32),
        vm((2, trades, 4 * pad), BF16),
        vm((trades, 2 * LANE), F32),
        vm((trades // 2, 2 * LANE), F32),
        vm((CHIPS, 2 * strip, LANE), BF16),
        vm((CHIPS, 2 * strip, LANE), BF16),
        dma((RING + 1,)), dma((RING + 1,)), dma((7,)),
        dma((RING, 6)), dma((RING, 6)),
        dma((RING, RING)), dma((RING,)),
        dma((2, DEPTH)), dma((2,)),
        dma((2, DEPTH)), dma((2,)),
        dma((RING, RING)), dma((RING,)),
        dma((RING, 6)), dma((RING, 6)),
        dma((DEPTH,)), dma((2, RING)), dma((3, 2)),
        dma((2, 6)), dma((2, 6)),
        dma((2,)), dma((2,)),
        dma((1,)), dma((1,)),
        pltpu.SemaphoreType.REGULAR((2,)),
    ]
    vmem = pl.BlockSpec(memory_space=pltpu.VMEM)
    hbm = pl.BlockSpec(memory_space=pl.ANY)
    return pl.pallas_call(
        kernel,
        out_shape=jax.ShapeDtypeStruct((strip, params), F32),
        in_specs=[hbm] * 7,
        out_specs=vmem,
        scratch_shapes=scratch,
        compiler_params=pltpu.CompilerParams(
            collective_id=0, has_side_effects=True, vmem_limit_bytes=56 * 1024 * 1024
        ),
    )(
        discounts,
        path_sens.T,
        cash_flows.T,
        flow_index.T,
        exercise_step.reshape(1, trades),
        trade_steps.reshape(1, trades),
        jacobian_inv,
    )


def solution(mesh):
    placed = (
        P(("grp", "path"), None),
        P(("grp", "path"), None),
        P("grp", None),
        P("grp", None),
        P("grp"),
        P("grp"),
        P("path", None),
    )
    return jax.shard_map(
        per_device, mesh=mesh, in_specs=placed, out_specs=P(("grp", "path"), None), check_vma=False
    )
```

```python
import jax
import jax.numpy as jnp
from jax import lax
from jax.experimental import pallas as pl
from jax.experimental.pallas import tpu as pltpu
from jax.sharding import PartitionSpec as P

NB = 40
LANE = 128
RING = 4
DEPTH = 8
CHIPS = RING * DEPTH
PATHS = 2 * CHIPS
GROUP = 16
F32 = jnp.float32
BF16 = jnp.bfloat16
MESH = pl.DeviceIdType.MESH


def kernel(
    disc, sens, cash, index, exer, steps, jac, out,
    dv, cv, iv, ev, sv, s_own, s_in, d_in, xs, xp, r1, y2, r2, zb, rz, zr, zf, xf,
    jv, je, jp, jz, jr, jx, jb, wt, room, mk, acc, pr, po, ob,
    ss_s, rs_s, ls, ss_1, rs_1, ss_2, rs_2, ss_z, rs_z, ss_g, rs_g,
    ss_a2, rs_a2, ss_a1, rs_a1, ss_j, ss_jx, rs_j, ss_ja, rs_ja, ss_p, rs_p, ss_o, rs_o, near_z,
):
    y = lax.axis_index("grp")
    me = lax.axis_index("path")
    j = lax.div(me, 2)
    c = lax.rem(me, 2)
    x = lax.div(j, DEPTH)
    z = lax.rem(j, DEPTH)
    sib = 1 - c
    params = sens.shape[0]
    width = params // NB
    half = params // 2
    jrows = jac.shape[0]
    pad = xp.shape[2] // 2
    trades = cash.shape[1]

    def at_chip(xx, zz, cc):
        return {"grp": y, "path": (xx * DEPTH + zz) * 2 + cc}

    def rdma(src, dst, ss, rs, dev):
        return pltpu.make_async_remote_copy(
            src_ref=src, dst_ref=dst, send_sem=ss, recv_sem=rs, device_id=dev, device_id_type=MESH
        )

    sent = []

    def send(*args):
        d = rdma(*args)
        d.start()
        sent.append((None, d))

    def send_if(cond, *args):
        d = rdma(*args)

        @pl.when(cond)
        def _():
            d.start()

        sent.append((cond, d))

    sibling = at_chip(x, z, sib)

    def on_x(k):
        return at_chip(lax.rem(x + k, RING), z, c)

    def on_y(k):
        return {"grp": lax.rem(y + k, RING), "path": me}

    def on_z(k):
        return at_chip(x, lax.rem(z + k, DEPTH), c)

    lines = ((x, on_x), (y, on_y))

    barrier = pltpu.get_barrier_semaphore()
    partners = [sibling] + [on(k) for on in (on_x, on_y) for k in (1, RING - 1)]
    partners += [on_z(k) for k in (1, DEPTH - 1, 2, DEPTH - 2)]
    for d in partners:
        pl.semaphore_signal(barrier, inc=1, device_id=d, device_id_type=MESH)

    fetched = [
        pltpu.make_async_copy(src, dst, ls.at[n])
        for n, (src, dst) in enumerate(
            (
                (disc, dv),
                (sens.at[pl.ds(pl.multiple_of(c * half, 16), half)], s_own),
                (cash, cv), (index, iv), (exer, ev), (steps, sv), (jac, jv),
            )
        )
    ]
    for f in fetched:
        f.start()

    first_cut = (half // 4 // 16 + 1) * 16
    cuts = (0, first_cut, half // 2, half // 2 + first_cut, half)

    def s_copy(q):
        n = cuts[q + 1] - cuts[q]
        return (
            sens.at[pl.ds(pl.multiple_of(sib * half + cuts[q], 16), n)],
            s_in.at[pl.ds(cuts[q], n)], ss_s.at[q], rs_s.at[q], sibling,
        )

    d_copy = (disc, d_in, ss_s.at[RING], rs_s.at[RING], sibling)

    xs[half : half + 8] = jnp.zeros((8, LANE), F32)
    for f in fetched[:2]:
        f.wait()
    third = half // 3

    @pl.loop(0, 3)
    def _(n):
        rws = pl.ds(pl.multiple_of(n * third, 16), third)
        xs[rws] = jnp.dot(s_own[rws], dv[...], preferred_element_type=F32)

    pl.semaphore_wait(barrier, len(partners))
    send(*d_copy)
    leading = [rdma(*s_copy(q)) for q in (0, 1)]
    for d in leading:
        d.start()
    for n, k in enumerate((2, DEPTH - 2)):
        pl.semaphore_signal(near_z.at[n], inc=1, device_id=on_z(k), device_id_type=MESH)

    main = CHIPS * LANE
    more = (params - main) // CHIPS
    groups = pad // GROUP
    turn = lax.rem(z, RING) == y
    core = lax.div(x, 2)
    high = lax.div(z, RING)
    for f in fetched[2:]:
        f.wait()

    @pl.when(turn)
    def _():
        jp[...] = jnp.zeros(jp.shape, BF16)

        @pl.loop(0, DEPTH)
        def _(zz):
            for t in range(RING):
                col = pl.multiple_of((zz * RING + t) * LANE, LANE)
                jp[zz, t, 0:jrows] = jv[:, pl.ds(col, LANE)]

        je[...] = jnp.zeros(je.shape, F32)
        je[0:jrows, 0 : params - main] = jv[:, main:params].astype(F32)
        for t in range(CHIPS):
            packed = [
                je[r * GROUP : (r + 1) * GROUP, t * more : (t + 1) * more] for r in range(groups)
            ]
            packed.append(jnp.zeros((GROUP, LANE - groups * more), F32))
            jp[t // RING, t % RING, pad : pad + GROUP] = jnp.concatenate(packed, axis=1).astype(BF16)

        pltpu.make_async_copy(jp.at[z], jz.at[high], rs_j.at[2, high]).start()

    def j_line(k):
        zz = lax.rem(z + k, DEPTH)
        return jp.at[zz], jz.at[high], ss_j.at[k], rs_j.at[2, high], on_z(k)

    def j_depth(*steps_):
        @pl.when(turn)
        def _():
            for k in steps_:
                rdma(*j_line(k)).start()

    j_depth(2, 6, 1, 7)

    def part_rows(n, size):
        return pl.ds(pl.multiple_of(n * size, 8), size)

    class Scatter:
        def __init__(self, q):
            self.q = q
            self.i, self.on = lines[q % 2]
            self.nr, self.far, self.nl = (lax.rem(self.i + k, RING) for k in (1, 2, 3))
            self.right, self.left = self.on(1), self.on(3)

        def msg(self, n, h, k, dev):
            q = self.q
            return (
                xp.at[q, k, h * pad : (h + 1) * pad], r1.at[q, n],
                ss_1.at[q, n], rs_1.at[q, n], dev,
            )

        def first(self):
            send(*self.msg(0, 0, self.far, self.right))
            send(*self.msg(2, 1, self.far, self.left))

        def near(self):
            send(*self.msg(3, 1, self.nr, self.right))
            send(*self.msg(1, 0, self.nl, self.left))

        def second(self):
            for h, n, k, dev in ((0, 0, self.nr, self.right), (1, 2, self.nl, self.left)):
                rdma(*self.msg(n, h, k, dev)).wait_recv()
                xp[self.q, k, h * pad : (h + 1) * pad] += r1[self.q, n]
                send(*self.msg(4 + h, h, k, dev))

        def result(self):
            for h, n in ((0, 1), (1, 3)):
                rdma(*self.msg(n, h, self.i, self.left)).wait_recv()
                rdma(*self.msg(4 + h, h, self.i, self.left)).wait_recv()
                rws = slice(h * pad, (h + 1) * pad)
                y2[self.q, rws] = xp[self.q, self.i, rws] + r1[self.q, n] + r1[self.q, 4 + h]

    one = [Scatter(q) for q in range(RING)]
    for q, d in enumerate(leading):
        d.wait_send()
        send(*s_copy(q + 2))
    rdma(*d_copy).wait_recv()
    for q in range(RING):
        rdma(*s_copy(q)).wait_recv()
        xs[cuts[q] : cuts[q + 1]] += jnp.dot(
            s_in[cuts[q] : cuts[q + 1]], d_in[...], preferred_element_type=F32
        )
        for k in range(RING):
            for u in (0, 1):
                top = (8 * q + 2 * k + u) * jrows
                xp[q, k, u * pad : (u + 1) * pad] = xs[top : top + pad]
        one[q].first()
    for r in one:
        r.near()

    for n in (0, 1):
        pl.semaphore_wait(near_z.at[n], 1)
    j_depth(4, 3, 5)
    one[0].second()
    one[1].second()
    one[2].second()
    one[3].second()

    def j_cross(e, k):
        xx = lax.rem(x + k, RING)
        two_ = pl.ds(2 * lax.rem(x, 2), 2)
        if e == 0:
            src = jz.at[:, xx, 0:pad]
            dst = jr.at[two_, y, pl.ds(pl.multiple_of(c * pad, 16), pad)]
        else:
            src = jz.at[:, xx, pad : pad + GROUP]
            dst = jx.at[two_, y, c]
        return src, dst, ss_jx.at[e, k], rs_j.at[e, 0], at_chip(xx, z, core)

    def both(f):
        f(0)
        f(1)

    def j_send(e):
        for k in (2, 1, 3):
            rdma(*j_cross(e, k)).start()
        src, dst, ss, rs, dev = j_cross(e, 0)

        @pl.when(core == c)
        def _():
            pltpu.make_async_copy(src, dst, rs).start()

        @pl.when(core != c)
        def _():
            rdma(src, dst, ss, rs, dev).start()


    part = y2.shape[1] // RING

    def two(q, k):
        i, on = lines[1 - q % 2]
        return (
            y2.at[q, part_rows(lax.rem(i + k, RING), part)], r2.at[q, i],
            ss_2.at[q, k], rs_2.at[q], on(k),
        )

    for g in (0, 1):
        for q in (2 * g, 2 * g + 1):
            one[q].result()
            for k in (2, 1, 3):
                send(*two(q, k))
    for n in (0, 1):
        pltpu.make_async_copy(jp.at[0], jz.at[n], rs_j.at[2, n]).wait()
    both(j_send)

    share = zr.shape[1]
    count = 2 * part // share
    spread = (4, 3, 5, 2, 6, 1, 7)

    def turn_of(g, d):
        return lax.rem(d + count * g, DEPTH)

    def reduces(g):
        return turn_of(g, z) < count

    def z_piece(g, d):
        return part_rows(jnp.minimum(turn_of(g, d), count - 1), share)

    for g in (0, 1):
        for p in (0, 1):
            q = 2 * g + p
            i, on = lines[1 - p]
            total = y2[q, part_rows(i, part)]
            three = r2.at[q, 0 : RING - 1]
            rdma(three, three, ss_2.at[q, 0], rs_2.at[q], sibling).wait_recv()
            for k in (1, 2, 3):
                total += r2[q, lax.rem(i + k, RING)]
            zb[g, p * part : (p + 1) * part] = total
        for k in spread:
            d = lax.rem(z + k, DEPTH)
            send_if(
                turn_of(g, d) < count,
                zb.at[g, z_piece(g, d)], rz.at[g, z], ss_z.at[g, k], rs_z.at[g], on_z(k),
            )


    def j_ring(half_, k, n, dev):
        ref = jr.at[pl.ds(2 * half_, 2), k]
        return ref, ref, ss_ja.at[0, n], rs_ja.at[0, n], dev

    def j_fan(k):
        ref = jx.at[:, y]
        return ref, ref, ss_ja.at[1, k], rs_ja.at[1, 0], on_y(k)

    yr, yl = on_y(1), on_y(3)
    ynr, yfar, ynl = (lax.rem(y + k, RING) for k in (1, 2, 3))

    def j_start():
        for e, whole in ((0, jr.at[:, y]), (1, jx.at[:, y])):
            pltpu.make_async_copy(whole, whole, rs_j.at[e, 0]).wait()
        for n, (hh, d) in enumerate(((0, yr), (1, yl), (1, yr), (0, yl))):
            send(*j_ring(hh, y, n, d))
        for k in (2, 1, 3):
            send(*j_fan(k))

    def j_forward():
        rdma(*j_ring(0, ynl, 0, yr)).wait_recv()
        send(*j_ring(0, ynl, 4, yr))
        rdma(*j_ring(1, ynr, 1, yl)).wait_recv()
        send(*j_ring(1, ynr, 5, yl))

    def j_finish():
        for hh, k, n, d in ((1, ynl, 2, yr), (0, ynr, 3, yl), (0, yfar, 4, yr), (1, yfar, 5, yl)):
            rdma(*j_ring(hh, k, n, d)).wait_recv()

    def j_unpack():
        three = jx.at[0 : RING - 1]
        rdma(three, three, ss_ja.at[1, 0], rs_ja.at[1, 0], sibling).wait_recv()

        @pl.loop(0, RING * RING)
        def _(n):
            q, k = lax.div(n, RING), lax.rem(n, RING)
            for u in (0, 1):
                tile = jx[q, k, u].astype(F32)
                for r in range(groups):
                    at = u * pad + r * GROUP
                    turned_ = tile if r == 0 else pltpu.roll(tile, LANE - r * more, 1)
                    jb[n, at : at + GROUP] = turned_.astype(BF16)

    j_start()
    early = len(sent)

    for g in (0, 1):
        reducer = reduces(g)

        @pl.when(reducer)
        def _():
            total = zb[g, z_piece(g, z)]
            seven = rz.at[g, 0 : DEPTH - 1]
            rdma(seven, seven, ss_z.at[g, 0], rs_z.at[g], sibling).wait_recv()
            for k in range(1, DEPTH):
                total += rz[g, lax.rem(z + k, DEPTH)]
            zr[g] = total
            zf[g, z_piece(g, z)] = total

        for k in spread:
            send_if(
                reducer, zr.at[g], zf.at[g, z_piece(g, z)], ss_g.at[g, k], rs_g.at[g], on_z(k)
            )


    slots = cash.shape[0]
    forwards = lax.broadcasted_iota(jnp.int32, (LANE, trades), 0)
    late = forwards >= ev[...]
    weights = jnp.zeros((LANE, trades), F32)
    for s in range(slots):
        weights += jnp.where(late & (iv[s : s + 1] == forwards), cv[s : s + 1], 0.0)
    weights = weights * (1.0 / (disc.shape[0] * PATHS * RING))
    weights = weights.T
    w_hi = weights.astype(BF16)
    w_lo = (weights - w_hi.astype(F32)).astype(BF16)
    wt[...] = jnp.concatenate([w_hi, w_hi, w_lo], axis=1)
    reach = jnp.broadcast_to((sv[...] * width).astype(F32), (LANE, trades)).T.astype(jnp.int32)
    span = room.shape[1]
    lane = lax.broadcasted_iota(jnp.int32, (trades, span), 1)
    lane = lax.rem(lane, 2 * pad)
    room[...] = (
        jnp.concatenate([reach] * (span // LANE), axis=1)
        - lane + jnp.where(lane >= pad, pad - jrows, 0) - c * half
    )

    def all_left(n):
        for cond, d in sent[:n]:
            if cond is None:
                d.wait_send()
            else:
                pl.when(cond)(d.wait_send)
        del sent[:n]

    all_left(early)

    def home(q, i):
        return xf.at[q, lines[q % 2][0], part_rows(i, part)]

    for g in (0, 1):
        for some, ref in ((reduces(g), zf.at[g, 0 : (count - 1) * share]), (~reduces(g), zf.at[g])):

            @pl.when(some)
            def _():
                rdma(ref, ref, ss_g.at[g, 0], rs_g.at[g], sibling).wait_recv()

        for p in (0, 1):
            q = 2 * g + p
            i, on = lines[1 - p]
            mine = zf.at[g, p * part : (p + 1) * part]
            for k in (2, 1, 3):
                send(mine, home(q, i), ss_a2.at[q, k], rs_a2.at[q], on(k))
            home(q, i)[...] = mine[...]

    j_forward()

    class Gather:
        def __init__(self, q):
            self.q = q
            self.i, self.on = lines[q % 2]
            self.nr, self.far, self.nl = (lax.rem(self.i + k, RING) for k in (1, 2, 3))
            self.right, self.left = self.on(1), self.on(3)

        def msg(self, n, h, k, dev):
            ref = xf.at[self.q, k, h * pad : (h + 1) * pad]
            return ref, ref, ss_a1.at[self.q, n], rs_a1.at[self.q, n], dev

        def start(self):
            q = self.q
            three = xf.at[q, 0, 0 : (RING - 1) * part]
            rdma(three, three, ss_a2.at[q, 0], rs_a2.at[q], sibling).wait_recv()
            send(*self.msg(0, 0, self.i, self.right))
            send(*self.msg(1, 1, self.i, self.left))
            send(*self.msg(2, 1, self.i, self.right))
            send(*self.msg(3, 0, self.i, self.left))

        def forward(self):
            rdma(*self.msg(0, 0, self.nl, self.right)).wait_recv()
            send(*self.msg(4, 0, self.nl, self.right))
            rdma(*self.msg(1, 1, self.nr, self.left)).wait_recv()
            send(*self.msg(5, 1, self.nr, self.left))

    ring = [Gather(q) for q in range(RING)]
    for q in range(RING):
        ring[q].start()

    acc[...] = jnp.zeros(acc.shape, F32)


    def mask(*both_):
        values = jnp.concatenate([xf[q, k] for q, k in both_], axis=0)
        hi = values.astype(BF16)
        lo = (values - hi.astype(F32)).astype(BF16)
        vega = lax.dot_general(
            wt[...], jnp.concatenate([hi, lo, hi], axis=1), (((1,), (1,)), ((), ())),
            preferred_element_type=F32,
        )
        wide_ = len(both_) * 2 * pad
        lanes = lax.broadcasted_iota(jnp.int32, (1, wide_), 1)
        start = jnp.zeros((1, wide_), jnp.int32)
        for n, (q, k) in enumerate(both_):
            start = jnp.where(lanes >= n * 2 * pad, (8 * q + 2 * k) * jrows, start)
        keep = room[:, 0:wide_] > start
        return jnp.where(keep, vega, 0.0).astype(BF16)

    def add(masked, *both_):
        columns = [
            jnp.concatenate([jr[q, k], jb[RING * q + k]], axis=1) for q, k in both_
        ]
        acc[...] += jnp.dot(
            masked, jnp.concatenate(columns, axis=0), preferred_element_type=F32
        )

    def pair(*both_):
        add(mask(*both_), *both_)

    def landed(q, k, h, n):
        ref = xf.at[q, k, h * pad : (h + 1) * pad]
        rdma(ref, ref, ss_a1.at[q, n], rs_a1.at[q, n], sibling).wait_recv()

    mine = lambda g: ((2 * g, x), (2 * g + 1, y))

    @pl.loop(0, 2)
    def _(g):
        mk[g] = mask(*mine(g))

    j_unpack()

    for r in ring:
        r.forward()
    j_finish()

    @pl.loop(0, 2)
    def _(g):
        add(mk[g], *mine(g))

    @pl.loop(0, 2)
    def _(g):
        blocks = []
        for p in (0, 1):
            q = 2 * g + p
            landed(q, ring[p].nl, 1, 2)
            landed(q, ring[p].nr, 0, 3)
            blocks += [(q, ring[p].nl), (q, ring[p].nr)]
        pair(*blocks)

    far_x, far_y = ring[0].far, ring[1].far

    @pl.loop(0, 2)
    def _(g):
        for q, k in ((2 * g, far_x), (2 * g + 1, far_y)):
            landed(q, k, 0, 4)
            landed(q, k, 1, 5)
        pair((2 * g, far_x), (2 * g + 1, far_y))

    rows_c = pl.ds(pl.multiple_of(c * (trades // 2), 8), trades // 2)
    rows_sib = pl.ds(pl.multiple_of(sib * (trades // 2), 8), trades // 2)
    swap = (acc.at[rows_sib], pr, ss_p.at[0], rs_p.at[0], sibling)
    send(*swap)
    strip_rows = out.shape[0]
    rdma(*swap).wait_recv()
    total = acc[rows_c] + pr[...]
    po[...] = jnp.concatenate(
        [total[:, s * LANE : (s + 1) * LANE].reshape(CHIPS, strip_rows, LANE) for s in (0, 1)], axis=1
    ).astype(BF16)

    tile = ob.at[z * RING + x]

    def deliver(n, dst):
        rdma(po.at[n], tile, ss_o.at[0], rs_o.at[0], {"grp": y, "path": dst}).start()

    for k in (4, 3, 5, 2, 6, 1, 7, 0):
        zz = lax.rem(z + k, DEPTH)
        for side in (0, 1):
            for u in (0, 1):
                n = side * 2 * DEPTH + 2 * zz + u
                dst = c * CHIPS + n
                if k:
                    deliver(n, dst)
                else:
                    pl.when(dst != me)(lambda n=n, dst=dst: deliver(n, dst))

                    @pl.when(dst == me)
                    def _():
                        pltpu.make_async_copy(po.at[n], tile, rs_o.at[0]).start()

    all_left(len(sent))

    def j_crossed(e):
        for k in (1, 2, 3):
            rdma(*j_cross(e, k)).wait_send()

        @pl.when(core != c)
        def _():
            rdma(*j_cross(e, 0)).wait_send()

    both(j_crossed)

    @pl.when(turn)
    def _():
        for k in range(1, DEPTH):
            rdma(*j_line(k)).wait_send()

    pltpu.make_async_copy(ob, ob, rs_o.at[0]).wait()

    rest = []
    for t in range(CHIPS):
        tile = ob[t].astype(F32)
        out[:, t * LANE : (t + 1) * LANE] = tile[0:strip_rows]
        rest.append(tile[strip_rows : 2 * strip_rows, 0:more])
    out[:, main:params] = jnp.concatenate(rest, axis=1)

    def po_sent(n):
        rdma(po.at[0:n], po.at[0:n], ss_o.at[0], rs_o.at[0], sibling).wait_send()

    pl.when(core == c)(lambda: po_sent(CHIPS - 1))
    pl.when(core != c)(lambda: po_sent(CHIPS))


def per_device(
    path_sens, discounts, cash_flows, flow_index, exercise_step, trade_steps, jacobian_inv
):
    paths_own, params = path_sens.shape
    trades = cash_flows.shape[0]
    jrows = jacobian_inv.shape[0]
    strip = trades // PATHS
    rest = params - CHIPS * LANE
    pad = -(-jrows // 16) * 16
    half = params // 2
    slots = cash_flows.shape[1]
    part = pad // 2
    share = 16
    vm = pltpu.VMEM
    dma = pltpu.SemaphoreType.DMA
    scratch = [
        vm((paths_own, LANE), BF16),
        vm((slots, trades), F32),
        vm((slots, trades), jnp.int32),
        vm((1, trades), jnp.int32),
        vm((1, trades), jnp.int32),
        vm((half, paths_own), BF16),
        vm((half, paths_own), BF16),
        vm((paths_own, LANE), BF16),
        vm((half + 8, LANE), F32),
        vm((RING, RING, 2 * pad, LANE), F32),
        vm((RING, 6, pad, LANE), F32),
        vm((RING, 2 * pad, LANE), F32),
        vm((RING, RING, part, LANE), F32),
        vm((2, 2 * part, LANE), F32),
        vm((2, DEPTH, share, LANE), F32),
        vm((2, share, LANE), F32),
        vm((2, 2 * part, LANE), F32),
        vm((RING, RING, 2 * pad, LANE), F32),
        vm((jrows, params), BF16),
        vm((pad, -(-rest // LANE) * LANE), F32),
        vm((DEPTH, RING, pad + GROUP, LANE), BF16),
        vm((2, RING, pad + GROUP, LANE), BF16),
        vm((RING, RING, 2 * pad, LANE), BF16),
        vm((RING, RING, 2, GROUP, LANE), BF16),
        vm((RING * RING, 2 * pad, LANE), BF16),
        vm((trades, 3 * LANE), BF16),
        vm((trades, 8 * pad), jnp.int32),
        vm((2, trades, 4 * pad), BF16),
        vm((trades, 2 * LANE), F32),
        vm((trades // 2, 2 * LANE), F32),
        vm((CHIPS, 2 * strip, LANE), BF16),
        vm((CHIPS, 2 * strip, LANE), BF16),
        dma((RING + 1,)), dma((RING + 1,)), dma((7,)),
        dma((RING, 6)), dma((RING, 6)),
        dma((RING, RING)), dma((RING,)),
        dma((2, DEPTH)), dma((2,)),
        dma((2, DEPTH)), dma((2,)),
        dma((RING, RING)), dma((RING,)),
        dma((RING, 6)), dma((RING, 6)),
        dma((DEPTH,)), dma((2, RING)), dma((3, 2)),
        dma((2, 6)), dma((2, 6)),
        dma((2,)), dma((2,)),
        dma((1,)), dma((1,)),
        pltpu.SemaphoreType.REGULAR((2,)),
    ]
    vmem = pl.BlockSpec(memory_space=pltpu.VMEM)
    hbm = pl.BlockSpec(memory_space=pl.ANY)
    return pl.pallas_call(
        kernel,
        out_shape=jax.ShapeDtypeStruct((strip, params), F32),
        in_specs=[hbm] * 7,
        out_specs=vmem,
        scratch_shapes=scratch,
        compiler_params=pltpu.CompilerParams(
            collective_id=0, has_side_effects=True, vmem_limit_bytes=56 * 1024 * 1024
        ),
    )(
        discounts,
        path_sens.T,
        cash_flows.T,
        flow_index.T,
        exercise_step.reshape(1, trades),
        trade_steps.reshape(1, trades),
        jacobian_inv,
    )


def solution(mesh):
    placed = (
        P(("grp", "path"), None),
        P(("grp", "path"), None),
        P("grp", None),
        P("grp", None),
        P("grp"),
        P("grp"),
        P("path", None),
    )
    return jax.shard_map(
        per_device, mesh=mesh, in_specs=placed, out_specs=P(("grp", "path"), None), check_vma=False
    )
```

```python
import jax
import jax.numpy as jnp
from jax import lax
from jax.experimental import pallas as pl
from jax.experimental.pallas import tpu as pltpu
from jax.sharding import PartitionSpec as P

NB = 40
LANE = 128
RING = 4
DEPTH = 8
CHIPS = RING * DEPTH
PATHS = 2 * CHIPS
GROUP = 16
F32 = jnp.float32
BF16 = jnp.bfloat16
MESH = pl.DeviceIdType.MESH


def kernel(
    disc, sens, cash, index, exer, steps, jac, out,
    dv, cv, iv, ev, sv, s_own, s_in, d_in, xs, xp, r1, y2, r2, zb, rz, zr, zf, xf,
    jv, je, jp, jz, jr, jx, jb, wt, room, mk, acc, pr, po, ob,
    ss_s, rs_s, ls, ss_1, rs_1, ss_2, rs_2, ss_z, rs_z, ss_g, rs_g,
    ss_a2, rs_a2, ss_a1, rs_a1, ss_j, ss_jx, rs_j, ss_ja, rs_ja, ss_p, rs_p, ss_o, rs_o, near_z,
):
    y = lax.axis_index("grp")
    me = lax.axis_index("path")
    j = lax.div(me, 2)
    c = lax.rem(me, 2)
    x = lax.div(j, DEPTH)
    z = lax.rem(j, DEPTH)
    sib = 1 - c
    params = sens.shape[0]
    width = params // NB
    half = params // 2
    jrows = jac.shape[0]
    pad = xp.shape[2] // 2
    trades = cash.shape[1]

    def at_chip(xx, zz, cc):
        return {"grp": y, "path": (xx * DEPTH + zz) * 2 + cc}

    def rdma(src, dst, ss, rs, dev):
        return pltpu.make_async_remote_copy(
            src_ref=src, dst_ref=dst, send_sem=ss, recv_sem=rs, device_id=dev, device_id_type=MESH
        )

    sent = []

    def send(*args):
        d = rdma(*args)
        d.start()
        sent.append((None, d))

    def send_if(cond, *args):
        d = rdma(*args)

        @pl.when(cond)
        def _():
            d.start()

        sent.append((cond, d))

    sibling = at_chip(x, z, sib)

    def on_x(k):
        return at_chip(lax.rem(x + k, RING), z, c)

    def on_y(k):
        return {"grp": lax.rem(y + k, RING), "path": me}

    def on_z(k):
        return at_chip(x, lax.rem(z + k, DEPTH), c)

    lines = ((x, on_x), (y, on_y))

    barrier = pltpu.get_barrier_semaphore()
    partners = [sibling] + [on(k) for on in (on_x, on_y) for k in (1, RING - 1)]
    partners += [on_z(k) for k in (1, DEPTH - 1, 2, DEPTH - 2)]
    for d in partners:
        pl.semaphore_signal(barrier, inc=1, device_id=d, device_id_type=MESH)

    fetched = [
        pltpu.make_async_copy(src, dst, ls.at[n])
        for n, (src, dst) in enumerate(
            (
                (disc, dv),
                (sens.at[pl.ds(pl.multiple_of(c * half, 16), half)], s_own),
                (cash, cv), (index, iv), (exer, ev), (steps, sv), (jac, jv),
            )
        )
    ]
    for f in fetched:
        f.start()

    first_cut = (half // 4 // 16 + 1) * 16
    cuts = (0, first_cut, half // 2, half // 2 + first_cut, half)

    def s_copy(q):
        n = cuts[q + 1] - cuts[q]
        return (
            sens.at[pl.ds(pl.multiple_of(sib * half + cuts[q], 16), n)],
            s_in.at[pl.ds(cuts[q], n)], ss_s.at[q], rs_s.at[q], sibling,
        )

    d_copy = (disc, d_in, ss_s.at[RING], rs_s.at[RING], sibling)

    xs[half : half + 8] = jnp.zeros((8, LANE), F32)
    for f in fetched[:2]:
        f.wait()
    third = half // 3

    @pl.loop(0, 3)
    def _(n):
        rws = pl.ds(pl.multiple_of(n * third, 16), third)
        xs[rws] = jnp.dot(s_own[rws], dv[...], preferred_element_type=F32)

    pl.semaphore_wait(barrier, len(partners))
    send(*d_copy)
    leading = [rdma(*s_copy(q)) for q in (0, 1)]
    for d in leading:
        d.start()
    for n, k in enumerate((2, DEPTH - 2)):
        pl.semaphore_signal(near_z.at[n], inc=1, device_id=on_z(k), device_id_type=MESH)

    main = CHIPS * LANE
    more = (params - main) // CHIPS
    groups = pad // GROUP
    turn = lax.rem(z, RING) == y
    core = lax.div(x, 2)
    high = lax.div(z, RING)
    for f in fetched[2:]:
        f.wait()

    @pl.when(turn)
    def _():
        jp[...] = jnp.zeros(jp.shape, BF16)

        @pl.loop(0, DEPTH)
        def _(zz):
            for t in range(RING):
                col = pl.multiple_of((zz * RING + t) * LANE, LANE)
                jp[zz, t, 0:jrows] = jv[:, pl.ds(col, LANE)]

        je[...] = jnp.zeros(je.shape, F32)
        je[0:jrows, 0 : params - main] = jv[:, main:params].astype(F32)
        for t in range(CHIPS):
            packed = [
                je[r * GROUP : (r + 1) * GROUP, t * more : (t + 1) * more] for r in range(groups)
            ]
            packed.append(jnp.zeros((GROUP, LANE - groups * more), F32))
            jp[t // RING, t % RING, pad : pad + GROUP] = jnp.concatenate(packed, axis=1).astype(BF16)

        pltpu.make_async_copy(jp.at[z], jz.at[high], rs_j.at[2, high]).start()

    def j_line(k):
        zz = lax.rem(z + k, DEPTH)
        return jp.at[zz], jz.at[high], ss_j.at[k], rs_j.at[2, high], on_z(k)

    def j_depth(*steps_):
        @pl.when(turn)
        def _():
            for k in steps_:
                rdma(*j_line(k)).start()

    j_depth(2, 6, 1, 7)

    def part_rows(n, size):
        return pl.ds(pl.multiple_of(n * size, 8), size)

    class Scatter:
        def __init__(self, q):
            self.q = q
            self.i, self.on = lines[q % 2]
            self.nr, self.far, self.nl = (lax.rem(self.i + k, RING) for k in (1, 2, 3))
            self.right, self.left = self.on(1), self.on(3)

        def msg(self, n, h, k, dev):
            q = self.q
            return (
                xp.at[q, k, h * pad : (h + 1) * pad], r1.at[q, n],
                ss_1.at[q, n], rs_1.at[q, n], dev,
            )

        def first(self):
            send(*self.msg(0, 0, self.far, self.right))
            send(*self.msg(2, 1, self.far, self.left))

        def near(self):
            send(*self.msg(3, 1, self.nr, self.right))
            send(*self.msg(1, 0, self.nl, self.left))

        def second(self):
            for h, n, k, dev in ((0, 0, self.nr, self.right), (1, 2, self.nl, self.left)):
                rdma(*self.msg(n, h, k, dev)).wait_recv()
                xp[self.q, k, h * pad : (h + 1) * pad] += r1[self.q, n]
                send(*self.msg(4 + h, h, k, dev))

        def result(self):
            for h, n in ((0, 1), (1, 3)):
                rdma(*self.msg(n, h, self.i, self.left)).wait_recv()
                rdma(*self.msg(4 + h, h, self.i, self.left)).wait_recv()
                rws = slice(h * pad, (h + 1) * pad)
                y2[self.q, rws] = xp[self.q, self.i, rws] + r1[self.q, n] + r1[self.q, 4 + h]

    one = [Scatter(q) for q in range(RING)]
    for q, d in enumerate(leading):
        d.wait_send()
        send(*s_copy(q + 2))
    rdma(*d_copy).wait_recv()
    for q in range(RING):
        rdma(*s_copy(q)).wait_recv()
        xs[cuts[q] : cuts[q + 1]] += jnp.dot(
            s_in[cuts[q] : cuts[q + 1]], d_in[...], preferred_element_type=F32
        )
        for k in range(RING):
            for u in (0, 1):
                top = (8 * q + 2 * k + u) * jrows
                xp[q, k, u * pad : (u + 1) * pad] = xs[top : top + pad]
        one[q].first()
    for r in one:
        r.near()

    for n in (0, 1):
        pl.semaphore_wait(near_z.at[n], 1)
    j_depth(4, 3, 5)
    one[0].second()
    one[1].second()
    one[2].second()
    one[3].second()

    def j_cross(e, k):
        xx = lax.rem(x + k, RING)
        two_ = pl.ds(2 * lax.rem(x, 2), 2)
        if e == 0:
            src = jz.at[:, xx, 0:pad]
            dst = jr.at[two_, y, pl.ds(pl.multiple_of(c * pad, 16), pad)]
        else:
            src = jz.at[:, xx, pad : pad + GROUP]
            dst = jx.at[two_, y, c]
        return src, dst, ss_jx.at[e, k], rs_j.at[e, 0], at_chip(xx, z, core)

    def both(f):
        f(0)
        f(1)

    def j_send(e):
        for k in (2, 1, 3):
            rdma(*j_cross(e, k)).start()
        src, dst, ss, rs, dev = j_cross(e, 0)

        @pl.when(core == c)
        def _():
            pltpu.make_async_copy(src, dst, rs).start()

        @pl.when(core != c)
        def _():
            rdma(src, dst, ss, rs, dev).start()


    part = y2.shape[1] // RING

    def two(q, k):
        i, on = lines[1 - q % 2]
        return (
            y2.at[q, part_rows(lax.rem(i + k, RING), part)], r2.at[q, i],
            ss_2.at[q, k], rs_2.at[q], on(k),
        )

    for g in (0, 1):
        for q in (2 * g, 2 * g + 1):
            one[q].result()
            for k in (2, 1, 3):
                send(*two(q, k))
    for n in (0, 1):
        pltpu.make_async_copy(jp.at[0], jz.at[n], rs_j.at[2, n]).wait()
    both(j_send)

    share = zr.shape[1]
    count = 2 * part // share
    spread = (4, 3, 5, 2, 6, 1, 7)

    def turn_of(g, d):
        return lax.rem(d + count * g, DEPTH)

    def reduces(g):
        return turn_of(g, z) < count

    def z_piece(g, d):
        return part_rows(jnp.minimum(turn_of(g, d), count - 1), share)

    for g in (0, 1):
        for p in (0, 1):
            q = 2 * g + p
            i, on = lines[1 - p]
            total = y2[q, part_rows(i, part)]
            three = r2.at[q, 0 : RING - 1]
            rdma(three, three, ss_2.at[q, 0], rs_2.at[q], sibling).wait_recv()
            for k in (1, 2, 3):
                total += r2[q, lax.rem(i + k, RING)]
            zb[g, p * part : (p + 1) * part] = total
        for k in spread:
            d = lax.rem(z + k, DEPTH)
            send_if(
                turn_of(g, d) < count,
                zb.at[g, z_piece(g, d)], rz.at[g, z], ss_z.at[g, k], rs_z.at[g], on_z(k),
            )


    def j_ring(half_, k, n, dev):
        ref = jr.at[pl.ds(2 * half_, 2), k]
        return ref, ref, ss_ja.at[0, n], rs_ja.at[0, n], dev

    def j_fan(k):
        ref = jx.at[:, y]
        return ref, ref, ss_ja.at[1, k], rs_ja.at[1, 0], on_y(k)

    yr, yl = on_y(1), on_y(3)
    ynr, yfar, ynl = (lax.rem(y + k, RING) for k in (1, 2, 3))

    def j_start():
        for e, whole in ((0, jr.at[:, y]), (1, jx.at[:, y])):
            pltpu.make_async_copy(whole, whole, rs_j.at[e, 0]).wait()
        for n, (hh, d) in enumerate(((0, yr), (1, yl), (1, yr), (0, yl))):
            send(*j_ring(hh, y, n, d))
        for k in (2, 1, 3):
            send(*j_fan(k))

    def j_forward():
        rdma(*j_ring(0, ynl, 0, yr)).wait_recv()
        send(*j_ring(0, ynl, 4, yr))
        rdma(*j_ring(1, ynr, 1, yl)).wait_recv()
        send(*j_ring(1, ynr, 5, yl))

    def j_finish():
        for hh, k, n, d in ((1, ynl, 2, yr), (0, ynr, 3, yl), (0, yfar, 4, yr), (1, yfar, 5, yl)):
            rdma(*j_ring(hh, k, n, d)).wait_recv()

    def j_unpack():
        three = jx.at[0 : RING - 1]
        rdma(three, three, ss_ja.at[1, 0], rs_ja.at[1, 0], sibling).wait_recv()

        @pl.loop(0, RING * RING)
        def _(n):
            q, k = lax.div(n, RING), lax.rem(n, RING)
            for u in (0, 1):
                tile = jx[q, k, u].astype(F32)
                for r in range(groups):
                    at = u * pad + r * GROUP
                    turned_ = tile if r == 0 else pltpu.roll(tile, LANE - r * more, 1)
                    jb[n, at : at + GROUP] = turned_.astype(BF16)

    j_start()
    early = len(sent)

    for g in (0, 1):
        reducer = reduces(g)

        @pl.when(reducer)
        def _():
            total = zb[g, z_piece(g, z)]
            seven = rz.at[g, 0 : DEPTH - 1]
            rdma(seven, seven, ss_z.at[g, 0], rs_z.at[g], sibling).wait_recv()
            for k in range(1, DEPTH):
                total += rz[g, lax.rem(z + k, DEPTH)]
            zr[g] = total
            zf[g, z_piece(g, z)] = total

        for k in spread:
            send_if(
                reducer, zr.at[g], zf.at[g, z_piece(g, z)], ss_g.at[g, k], rs_g.at[g], on_z(k)
            )


    slots = cash.shape[0]
    forwards = lax.broadcasted_iota(jnp.int32, (LANE, trades), 0)
    late = forwards >= ev[...]
    weights = jnp.zeros((LANE, trades), F32)
    for s in range(slots):
        weights += jnp.where(late & (iv[s : s + 1] == forwards), cv[s : s + 1], 0.0)
    weights = weights * (1.0 / (disc.shape[0] * PATHS * RING))
    weights = weights.T
    w_hi = weights.astype(BF16)
    w_lo = (weights - w_hi.astype(F32)).astype(BF16)
    wt[...] = jnp.concatenate([w_hi, w_hi, w_lo], axis=1)
    reach = jnp.broadcast_to((sv[...] * width).astype(F32), (LANE, trades)).T.astype(jnp.int32)
    span = room.shape[1]
    lane = lax.broadcasted_iota(jnp.int32, (trades, span), 1)
    lane = lax.rem(lane, 2 * pad)
    room[...] = (
        jnp.concatenate([reach] * (span // LANE), axis=1)
        - lane + jnp.where(lane >= pad, pad - jrows, 0) - c * half
    )

    def all_left(n):
        for cond, d in sent[:n]:
            if cond is None:
                d.wait_send()
            else:
                pl.when(cond)(d.wait_send)
        del sent[:n]

    all_left(early)

    def home(q, i):
        return xf.at[q, lines[q % 2][0], part_rows(i, part)]

    for g in (0, 1):
        for some, ref in ((reduces(g), zf.at[g, 0 : (count - 1) * share]), (~reduces(g), zf.at[g])):

            @pl.when(some)
            def _():
                rdma(ref, ref, ss_g.at[g, 0], rs_g.at[g], sibling).wait_recv()

        for p in (0, 1):
            q = 2 * g + p
            i, on = lines[1 - p]
            mine = zf.at[g, p * part : (p + 1) * part]
            for k in (2, 1, 3):
                send(mine, home(q, i), ss_a2.at[q, k], rs_a2.at[q], on(k))
            home(q, i)[...] = mine[...]

    j_forward()

    class Gather:
        def __init__(self, q):
            self.q = q
            self.i, self.on = lines[q % 2]
            self.nr, self.far, self.nl = (lax.rem(self.i + k, RING) for k in (1, 2, 3))
            self.right, self.left = self.on(1), self.on(3)

        def msg(self, n, h, k, dev):
            ref = xf.at[self.q, k, h * pad : (h + 1) * pad]
            return ref, ref, ss_a1.at[self.q, n], rs_a1.at[self.q, n], dev

        def start(self):
            q = self.q
            three = xf.at[q, 0, 0 : (RING - 1) * part]
            rdma(three, three, ss_a2.at[q, 0], rs_a2.at[q], sibling).wait_recv()
            send(*self.msg(0, 0, self.i, self.right))
            send(*self.msg(1, 1, self.i, self.left))
            send(*self.msg(2, 1, self.i, self.right))
            send(*self.msg(3, 0, self.i, self.left))

        def forward(self):
            rdma(*self.msg(0, 0, self.nl, self.right)).wait_recv()
            send(*self.msg(4, 0, self.nl, self.right))
            rdma(*self.msg(1, 1, self.nr, self.left)).wait_recv()
            send(*self.msg(5, 1, self.nr, self.left))

    ring = [Gather(q) for q in range(RING)]
    for q in range(RING):
        ring[q].start()

    acc[...] = jnp.zeros(acc.shape, F32)


    def mask(*both_):
        values = jnp.concatenate([xf[q, k] for q, k in both_], axis=0)
        hi = values.astype(BF16)
        lo = (values - hi.astype(F32)).astype(BF16)
        vega = lax.dot_general(
            wt[...], jnp.concatenate([hi, lo, hi], axis=1), (((1,), (1,)), ((), ())),
            preferred_element_type=F32,
        )
        wide_ = len(both_) * 2 * pad
        lanes = lax.broadcasted_iota(jnp.int32, (1, wide_), 1)
        start = jnp.zeros((1, wide_), jnp.int32)
        for n, (q, k) in enumerate(both_):
            start = jnp.where(lanes >= n * 2 * pad, (8 * q + 2 * k) * jrows, start)
        keep = room[:, 0:wide_] > start
        return jnp.where(keep, vega, 0.0).astype(BF16)

    def add(masked, *both_):
        columns = [
            jnp.concatenate([jr[q, k], jb[RING * q + k]], axis=1) for q, k in both_
        ]
        acc[...] += jnp.dot(
            masked, jnp.concatenate(columns, axis=0), preferred_element_type=F32
        )

    def pair(*both_):
        add(mask(*both_), *both_)

    def landed(q, k, h, n):
        ref = xf.at[q, k, h * pad : (h + 1) * pad]
        rdma(ref, ref, ss_a1.at[q, n], rs_a1.at[q, n], sibling).wait_recv()

    mine = ((0, x), (1, y), (2, x), (3, y))

    mk[...] = mask(*mine)

    j_unpack()

    for r in ring:
        r.forward()
    j_finish()

    add(mk[...], *mine)

    @pl.loop(0, 2)
    def _(g):
        blocks = []
        for p in (0, 1):
            q = 2 * g + p
            landed(q, ring[p].nl, 1, 2)
            landed(q, ring[p].nr, 0, 3)
            blocks += [(q, ring[p].nl), (q, ring[p].nr)]
        pair(*blocks)

    far_x, far_y = ring[0].far, ring[1].far

    @pl.loop(0, 2)
    def _(g):
        for q, k in ((2 * g, far_x), (2 * g + 1, far_y)):
            landed(q, k, 0, 4)
            landed(q, k, 1, 5)
        pair((2 * g, far_x), (2 * g + 1, far_y))

    rows_c = pl.ds(pl.multiple_of(c * (trades // 2), 8), trades // 2)
    rows_sib = pl.ds(pl.multiple_of(sib * (trades // 2), 8), trades // 2)
    swap = (acc.at[rows_sib], pr, ss_p.at[0], rs_p.at[0], sibling)
    send(*swap)
    strip_rows = out.shape[0]
    rdma(*swap).wait_recv()
    total = acc[rows_c] + pr[...]
    po[...] = jnp.concatenate(
        [total[:, s * LANE : (s + 1) * LANE].reshape(CHIPS, strip_rows, LANE) for s in (0, 1)], axis=1
    ).astype(BF16)

    tile = ob.at[z * RING + x]

    def deliver(n, dst):
        rdma(po.at[n], tile, ss_o.at[0], rs_o.at[0], {"grp": y, "path": dst}).start()

    for k in (4, 3, 5, 2, 6, 1, 7, 0):
        zz = lax.rem(z + k, DEPTH)
        for side in (0, 1):
            for u in (0, 1):
                n = side * 2 * DEPTH + 2 * zz + u
                dst = c * CHIPS + n
                if k:
                    deliver(n, dst)
                else:
                    pl.when(dst != me)(lambda n=n, dst=dst: deliver(n, dst))

                    @pl.when(dst == me)
                    def _():
                        pltpu.make_async_copy(po.at[n], tile, rs_o.at[0]).start()

    all_left(len(sent))

    def j_crossed(e):
        for k in (1, 2, 3):
            rdma(*j_cross(e, k)).wait_send()

        @pl.when(core != c)
        def _():
            rdma(*j_cross(e, 0)).wait_send()

    both(j_crossed)

    @pl.when(turn)
    def _():
        for k in range(1, DEPTH):
            rdma(*j_line(k)).wait_send()

    pltpu.make_async_copy(ob, ob, rs_o.at[0]).wait()

    rest = []
    for t in range(CHIPS):
        tile = ob[t].astype(F32)
        out[:, t * LANE : (t + 1) * LANE] = tile[0:strip_rows]
        rest.append(tile[strip_rows : 2 * strip_rows, 0:more])
    out[:, main:params] = jnp.concatenate(rest, axis=1)

    def po_sent(n):
        rdma(po.at[0:n], po.at[0:n], ss_o.at[0], rs_o.at[0], sibling).wait_send()

    pl.when(core == c)(lambda: po_sent(CHIPS - 1))
    pl.when(core != c)(lambda: po_sent(CHIPS))


def per_device(
    path_sens, discounts, cash_flows, flow_index, exercise_step, trade_steps, jacobian_inv
):
    paths_own, params = path_sens.shape
    trades = cash_flows.shape[0]
    jrows = jacobian_inv.shape[0]
    strip = trades // PATHS
    rest = params - CHIPS * LANE
    pad = -(-jrows // 16) * 16
    half = params // 2
    slots = cash_flows.shape[1]
    part = pad // 2
    share = 16
    vm = pltpu.VMEM
    dma = pltpu.SemaphoreType.DMA
    scratch = [
        vm((paths_own, LANE), BF16),
        vm((slots, trades), F32),
        vm((slots, trades), jnp.int32),
        vm((1, trades), jnp.int32),
        vm((1, trades), jnp.int32),
        vm((half, paths_own), BF16),
        vm((half, paths_own), BF16),
        vm((paths_own, LANE), BF16),
        vm((half + 8, LANE), F32),
        vm((RING, RING, 2 * pad, LANE), F32),
        vm((RING, 6, pad, LANE), F32),
        vm((RING, 2 * pad, LANE), F32),
        vm((RING, RING, part, LANE), F32),
        vm((2, 2 * part, LANE), F32),
        vm((2, DEPTH, share, LANE), F32),
        vm((2, share, LANE), F32),
        vm((2, 2 * part, LANE), F32),
        vm((RING, RING, 2 * pad, LANE), F32),
        vm((jrows, params), BF16),
        vm((pad, -(-rest // LANE) * LANE), F32),
        vm((DEPTH, RING, pad + GROUP, LANE), BF16),
        vm((2, RING, pad + GROUP, LANE), BF16),
        vm((RING, RING, 2 * pad, LANE), BF16),
        vm((RING, RING, 2, GROUP, LANE), BF16),
        vm((RING * RING, 2 * pad, LANE), BF16),
        vm((trades, 3 * LANE), BF16),
        vm((trades, 8 * pad), jnp.int32),
        vm((trades, 8 * pad), BF16),
        vm((trades, 2 * LANE), F32),
        vm((trades // 2, 2 * LANE), F32),
        vm((CHIPS, 2 * strip, LANE), BF16),
        vm((CHIPS, 2 * strip, LANE), BF16),
        dma((RING + 1,)), dma((RING + 1,)), dma((7,)),
        dma((RING, 6)), dma((RING, 6)),
        dma((RING, RING)), dma((RING,)),
        dma((2, DEPTH)), dma((2,)),
        dma((2, DEPTH)), dma((2,)),
        dma((RING, RING)), dma((RING,)),
        dma((RING, 6)), dma((RING, 6)),
        dma((DEPTH,)), dma((2, RING)), dma((3, 2)),
        dma((2, 6)), dma((2, 6)),
        dma((2,)), dma((2,)),
        dma((1,)), dma((1,)),
        pltpu.SemaphoreType.REGULAR((2,)),
    ]
    vmem = pl.BlockSpec(memory_space=pltpu.VMEM)
    hbm = pl.BlockSpec(memory_space=pl.ANY)
    return pl.pallas_call(
        kernel,
        out_shape=jax.ShapeDtypeStruct((strip, params), F32),
        in_specs=[hbm] * 7,
        out_specs=vmem,
        scratch_shapes=scratch,
        compiler_params=pltpu.CompilerParams(
            collective_id=0, has_side_effects=True, vmem_limit_bytes=56 * 1024 * 1024
        ),
    )(
        discounts,
        path_sens.T,
        cash_flows.T,
        flow_index.T,
        exercise_step.reshape(1, trades),
        trade_steps.reshape(1, trades),
        jacobian_inv,
    )


def solution(mesh):
    placed = (
        P(("grp", "path"), None),
        P(("grp", "path"), None),
        P("grp", None),
        P("grp", None),
        P("grp"),
        P("grp"),
        P("path", None),
    )
    return jax.shard_map(
        per_device, mesh=mesh, in_specs=placed, out_specs=P(("grp", "path"), None), check_vma=False
    )
```
